32 devices in a mesh: blk: 8 (over y, x, core), ch: 4 (over z).
Axes of the slice: x: 2, y: 2, z: 4, core: 2. Of those that a mesh axis runs over, the one named last changes fastest.
Arguments:
- block_input: bfloat16 [2, 64, 64, 512], P(None, 'blk', None, 'ch'), may hold values from -18 to 18
- cotangent: bfloat16 [2, 64, 64, 512], P(None, 'blk', None, 'ch'), may hold values from -6 to 6
- image_embed: float32 [2, 2048], replicated, may hold values from -6 to 6
- timesteps: int32 [2], replicated, may hold values from 0 to 999
- text_len: int32 [2], replicated, may hold values from 5 to 256, as said below
- context: bfloat16 [2, 260, 2048], P(None, None, 'ch'), may hold values from -6 to 6
- conv1_weight: bfloat16 [3, 3, 512, 512], P(None, None, None, 'ch'), may hold values from -0.09375 to 0.09375
- conv2_weight: bfloat16 [3, 3, 512, 512], P(None, None, None, 'ch'), may hold values from -0.09375 to 0.09375
- embed_weight: bfloat16 [2048, 2, 512], P(None, None, 'ch'), may hold values from -0.125 to 0.125
- embed_bias: float32 [2, 512], P(None, 'ch'), may hold values from -2 to 2
- norm1_gain: float32 [512], P('ch'), may hold values from 0.5 to 1.5
- norm1_bias: float32 [512], P('ch'), may hold values from -2 to 2
- norm2_gain: float32 [512], P('ch'), may hold values from 0.5 to 1.5
- norm2_bias: float32 [512], P('ch'), may hold values from -2 to 2
- norm3_gain: float32 [512], P('ch'), may hold values from 0.5 to 1.5
- norm3_bias: float32 [512], P('ch'), may hold values from -2 to 2
- qkv_weight: bfloat16 [512, 3, 512], P(None, None, 'ch'), may hold values from -0.25 to 0.25
- out_weight: bfloat16 [512, 512], P('ch'), may hold values from -2 to 2
- ctx_weight: bfloat16 [2048, 2, 512], P('ch'), may hold values from -0.125 to 0.125
Outputs:
- block_output: bfloat16 [2, 64, 64, 512], P(None, 'blk', None, 'ch')
- input_grad: float32 [2, 64, 64, 512], P(None, 'blk', None, 'ch')
- conv1_grad: float32 [3, 3, 512, 512], P(None, None, None, 'ch')
- conv2_grad: float32 [3, 3, 512, 512], P(None, None, None, 'ch')
- embed_weight_grad: float32 [2048, 2, 512], P(None, None, 'ch')
- embed_bias_grad: float32 [2, 512], P(None, 'ch')
- norm1_gain_grad: float32 [512], P('ch')
- norm1_bias_grad: float32 [512], P('ch')
- norm2_gain_grad: float32 [512], P('ch')
- norm2_bias_grad: float32 [512], P('ch')
- norm3_gain_grad: float32 [512], P('ch')
- norm3_bias_grad: float32 [512], P('ch')
- qkv_grad: float32 [512, 3, 512], P(None, None, 'ch')
- out_grad: float32 [512, 512], P('ch')
- ctx_grad: float32 [2048, 2, 512], P('ch')
The draws below stay inside these ranges and needn't reach their ends.
Inputs may be any that keep to these rules, and one draw needn't show every extreme that they name: `text_len`: in every draw one image's text has exactly 256 tokens.
All inputs are finite; a program needn't handle non-finite values.
Results may differ from the reference program's by a relative error of at most 0.024.
Values may be sent and summed in bfloat16 or wider, within the bound.
No kernel may reach another device: no remote copies, remote signals or barrier semaphores. Data moves between devices by JAX's collectives and lax.ppermute only.
A program may use at most 192 MiB of HBM per device.

```python
import math
import jax
import jax.numpy as jnp
from jax import lax

HEADS = 8
HEAD = 64
C = 512
GROUPS = 32
EMB = 2048
XF = 2048
RES = 64
TEXT = 256
CLIPTOK = 4
CTX = 260
IMAGES = 2


def draw_block_input(key, part):
    key = jax.random.fold_in(key, 5)
    field_key = jax.random.fold_in(key, 0)
    dir_key = jax.random.fold_in(key, 2)
    rough_key = jax.random.fold_in(key, 3)
    sign_key = jax.random.fold_in(key, 4)
    level_key = jax.random.fold_in(key, 5)
    prof_key = jax.random.fold_in(key, 6)
    ramp = jnp.arange(RES, dtype=jnp.float32) / (RES - 1)
    flip = jax.random.randint(dir_key, (IMAGES, 1), 0, 2).astype(jnp.float32)
    along = flip * ramp[None, :] + (1.0 - flip) * (1.0 - ramp[None, :])
    rough = jnp.exp(jax.random.uniform(rough_key, (IMAGES, RES), jnp.float32, -0.2, 0.2))
    row_scale = ((1.0 + 2.0 * along) * rough)[:, :, None, None]
    turn = jax.random.randint(prof_key, (IMAGES, 1), 0, 2).astype(jnp.float32)
    profile = 0.5 + turn * ramp[None, :] + (1.0 - turn) * (1.0 - ramp[None, :])
    signs = 2.0 * jax.random.randint(sign_key, (IMAGES, GROUPS), 0, 2).astype(jnp.float32) - 1.0
    levels = signs * jax.random.uniform(level_key, (IMAGES, GROUPS), jnp.float32, 2.0, 4.0)
    offset = jnp.repeat(levels, C // GROUPS, axis=1)[:, None, None, :] * profile[:, :, None, None]
    field = jnp.clip(jax.random.normal(field_key, (IMAGES, RES, RES, C), jnp.float32), -3.0, 3.0)
    return jnp.clip(field * row_scale + offset, -17.9, 17.9).astype(jnp.bfloat16)


def draw_text_len(key, part):
    key = jax.random.fold_in(key, 11)
    len_key, pick_key = jax.random.split(key)
    drawn = jax.random.randint(len_key, (IMAGES,), 5, TEXT + 1)
    chosen = jax.random.randint(pick_key, (), 0, IMAGES)
    return jnp.where(jnp.arange(IMAGES) == chosen, TEXT, drawn).astype(jnp.int32)


def block_levels(stream_key, dims, cuts, smallest, high):
    loudness, own = 1.0, jax.random.fold_in(stream_key, 6)
    for position, parts in cuts:
        draws = jnp.exp(jax.random.uniform(jax.random.fold_in(own, position), (parts,), jnp.float32, smallest / len(cuts), high / len(cuts)))
        loudness = loudness * jnp.repeat(draws, dims[position] // parts).reshape([-1 if axis == position else 1 for axis in range(len(dims))])
    return loudness


def gaussian(rng, extent, deviation, limit, cuts=(), kind=jnp.bfloat16):
    values = jax.random.normal(rng, extent, jnp.float32) * deviation
    if len(cuts) > 0:
        values = block_levels(rng, extent, cuts, -0.22, 0.18) * values
    return jnp.clip(values, min=-limit, max=limit).astype(kind)


def setup_inputs(seed: int = 0) -> dict:
    streams_of = jax.random.split(jax.random.key(seed), 20)
    block_input = draw_block_input(jax.random.fold_in(streams_of[19], 71), 0)
    cotangent = gaussian(streams_of[1], (IMAGES, RES, RES, C), 1.0, 6.0, ((1, 8), (3, 4)))
    image_embed = gaussian(streams_of[2], (IMAGES, EMB), 1.0, 6.0, (), jnp.float32)
    timesteps = jax.random.randint(streams_of[3], (IMAGES,), 0, 1000).astype(jnp.int32)
    text_len = draw_text_len(jax.random.fold_in(streams_of[19], 71), 0)
    context = gaussian(streams_of[5], (IMAGES, CTX, XF), 1.0, 6.0, ((2, 4),))
    conv1_weight = gaussian(streams_of[6], (3, 3, C, C), (9 * C) ** -0.5, 0.09375, ((3, 4),))
    conv2_weight = gaussian(streams_of[7], (3, 3, C, C), (9 * C) ** -0.5, 0.09375, ((3, 4),))
    embed_weight = gaussian(streams_of[8], (EMB, 2, C), EMB ** -0.5, 0.125, ((2, 4),))
    embed_bias = gaussian(streams_of[9], (2, C), 0.3, 2.0, ((1, 4),), jnp.float32)
    norm1_gain = jnp.clip(1.0 + 0.1 * jax.random.normal(streams_of[10], (C,), jnp.float32), 0.5, 1.5)
    norm1_bias = gaussian(streams_of[11], (C,), 0.3, 2.0, ((0, 4),), jnp.float32)
    norm2_gain = jnp.clip(1.0 + 0.1 * jax.random.normal(streams_of[12], (C,), jnp.float32), 0.5, 1.5)
    norm2_bias = gaussian(streams_of[13], (C,), 0.3, 2.0, ((0, 4),), jnp.float32)
    norm3_gain = jnp.clip(1.0 + 0.1 * jax.random.normal(streams_of[14], (C,), jnp.float32), 0.5, 1.5)
    norm3_bias = gaussian(streams_of[15], (C,), 0.3, 2.0, ((0, 4),), jnp.float32)
    qkv_weight = gaussian(streams_of[16], (C, 3, C), C ** -0.5, 0.25, ((2, 4),))
    out_weight = gaussian(streams_of[17], (C, C), (C // 64) ** -0.5, 2.0, ((0, 4),))
    ctx_weight = gaussian(streams_of[18], (XF, 2, C), XF ** -0.5, 0.125, ((0, 4),))
    return {"block_input": block_input, "cotangent": cotangent, "image_embed": image_embed, "timesteps": timesteps, "text_len": text_len, "context": context, "conv1_weight": conv1_weight, "conv2_weight": conv2_weight, "embed_weight": embed_weight, "embed_bias": embed_bias, "norm1_gain": norm1_gain, "norm1_bias": norm1_bias, "norm2_gain": norm2_gain, "norm2_bias": norm2_bias, "norm3_gain": norm3_gain, "norm3_bias": norm3_bias, "qkv_weight": qkv_weight, "out_weight": out_weight, "ctx_weight": ctx_weight}


@jax.custom_vjp
def low(v):
    return lax.optimization_barrier(v.astype(jnp.bfloat16)).astype(jnp.float32)

@jax.custom_vjp
def low_back(v):
    return v

def low_keep(v):
    return (low(v), None)

def low_pass(kept, grad):
    return (grad,)

def back_keep(v):
    return (v, None)

def back_low(kept, grad):
    return (low(grad),)
low.defvjp(low_keep, low_pass)
low_back.defvjp(back_keep, back_low)

def round_both(field):
    return low_back(low(field))

def group_norm(field, gain, offset):
    shape = field.shape
    grouped = field.reshape(shape[0], shape[1], shape[2], GROUPS, shape[3] // GROUPS)
    mean_val = lax.optimization_barrier(jnp.mean(grouped, axis=(1, 2, 4), keepdims=True))
    variance = lax.optimization_barrier(jnp.mean(jnp.square(grouped - mean_val), axis=(1, 2, 4), keepdims=True))
    normed = (grouped - mean_val) * lax.rsqrt(variance + 1e-05)
    return normed.reshape(shape) * gain + offset

def convolve(field, weight):
    return lax.conv_general_dilated(field, weight, (1, 1), ((1, 1), (1, 1)), dimension_numbers=('NHWC', 'HWIO', 'NHWC'), precision=lax.Precision.HIGHEST)

def embed_features(timesteps, image_embed):
    half_width = EMB // 2
    freqs = jnp.exp(-math.log(10000.0) * jnp.arange(half_width, dtype=jnp.float32) / half_width)
    angles = timesteps.astype(jnp.float32)[:, None] * freqs[None, :]
    return jax.nn.silu(jnp.concatenate([jnp.cos(angles), jnp.sin(angles)], axis=1) + image_embed)

def attend_image(query, keys, values, key_ctx, val_ctx, live_ctx):
    all_keys = jnp.concatenate([key_ctx, keys], axis=0)
    all_vals = jnp.concatenate([val_ctx, values], axis=0)
    live = jnp.concatenate([live_ctx, jnp.ones((keys.shape[0],), dtype=bool)])
    score_scale = 1.0 / math.sqrt(HEAD)

    def one_block(query_rows):
        scores = low_back(jnp.einsum('qhd,khd->hqk', query_rows, all_keys, precision=lax.Precision.HIGHEST) * score_scale)
        scores = jnp.where(live[None, None, :], scores, -1e+30)
        top = lax.optimization_barrier(jnp.max(scores, axis=-1, keepdims=True))
        expo = jnp.exp(scores - top)
        probs = expo / lax.optimization_barrier(jnp.sum(expo, axis=-1, keepdims=True))
        return jnp.einsum('hqk,khd->qhd', low(probs), all_vals, precision=lax.Precision.HIGHEST)
    blocks = query.reshape(-1, 512, HEADS, HEAD)
    return lax.map(jax.checkpoint(one_block), blocks).reshape(query.shape)

def reference(block_input, cotangent, image_embed, timesteps, text_len, context, conv1_weight, conv2_weight, embed_weight, embed_bias, norm1_gain, norm1_bias, norm2_gain, norm2_bias, norm3_gain, norm3_bias, qkv_weight, out_weight, ctx_weight):
    emb_act = low(embed_features(timesteps, image_embed))
    ctx_float = context.astype(jnp.float32)
    live_ctx = jnp.arange(CTX)[None, :] < CLIPTOK + text_len[:, None]
    npix = RES * RES

    def forward(input_f, weight_one, weight_two, embed_mat, embed_vec, gain_one, bias_one, gain_two, bias_two, gain_three, bias_three, qkv_mat, out_mat, ctx_mat):
        scale_shift = jnp.einsum('ie,esc->isc', emb_act, embed_mat, precision=lax.Precision.HIGHEST) + embed_vec
        act_one = low(jax.nn.silu(group_norm(input_f, gain_one, bias_one)))
        hidden = low_back(convolve(act_one, weight_one))
        pre_two = group_norm(hidden, gain_two, bias_two) * (1.0 + scale_shift[:, 0][:, None, None, :]) + scale_shift[:, 1][:, None, None, :]
        act_two = low(jax.nn.silu(pre_two))
        resid = input_f + low_back(convolve(act_two, weight_two))
        act_three = low(group_norm(resid, gain_three, bias_three))
        qkv = jnp.einsum('ihwc,ctd->ihwtd', act_three, qkv_mat, precision=lax.Precision.HIGHEST)
        qkv = round_both(qkv.reshape(IMAGES, npix, 3, HEADS, HEAD))
        ctx_kv = jnp.einsum('itx,xsc->itsc', ctx_float, ctx_mat, precision=lax.Precision.HIGHEST)
        ctx_kv = round_both(ctx_kv.reshape(IMAGES, CTX, 2, HEADS, HEAD))

        def image_step(carry, item):
            return (carry, attend_image(*item))
        unused, attn = lax.scan(image_step, None, (qkv[:, :, 0], qkv[:, :, 1], qkv[:, :, 2], ctx_kv[:, :, 0], ctx_kv[:, :, 1], live_ctx))
        attn_low = round_both(attn).reshape(IMAGES, RES, RES, HEADS * HEAD)
        return resid + jnp.einsum('ihwc,cd->ihwd', attn_low, out_mat, precision=lax.Precision.HIGHEST)
    params = tuple((array_in.astype(jnp.float32) for array_in in (block_input, conv1_weight, conv2_weight, embed_weight, embed_bias, norm1_gain, norm1_bias, norm2_gain, norm2_bias, norm3_gain, norm3_bias, qkv_weight, out_weight, ctx_weight)))
    result, pullback = jax.vjp(forward, *params)
    grads = pullback(cotangent.astype(jnp.float32))
    return (result.astype(jnp.bfloat16), grads[0], grads[1], grads[2], grads[3], grads[4], grads[5], grads[6], grads[7], grads[8], grads[9], grads[10], grads[11], grads[12], grads[13])
```

```python
import functools
import math

import jax
import jax.numpy as jnp
from jax import lax
from jax.experimental import pallas as pl
from jax.experimental.pallas import tpu as pltpu
from jax.sharding import PartitionSpec as P

HEAD = 64
GROUPS = 32
CLIPTOK = 4
LANES = 128
HALF = 256
COLS = 64
VMEM_BYTES = 56 * 2**20
BF = jnp.bfloat16
F32 = jnp.float32


def dot(a, b):
    return jnp.dot(a, b, preferred_element_type=F32)


def dot_t(a, b):
    return lax.dot_general(a, b, (((1,), (1,)), ((), ())), preferred_element_type=F32)


def group_sum(vec, size):
    lane = lax.broadcasted_iota(jnp.int32, vec.shape, 1)
    step = 1
    while step < size:
        low = pltpu.roll(vec, step, 1)
        high = pltpu.roll(vec, LANES - step, 1)
        vec = vec + jnp.where((lane & step) != 0, low, high)
        step *= 2
    return vec


def norm_stats(sums, cells, size):
    total = group_sum(sums, size)
    mean = total[0:1] / cells
    inv = lax.rsqrt(total[1:2] / cells - mean * mean + 1e-05)
    return mean, inv


def affine_of(vec, shard, which, mean, inv):
    row = vec[pl.ds(shard, 1)][0]
    gain = row[2 * which : 2 * which + 1]
    bias = row[2 * which + 1 : 2 * which + 2]
    if which == 1:
        grow = 1.0 + row[6:7]
        gain, bias = gain * grow, bias * grow + row[7:8]
    slope = inv * gain
    return gain, slope, bias - mean * slope


def shards(scal):
    h = scal[0]
    return (h, h + 2, 1 - h, 3 - h)


def lanes_of(shard):
    return pl.ds(pl.multiple_of(shard * LANES, LANES), LANES)


def column_sums(first, second):
    rows = jnp.concatenate(
        [jnp.sum(first, axis=0, keepdims=True), jnp.sum(second, axis=0, keepdims=True)], axis=0
    )
    return jnp.concatenate([rows, jnp.zeros((6, rows.shape[1]), F32)], axis=0)


def shift_columns(total, left, right):
    col = lax.broadcasted_iota(jnp.int32, total.shape, 0) % COLS
    rows = total.shape[0]
    total = total + jnp.where(col > 0, pltpu.roll(left, 1, 0), 0.0)
    return total + jnp.where(col < COLS - 1, pltpu.roll(right, rows - 1, 0), 0.0)


def load_weights(scal, own_w, oth_w, w_scr):
    i = scal[1]
    w_scr[:, lanes_of(i)] = own_w[...]
    w_scr[:, lanes_of(1 - i)] = oth_w[...]


def conv_kernel(scal, own, oth, top, bot, sums, vec, own_w, oth_w, *rest, which, cells, size):
    if which == 0:
        out_low, out_sums, act_out, act_scr, w_scr = rest
    else:
        base, out_f, out_low, out_sums, act_out, act_scr, w_scr = rest
    pix = own.shape[0]
    load_weights(scal, own_w, oth_w, w_scr)
    for quarter, shard in enumerate(shards(scal)):
        lanes = slice(quarter * LANES, (quarter + 1) * LANES)
        mean, inv = norm_stats(sums[:, lanes], cells, size)
        gain, slope, offset = affine_of(vec, shard, which, mean, inv)

        def active(field):
            pre = field.astype(F32) * slope + offset
            return pre * jax.nn.sigmoid(pre)

        half = own if quarter < 2 else oth
        main = active(half[:, (quarter % 2) * LANES : (quarter % 2 + 1) * LANES])
        act_scr[COLS : COLS + pix, lanes_of(shard)] = main.astype(BF)
        act_scr[0:COLS, lanes_of(shard)] = jnp.where(
            scal[2] > 0, active(top[:, lanes]), 0.0
        ).astype(BF)
        act_scr[COLS + pix :, lanes_of(shard)] = jnp.where(
            scal[3] > 0, active(bot[:, lanes]), 0.0
        ).astype(BF)
    act_out[...] = act_scr[COLS : COLS + pix, :]
    channels = act_scr.shape[1]
    parts = []
    for kx in range(3):
        acc = None
        for ky in range(3):
            tap = (ky * 3 + kx) * channels
            term = dot(act_scr[ky * COLS : ky * COLS + pix, :], w_scr[tap : tap + channels, :])
            acc = term if acc is None else acc + term
        parts.append(acc)
    result = shift_columns(parts[1], parts[0], parts[2])
    if which == 1:
        result = result + base[...].astype(F32)
        out_f[...] = result
    out_low[...] = result.astype(BF)
    out_sums[...] = column_sums(result, result * result)


def qkv_kernel(
    scal, own, oth, sums, vec, cot_own, cot_oth, own_w, oth_w, out, act_out, cot_out, *, cells, size
):
    i = scal[1]
    for quarter, shard in enumerate(shards(scal)):
        lanes = slice(quarter * LANES, (quarter + 1) * LANES)
        part = slice((quarter % 2) * LANES, (quarter % 2 + 1) * LANES)
        mean, inv = norm_stats(sums[:, lanes], cells, size)
        gain, slope, offset = affine_of(vec, shard, 2, mean, inv)
        half = own if quarter < 2 else oth
        cot = cot_own if quarter < 2 else cot_oth
        act_out[:, lanes_of(shard)] = (half[:, part].astype(F32) * slope + offset).astype(BF)
        cot_out[:, lanes_of(shard)] = cot[:, part]
    for weight, first in ((own_w, 2 * i), (oth_w, 2 - 2 * i)):
        for head in range(2):
            columns = weight[:, head * HALF : (head + 1) * HALF]
            fwd = dot(act_out[...], columns)
            back = dot(cot_out[...], columns)
            lane = lax.broadcasted_iota(jnp.int32, fwd.shape, 1)
            out[pl.ds(first + head, 1)] = jnp.where(lane < 3 * HEAD, fwd, back).astype(BF)[None]


def below_stats(scal, total, own, oth, sums, vec, out_own, out_oth, out_stats, which, cells, size):
    for quarter, shard in enumerate(shards(scal)):
        lanes = slice(quarter * LANES, (quarter + 1) * LANES)
        part = slice((quarter % 2) * LANES, (quarter % 2 + 1) * LANES)
        mean, inv = norm_stats(sums[:, lanes], cells, size)
        gain, slope, offset = affine_of(vec, shard, which, mean, inv)
        half = own if quarter < 2 else oth
        grad = total[:, lanes_of(shard)]
        if quarter < 2:
            out_own[:, part] = grad
        else:
            out_oth[:, part] = grad.astype(BF)
        field = half[:, part].astype(F32)
        if which < 2:
            grad = grad * silu_slope(field * slope + offset)
        out_stats[:, lanes] = column_sums(grad, grad * ((field - mean) * inv))


def silu_slope(field):
    sigma = jax.nn.sigmoid(field)
    return sigma * (1.0 + field * (1.0 - sigma))


def qkv_back_kernel(
    scal, grads, own_w, oth_w, own, oth, sums, vec, out_own, out_oth, out_stats, tot_scr, *, cells, size
):
    i = scal[1]
    total = None
    for weight, first in ((own_w, 2 * i), (oth_w, 2 - 2 * i)):
        for head in range(2):
            columns = weight[:, head * HALF : (head + 1) * HALF]
            grad = grads[pl.ds(first + head, 1)][0]
            lane = lax.broadcasted_iota(jnp.int32, grad.shape, 1)
            term = dot_t(jnp.where(lane < 3 * HEAD, grad, jnp.zeros_like(grad)), columns)
            total = term if total is None else total + term
    tot_scr[...] = total
    below_stats(scal, tot_scr, own, oth, sums, vec, out_own, out_oth, out_stats, 2, cells, size)


def out_kernel(scal, grads, own_w, oth_w, act, cot, proj_own, proj_oth, keep, send, tot_scr):
    i = scal[1]
    total = None
    act_t = act[...].astype(F32).T.astype(BF)
    cot_t = cot[...].astype(F32).T.astype(BF)
    for weight, first, result in ((own_w, 2 * i, keep), (oth_w, 2 - 2 * i, send)):
        for head in range(2):
            lanes = slice(head * HALF, (head + 1) * HALF)
            columns = weight[:, lanes]
            grad = grads[pl.ds(first + head, 1)][0]
            lane = lax.broadcasted_iota(jnp.int32, grad.shape, 1)
            term = dot_t(jnp.where(lane < 3 * HEAD, jnp.zeros_like(grad), grad), columns)
            total = term if total is None else total + term
            first_grad, second_grad = dot(act_t, grad), dot(cot_t, grad)
            lane = lax.broadcasted_iota(jnp.int32, first_grad.shape, 1)
            result[:, lanes] = jnp.where(lane < 3 * HEAD, first_grad, second_grad).astype(
                result.dtype
            )
    tot_scr[...] = total
    for quarter, shard in enumerate(shards(scal)):
        part = slice((quarter % 2) * LANES, (quarter % 2 + 1) * LANES)
        if quarter < 2:
            proj_own[:, part] = tot_scr[:, lanes_of(shard)]
        else:
            proj_oth[:, part] = tot_scr[:, lanes_of(shard)].astype(BF)


def norm_back(scal, quarter, shard, sums, vec, stats, which, cells, size):
    lanes = slice(quarter * LANES, (quarter + 1) * LANES)
    mean, inv = norm_stats(sums[:, lanes], cells, size)
    gain, slope, offset = affine_of(vec, shard, which, mean, inv)
    means = group_sum(stats[:, lanes] * gain, size) / cells

    def back(grad, field):
        field = field.astype(F32)
        hat = (field - mean) * inv
        if which < 2:
            grad = grad * silu_slope(field * slope + offset)
        return (grad * gain - means[0:1] - hat * means[1:2]) * inv

    return back


def conv_back_kernel(
    scal, part_own, part_recv, dtop, dbot, field, ftop, fbot, sums, stats, vec,
    own_w, oth_w, low_own, low_oth, low_sums, *rest, which, cells, size,
):
    if which == 2:
        cot, ctop, cbot, out_f, ext, out_own, out_oth, out_stats, w_scr, tot_scr = rest
    else:
        ext, out_own, out_oth, out_stats, w_scr, tot_scr = rest
    pix = part_own.shape[0]
    load_weights(scal, own_w, oth_w, w_scr)
    for quarter in range(2):
        shard = shards(scal)[quarter]
        lanes = slice(quarter * LANES, (quarter + 1) * LANES)
        back = norm_back(scal, quarter, shard, sums, vec, stats, which, cells, size)
        main = back(part_own[:, lanes] + part_recv[:, lanes].astype(F32), field[:, lanes])
        head = back(dtop[:, lanes].astype(F32), ftop[:, lanes])
        tail = back(dbot[:, lanes].astype(F32), fbot[:, lanes])
        if which == 2:
            main = main + cot[:, lanes].astype(F32)
            head = head + ctop[:, lanes].astype(F32)
            tail = tail + cbot[:, lanes].astype(F32)
            out_f[:, lanes] = main
        ext[COLS : COLS + pix, lanes] = main.astype(BF)
        ext[0:COLS, lanes] = jnp.where(scal[2] > 0, head, 0.0).astype(BF)
        ext[COLS + pix :, lanes] = jnp.where(scal[3] > 0, tail, 0.0).astype(BF)
    channels = tot_scr.shape[1]
    parts = []
    for kx in range(3):
        acc = None
        for ky in range(3):
            tap = (ky * 3 + kx) * channels
            rows = (2 - ky) * COLS
            term = dot_t(ext[rows : rows + pix, :], w_scr[tap : tap + channels, :])
            acc = term if acc is None else acc + term
        parts.append(acc)
    tot_scr[...] = shift_columns(parts[1], parts[2], parts[0])
    below_stats(
        scal, tot_scr, low_own, low_oth, low_sums, vec, out_own, out_oth, out_stats,
        which - 1, cells, size,
    )


def last_kernel(
    scal, part_own, part_recv, field, sums, stats, vec, resid_grad, keep, send, tot_scr, *, cells, size
):
    i = scal[1]
    for quarter in range(2):
        shard = shards(scal)[quarter]
        lanes = slice(quarter * LANES, (quarter + 1) * LANES)
        back = norm_back(scal, quarter, shard, sums, vec, stats, 0, cells, size)
        main = back(part_own[:, lanes] + part_recv[:, lanes].astype(F32), field[:, lanes])
        tot_scr[:, lanes] = main + resid_grad[:, lanes]
    keep[...] = tot_scr[:, lanes_of(i)]
    send[...] = tot_scr[:, lanes_of(1 - i)].astype(BF)


def weight_grad_kernel(act_one, act_two, ext_one, ext_two, out, rhs_scr):
    pix, channels = act_one.shape
    rows = ext_one.shape[0]
    total = None
    for act, ext in ((act_one, ext_one), (act_two, ext_two)):
        wide = ext[...].astype(F32)
        col = lax.broadcasted_iota(jnp.int32, wide.shape, 0) % COLS
        for kx in range(3):
            if kx == 0:
                moved = jnp.where(col < COLS - 1, pltpu.roll(wide, rows - 1, 0), 0.0)
            elif kx == 2:
                moved = jnp.where(col > 0, pltpu.roll(wide, 1, 0), 0.0)
            else:
                moved = wide
            moved = moved.astype(BF)
            for ky in range(3):
                start = (2 - ky) * COLS
                tap = ky * 3 + kx
                rhs_scr[:, tap * LANES : (tap + 1) * LANES] = moved[start : start + pix]
        act_t = act[...].astype(F32).T.astype(BF)
        for tap in range(9):
            term = dot(act_t, rhs_scr[:, tap * LANES : (tap + 1) * LANES])
            if act is act_one:
                out[tap * channels : (tap + 1) * channels, :] = term
            else:
                out[tap * channels : (tap + 1) * channels, :] += term


def attend_kernel(
    live, qd, kva, kvb, ctx, dqo, dkva, dkvb, dctx,
    kv_scr, kt_scr, vt_scr, s_scr, e_scr, acc_scr, *, chunk, unroll,
):
    step = pl.program_id(0)
    half_a, half_b, extra = kva.shape[0], kvb.shape[0], ctx.shape[0]
    keys = half_a + half_b
    total = keys + extra
    block = qd.shape[0]

    @pl.when(step == 0)
    def _():
        kv_scr[0:half_a, :] = kva[...]
        kv_scr[half_a:keys, :] = kvb[...]
        kv_scr[keys:total, :] = ctx[...]
        acc_scr[...] = jnp.zeros_like(acc_scr)

        def turn(rows):
            flipped = kv_scr[rows, :].astype(F32).T.astype(BF)
            kt_scr[:, rows] = flipped[:HEAD]
            vt_scr[0:HEAD, rows] = flipped[HEAD:]

        def turn_step(n, carry):
            turn(pl.ds(pl.multiple_of(n * 256, 256), 256))
            return carry

        lax.fori_loop(0, keys // 256, turn_step, 0)
        turn(slice(keys, total))
        vt_scr[HEAD:, :] = jnp.ones((16, total), BF)

    both = qd[...].astype(F32).T
    q_t = both[:HEAD].astype(BF)
    zero = jnp.zeros((HEAD, block), BF)
    q_side = jnp.concatenate([q_t, zero], axis=0)

    def score(rows, top, masked):
        s = dot(kv_scr[rows, :], q_side)
        if masked:
            index = lax.broadcasted_iota(jnp.int32, s.shape, 0)
            s = jnp.where(index < live[0], s, -1e30)
        s_scr[rows, :] = s
        return jnp.maximum(top, jnp.max(s.reshape(-1, 8, block), axis=0))

    def span(n):
        return pl.ds(pl.multiple_of(n * chunk, chunk), chunk)

    def over_keys(func, carry):
        return lax.fori_loop(
            0, keys // chunk, lambda n, c: func(span(n), c), carry, unroll=unroll
        )

    tail = pl.ds(keys, extra)
    top = score(tail, jnp.full((8, block), -1e30, F32), True)
    top = over_keys(lambda rows, c: score(rows, c, False), top)
    top = jnp.max(top, axis=0, keepdims=True)

    def weigh(rows, acc):
        e = jnp.exp(s_scr[rows, :] - top).astype(BF)
        e_scr[rows, :] = e
        return acc + dot(vt_scr[:, rows], e)

    out_t = weigh(tail, jnp.zeros((HEAD + 16, block), F32))
    out_t = over_keys(weigh, out_t)
    inv = 1.0 / out_t[HEAD : HEAD + 1]
    out_t = out_t[:HEAD] * inv
    d_t = both[HEAD:]
    delta = jnp.sum(d_t * out_t, axis=0, keepdims=True) * inv
    d_t = d_t * inv
    d_side = jnp.concatenate([zero, d_t.astype(BF)], axis=0)
    zero_q = jnp.zeros((block, HEAD), BF)
    rows_q = jnp.concatenate([qd[:, :HEAD], zero_q], axis=1)
    rows_d = jnp.concatenate([zero_q, d_t.T.astype(BF)], axis=1)
    right = jnp.concatenate([rows_q, rows_d], axis=0)

    def back(rows, acc):
        d_prob = dot(kv_scr[rows, :], d_side)
        e = e_scr[rows, :]
        d_score = (e.astype(F32) * (d_prob - delta)).astype(BF)
        acc_scr[rows, :] += dot(jnp.concatenate([d_score, e], axis=1), right)
        return acc + dot(kt_scr[:, rows], d_score)

    dq_t = back(tail, jnp.zeros((HEAD, block), F32))
    dq_t = over_keys(back, dq_t)
    dqo[...] = jnp.concatenate([dq_t, out_t], axis=0).T.astype(BF)

    @pl.when(step == pl.num_programs(0) - 1)
    def _():
        dkva[...] = acc_scr[0:half_a, :]
        dkvb[...] = acc_scr[half_a:keys, :].astype(BF)
        dctx[...] = acc_scr[keys:total, :]


def attend(live, recv, kva, kvb, ctx):
    queries = recv.shape[0]
    block = min(512, queries)
    half_a, half_b, extra = recv.shape[0] if kva is recv else kva.shape[0], kvb.shape[0], ctx.shape[0]
    total = half_a + half_b + extra
    whole = lambda shape: pl.BlockSpec(shape, lambda n: (0, 0))
    flops = 12 * queries * total * HEAD
    return pl.pallas_call(
        functools.partial(attend_kernel, chunk=512, unroll=4),
        grid=(queries // block,),
        in_specs=[
            pl.BlockSpec(memory_space=pltpu.SMEM),
            pl.BlockSpec((block, LANES), lambda n: (n, 1)),
            whole((half_a, LANES)),
            whole((half_b, LANES)),
            whole((extra, LANES)),
        ],
        out_specs=[
            pl.BlockSpec((block, LANES), lambda n: (n, 0)),
            whole((half_a, LANES)),
            whole((half_b, LANES)),
            whole((extra, LANES)),
        ],
        out_shape=[
            jax.ShapeDtypeStruct((queries, LANES), BF),
            jax.ShapeDtypeStruct((half_a, LANES), F32),
            jax.ShapeDtypeStruct((half_b, LANES), BF),
            jax.ShapeDtypeStruct((extra, LANES), F32),
        ],
        scratch_shapes=[
            pltpu.VMEM((total, LANES), BF),
            pltpu.VMEM((HEAD, total), BF),
            pltpu.VMEM((HEAD + 16, total), BF),
            pltpu.VMEM((total, block), F32),
            pltpu.VMEM((total, block), BF),
            pltpu.VMEM((total, LANES), F32),
        ],
        compiler_params=pltpu.CompilerParams(vmem_limit_bytes=VMEM_BYTES),
        cost_estimate=pl.CostEstimate(
            flops=4 * flops, bytes_accessed=8 * total * LANES, transcendentals=queries * total
        ),
    )(live, recv, kva, kvb, ctx)


def call(kernel, args, outs, scratch=(), flops=0, scalars=1):
    in_vmem = pl.BlockSpec(memory_space=pltpu.VMEM)
    in_smem = pl.BlockSpec(memory_space=pltpu.SMEM)
    size = sum(math.prod(a.shape) * a.dtype.itemsize for a in args)
    size += sum(math.prod(s) * jnp.dtype(d).itemsize for s, d in outs)
    return pl.pallas_call(
        kernel,
        in_specs=[in_smem] * scalars + [in_vmem] * (len(args) - scalars),
        out_specs=[in_vmem] * len(outs),
        out_shape=[jax.ShapeDtypeStruct(s, d) for s, d in outs],
        scratch_shapes=[pltpu.VMEM(s, d) for s, d in scratch],
        compiler_params=pltpu.CompilerParams(vmem_limit_bytes=VMEM_BYTES),
        cost_estimate=pl.CostEstimate(flops=flops, bytes_accessed=size, transcendentals=0),
    )(*args)


def embed_features(timesteps, image_embed):
    half_width = image_embed.shape[1] // 2
    freqs = jnp.exp(-math.log(10000.0) * jnp.arange(half_width, dtype=F32) / half_width)
    angles = timesteps.astype(F32)[:, None] * freqs[None, :]
    return jax.nn.silu(jnp.concatenate([jnp.cos(angles), jnp.sin(angles)], axis=1) + image_embed)


def body(
    block_input,
    cotangent,
    image_embed,
    timesteps,
    text_len,
    context,
    conv1_weight,
    conv2_weight,
    embed_weight,
    embed_bias,
    norm1_gain,
    norm1_bias,
    norm2_gain,
    norm2_bias,
    norm3_gain,
    norm3_bias,
    qkv_weight,
    out_weight,
    ctx_weight,
):
    images, row_count, col_count, width = block_input.shape
    channels = qkv_weight.shape[0]
    size = channels // GROUPS
    blocks = lax.axis_size("blk")
    pix = row_count * col_count
    cells = float(pix * blocks * size)
    split = blocks // 4
    ctx_len = context.shape[1]
    b = lax.axis_index("blk")
    z = lax.axis_index("ch")
    h, i = z % 2, z // 2
    scal = jnp.stack(
        [h, i, (b > 0).astype(jnp.int32), (b < blocks - 1).astype(jnp.int32)]
    ).astype(jnp.int32)

    def over_ch(value, mask):
        return lax.ppermute(value, "ch", [(n, n ^ mask) for n in range(4)])

    def over_blk(value, mask):
        return lax.ppermute(value, "blk", [(n, n ^ mask) for n in range(blocks)])

    def halo(first, last):
        up = [(n, n + 1) for n in range(blocks - 1)]
        down = [(n + 1, n) for n in range(blocks - 1)]
        return lax.ppermute(last, "blk", up), lax.ppermute(first, "blk", down)

    def halo_rows(field):
        return halo(field[:COLS], field[pix - COLS :])

    def blk_sum(value):
        spread = jnp.broadcast_to(value[None], (blocks,) + value.shape)
        return jnp.sum(lax.all_to_all(spread, "blk", 0, 0), axis=0)

    def by_image(first, second):
        return jnp.where(i == 0, first, second), jnp.where(i == 0, second, first)

    def halves(field):
        flat = field.reshape(images, pix, width)
        mine = lax.dynamic_index_in_dim(flat, i, 0, keepdims=False)
        theirs = lax.dynamic_index_in_dim(flat, 1 - i, 0, keepdims=False)
        one, two, three = over_ch(mine, 1), over_ch(theirs, 2), over_ch(theirs, 3)
        return (
            jnp.concatenate(by_image(mine, two), axis=1),
            jnp.concatenate(by_image(one, three), axis=1),
        )

    def other_shard(weight):
        rows = weight.shape[0] // blocks
        chunk = lax.dynamic_slice_in_dim(weight, b * rows, rows, 0)
        return lax.all_gather(over_ch(chunk, 2), "blk", axis=0, tiled=True)

    def all_reduce(value):
        if blocks != 8:
            return lax.psum(value.astype(BF), "blk").astype(F32)
        rows = value.shape[0]
        core, chip = b % 2, b // 2
        keep = lax.dynamic_slice_in_dim(value, core * (rows // 2), rows // 2, 0)
        send = lax.dynamic_slice_in_dim(value, (1 - core) * (rows // 2), rows // 2, 0)
        part = keep.astype(F32) + over_blk(send.astype(BF), 1).astype(F32)
        part = part.reshape(4, rows // 8, LANES)
        total = lax.dynamic_index_in_dim(part, chip, 0, keepdims=False)
        for mask in (3, 1, 2):
            chunk = lax.dynamic_index_in_dim(part, chip ^ mask, 0, keepdims=False)
            total = total + over_blk(chunk.astype(BF), 2 * mask).astype(F32)
        total = total.astype(BF)
        rel = jnp.stack([total] + [over_blk(total, 2 * mask) for mask in (1, 2, 3)])
        half = jnp.concatenate(
            [lax.dynamic_index_in_dim(rel, n ^ chip, 0, keepdims=False) for n in range(4)], axis=0
        )
        other = over_blk(half, 1)
        first = jnp.where(core == 0, half, other)
        second = jnp.where(core == 0, other, half)
        return jnp.concatenate([first, second], axis=0).astype(F32)

    emb_act = embed_features(timesteps, image_embed).astype(BF)
    scale_shift = (
        jnp.einsum("ie,esc->isc", emb_act, embed_weight, preferred_element_type=F32) + embed_bias
    )
    local_vec = jnp.concatenate(
        [
            jnp.stack([norm1_gain, norm1_bias, norm2_gain, norm2_bias, norm3_gain, norm3_bias]),
            scale_shift.reshape(4, width),
            jnp.zeros((6, width), F32),
        ],
        axis=0,
    )
    all_vec = lax.all_gather(local_vec, "ch", axis=0)
    emb_rows = lax.dynamic_slice_in_dim(all_vec, 6 + 2 * i, 2, 1)
    vec = jnp.concatenate([all_vec[:, :6], emb_rows], axis=1)

    x_own, x_oth = halves(block_input)
    w1_own = conv1_weight.reshape(-1, width)
    w1_oth = other_shard(w1_own)
    x_all = jnp.concatenate([x_own, x_oth], axis=1)
    x_top, x_bot = halo_rows(x_all)
    x_f = x_all.astype(F32)
    zeros6 = jnp.zeros((6, channels), F32)
    sums1 = blk_sum(
        jnp.concatenate([jnp.sum(x_f, axis=0)[None], jnp.sum(x_f * x_f, axis=0)[None], zeros6])
    )
    w2_own = conv2_weight.reshape(-1, width)
    w2_oth = other_shard(w2_own)
    heads = lambda v: v.reshape(channels, 2, HEAD)
    wp_own = jnp.concatenate(
        [
            heads(qkv_weight[:, 1]),
            heads(qkv_weight[:, 2]),
            heads(qkv_weight[:, 0] * 0.125),
            heads(out_weight.T),
        ],
        axis=2,
    ).reshape(channels, 2 * HALF)
    wp_oth = over_ch(wp_own, 2)
    cot_own, cot_oth = halves(cotangent)
    cot_top, cot_bot = halo_rows(cot_own)

    j = b // split
    ctx_rows = -(-ctx_len // 16) * 16
    ctx_w = jnp.stack(
        [
            lax.dynamic_slice_in_dim(
                ctx_weight, 128 * (hh + 2 * (j // 2)) + HEAD * (j % 2), HEAD, 2
            ).reshape(-1, 2 * HEAD)
            for hh in range(2)
        ]
    )
    ctx_term = jnp.einsum("itx,hxk->ihtk", context, ctx_w, preferred_element_type=F32)
    ctx_kv = lax.psum_scatter(
        ctx_term.astype(BF).reshape(4, ctx_len, 2 * HEAD), "ch", scatter_dimension=0
    )
    ctx_kv = jnp.pad(ctx_kv, ((0, ctx_rows - ctx_len), (0, 0)))
    live = (CLIPTOK + lax.dynamic_slice_in_dim(text_len, i, 1, 0)).astype(jnp.int32)

    conv_flops = 2 * pix * 9 * channels * HALF
    ext_rows = pix + 2 * COLS
    kind = dict(cells=cells, size=size)
    w_scratch = ((9 * channels, HALF), BF)

    hid_own, hid_part, act1 = call(
        functools.partial(conv_kernel, which=0, **kind),
        [scal, x_own, x_oth, x_top, x_bot, sums1, vec, w1_own, w1_oth],
        [((pix, HALF), BF), ((8, HALF), F32), ((pix, channels), BF)],
        [((ext_rows, channels), BF), w_scratch],
        conv_flops,
    )
    hid_oth = over_ch(hid_own, 1)
    hid_top, hid_bot = halo_rows(jnp.concatenate([hid_own, hid_oth], axis=1))
    hid_sum = blk_sum(hid_part)
    sums2 = jnp.concatenate([hid_sum, over_ch(hid_sum, 1)], axis=1)

    res_f, res_own, res_part, act2 = call(
        functools.partial(conv_kernel, which=1, **kind),
        [scal, hid_own, hid_oth, hid_top, hid_bot, sums2, vec, w2_own, w2_oth, x_own],
        [((pix, HALF), F32), ((pix, HALF), BF), ((8, HALF), F32), ((pix, channels), BF)],
        [((ext_rows, channels), BF), w_scratch],
        conv_flops,
    )
    res_oth = over_ch(res_own, 1)
    res_sum = blk_sum(res_part)
    sums3 = jnp.concatenate([res_sum, over_ch(res_sum, 1)], axis=1)

    packed, act3, cot_all = call(
        functools.partial(qkv_kernel, **kind),
        [scal, res_own, res_oth, sums3, vec, cot_own, cot_oth, wp_own, wp_oth],
        [((4, pix, HALF), BF), ((pix, channels), BF), ((pix, channels), BF)],
        (),
        4 * pix * channels * 4 * HALF,
    )
    recv = lax.all_to_all(packed.reshape(blocks, pix // split, HALF), "blk", 0, 0)
    recv = recv.reshape(-1, HALF)
    queries = recv.shape[0]
    if split == 2:
        kva, kvb = recv, over_blk(recv[:, :LANES], 1)
    else:
        groups = [[n * split + m for m in range(split)] for n in range(4)]
        kv_all = lax.all_gather(
            recv[:, :LANES], "blk", axis=0, tiled=True, axis_index_groups=groups
        )
        kva, kvb = kv_all[: kv_all.shape[0] // 2], kv_all[kv_all.shape[0] // 2 :]
    dqo, dkva, dkvb, dctx = attend(live, recv, kva, kvb, ctx_kv)
    if split == 2:
        d_kv = dkva + over_blk(dkvb, 1).astype(F32)
        d_ctx = dctx + over_blk(dctx, 1)
    else:
        d_kv = lax.psum_scatter(
            jnp.concatenate([dkva, dkvb.astype(F32)], axis=0),
            "blk",
            scatter_dimension=0,
            axis_index_groups=groups,
            tiled=True,
        )
        d_ctx = lax.psum(dctx, "blk", axis_index_groups=groups)
    back = jnp.concatenate([d_kv.astype(BF), dqo], axis=1)
    grads = lax.all_to_all(back.reshape(blocks, pix // split, HALF), "blk", 0, 0)
    grads = grads.reshape(4, pix, HALF)

    p3_own, p3_oth, st3 = call(
        functools.partial(qkv_back_kernel, **kind),
        [scal, grads, wp_own, wp_oth, res_own, res_oth, sums3, vec],
        [((pix, HALF), F32), ((pix, HALF), BF), ((8, channels), F32)],
        [((pix, channels), F32)],
        2 * pix * channels * 4 * HALF,
    )

    def exchange(part_own, part_oth, stats):
        recv_part = over_ch(part_oth, 1)
        own_stats = stats[:, :HALF] + over_ch(stats[:, HALF:], 1)
        first = (part_own[:COLS] + recv_part[:COLS].astype(F32)).astype(BF)
        last = (part_own[pix - COLS :] + recv_part[pix - COLS :].astype(F32)).astype(BF)
        return recv_part, first, last, blk_sum(own_stats)

    r3, first3, last3, stats3 = exchange(p3_own, p3_oth, st3)
    d_top3, d_bot3 = halo(first3, last3)
    res_top, res_bot = halo_rows(res_own)
    low_grad = [((pix, HALF), F32), ((pix, HALF), BF), ((8, channels), F32)]
    d_resid, ext2, p2_own, p2_oth, st2 = call(
        functools.partial(conv_back_kernel, which=2, **kind),
        [
            scal, p3_own, r3, d_top3, d_bot3, res_own, res_top, res_bot, res_sum, stats3, vec,
            w2_own, w2_oth, hid_own, hid_oth, sums2, cot_own, cot_top, cot_bot,
        ],
        [((pix, HALF), F32), ((ext_rows, HALF), BF)] + low_grad,
        [w_scratch, ((pix, channels), F32)],
        conv_flops,
    )
    r2, first2, last2, stats2 = exchange(p2_own, p2_oth, st2)
    d_top2, d_bot2 = halo(first2, last2)
    ext1, p1_own, p1_oth, st1 = call(
        functools.partial(conv_back_kernel, which=1, **kind),
        [
            scal, p2_own, r2, d_top2, d_bot2, hid_own, hid_top[:, :HALF], hid_bot[:, :HALF],
            hid_sum, stats2, vec, w1_own, w1_oth, x_own, x_oth, sums1,
        ],
        [((ext_rows, HALF), BF)] + low_grad,
        [w_scratch, ((pix, channels), F32)],
        conv_flops,
    )

    def conv_weight_grad(act, ext):
        shard_parts = by_image(ext[:, :LANES], ext[:, LANES:])
        act_there = over_ch(act, 2)
        ext_there = over_ch(shard_parts[1], 2)
        return call(
            weight_grad_kernel,
            [act, act_there, shard_parts[0], ext_there],
            [((9 * channels, width), F32)],
            [((pix, 9 * LANES), BF)],
            conv_flops,
            scalars=0,
        )[0]

    grad1_part = conv_weight_grad(act1, ext1)
    grad2_part = conv_weight_grad(act2, ext2)

    recv_part1 = over_ch(p1_oth, 1)
    stats1 = blk_sum(st1[:, :HALF] + over_ch(st1[:, HALF:], 1))
    in_keep, in_send = call(
        functools.partial(last_kernel, **kind),
        [scal, p1_own, recv_part1, x_own, sums1[:, :HALF], stats1, vec, d_resid],
        [((pix, width), F32), ((pix, width), BF)],
        [((pix, HALF), F32)],
    )
    input_grad = jnp.stack(by_image(in_keep, over_ch(in_send, 2).astype(F32))).reshape(
        block_input.shape
    )

    proj_own, proj_oth, wp_keep, wp_send = call(
        out_kernel,
        [scal, grads, wp_own, wp_oth, act3, cot_all],
        [
            ((pix, HALF), F32),
            ((pix, HALF), BF),
            ((channels, 2 * HALF), F32),
            ((channels, 2 * HALF), BF),
        ],
        [((pix, channels), F32)],
        6 * pix * channels * 4 * HALF,
    )
    out_own = (res_f + proj_own + over_ch(proj_oth, 1).astype(F32)).astype(BF)
    out_keep, out_send = by_image(out_own[:, :LANES], out_own[:, LANES:])
    block_output = jnp.stack(by_image(out_keep, over_ch(out_send, 2))).reshape(block_input.shape)
    wp_part = wp_keep + over_ch(wp_send, 2).astype(F32)
    grad1 = all_reduce(grad1_part)
    bundle = all_reduce(
        jnp.concatenate([grad2_part, wp_part.reshape(-1, LANES)], axis=0)
    )
    grad2 = bundle[: 9 * channels]
    wp_grad = bundle[9 * channels :].reshape(channels, 2, 4, HEAD)
    qkv_grad = jnp.stack(
        [
            wp_grad[:, :, 2].reshape(channels, width) * 0.125,
            wp_grad[:, :, 0].reshape(channels, width),
            wp_grad[:, :, 1].reshape(channels, width),
        ],
        axis=1,
    )
    out_grad = wp_grad[:, :, 3].reshape(channels, width).T

    def both_images(stats):
        mine, theirs = by_image(stats[:2, :LANES], stats[:2, LANES:])
        return jnp.stack(by_image(mine, over_ch(theirs, 2)))

    ab1, ab2, ab3 = both_images(stats1), both_images(stats2), both_images(stats3)
    grow = 1.0 + scale_shift[:, 0]
    d_shift = ab2[:, 0]
    d_scale = norm2_gain * ab2[:, 1] + norm2_bias * ab2[:, 0]
    d_scale_shift = jnp.stack((d_scale, d_shift), axis=1)
    embed_weight_grad = (
        emb_act[0].astype(F32)[:, None, None] * d_scale_shift[0]
        + emb_act[1].astype(F32)[:, None, None] * d_scale_shift[1]
    )

    d_ctx = lax.all_gather(d_ctx[:ctx_len].astype(BF), "ch", axis=0)
    d_ctx = d_ctx.reshape(images, 2, ctx_len, 2 * HEAD)
    features = context.shape[2] // split
    ctx_part = lax.dynamic_slice_in_dim(context, (b % split) * features, features, 2)
    ctx_partial = jnp.einsum("itx,ihtk->xhk", ctx_part, d_ctx, preferred_element_type=F32)
    ctx_grad = lax.all_gather(ctx_partial.astype(BF), "blk", axis=0)
    ctx_grad = ctx_grad.reshape(2, 2, split, features, 2, 2, HEAD)
    ctx_grad = jnp.transpose(ctx_grad, (2, 3, 5, 0, 4, 1, 6)).astype(F32)

    return (
        block_output,
        input_grad,
        grad1.reshape(conv1_weight.shape),
        grad2.reshape(conv2_weight.shape),
        embed_weight_grad,
        jnp.sum(d_scale_shift, axis=0),
        jnp.sum(ab1[:, 1], axis=0),
        jnp.sum(ab1[:, 0], axis=0),
        jnp.sum(grow * ab2[:, 1], axis=0),
        jnp.sum(grow * ab2[:, 0], axis=0),
        jnp.sum(ab3[:, 1], axis=0),
        jnp.sum(ab3[:, 0], axis=0),
        qkv_grad,
        out_grad,
        ctx_grad.reshape(ctx_weight.shape),
    )


def solution(mesh):
    return jax.shard_map(
        body,
        mesh=mesh,
        in_specs=(
            P(None, "blk", None, "ch"),
            P(None, "blk", None, "ch"),
            P(),
            P(),
            P(),
            P(None, None, "ch"),
            P(None, None, None, "ch"),
            P(None, None, None, "ch"),
            P(None, None, "ch"),
            P(None, "ch"),
            P("ch"),
            P("ch"),
            P("ch"),
            P("ch"),
            P("ch"),
            P("ch"),
            P(None, None, "ch"),
            P("ch", None),
            P("ch", None, None),
        ),
        out_specs=(
            P(None, "blk", None, "ch"),
            P(None, "blk", None, "ch"),
            P(None, None, None, "ch"),
            P(None, None, None, "ch"),
            P(None, None, "ch"),
            P(None, "ch"),
            P("ch"),
            P("ch"),
            P("ch"),
            P("ch"),
            P("ch"),
            P("ch"),
            P(None, None, "ch"),
            P("ch", None),
            P("ch", None, None),
        ),
        check_vma=False,
    )
```

```python
import functools
import math

import jax
import jax.numpy as jnp
from jax import lax
from jax.experimental import pallas as pl
from jax.experimental.pallas import tpu as pltpu
from jax.sharding import PartitionSpec as P

HEAD = 64
GROUPS = 32
CLIPTOK = 4
LANES = 128
HALF = 256
COLS = 64
VMEM_BYTES = 56 * 2**20
BF = jnp.bfloat16
F32 = jnp.float32

H, I, UP1, DOWN1, UP2, DOWN2, Z, B = range(8)


def dot(a, b):
    return jnp.dot(a, b, preferred_element_type=F32)


def dot_t(a, b):
    return lax.dot_general(a, b, (((1,), (1,)), ((), ())), preferred_element_type=F32)


def group_sum(vec, size):
    lane = lax.broadcasted_iota(jnp.int32, vec.shape, 1)
    step = 1
    while step < size:
        low = pltpu.roll(vec, step, 1)
        high = pltpu.roll(vec, LANES - step, 1)
        vec = vec + jnp.where((lane & step) != 0, low, high)
        step *= 2
    return vec


def shards(scal):
    h = scal[H]
    return (h, h + 2, 1 - h, 3 - h)


def lanes_of(shard):
    return pl.ds(pl.multiple_of(shard * LANES, LANES), LANES)


def part_of(quarter):
    return slice((quarter % 2) * LANES, (quarter % 2 + 1) * LANES)


def norm_stats(scal, sums, quarter, cells, size):
    wide = sums.shape[2] == HALF
    kinds = 2 if wide else 4
    shard = shards(scal)[quarter]
    total = None
    for source in range(sums.shape[0] // kinds):
        row = source * kinds + (shard % 2 if wide else shard)
        piece = sums[pl.ds(row, 1)][0]
        total = piece if total is None else total + piece
    if wide:
        total = total[:, part_of(quarter)]
    total = group_sum(total, size)
    mean = total[0:1] / cells
    inv = lax.rsqrt(total[1:2] / cells - mean * mean + 1e-05)
    return mean, inv


def affine_of(scal, vec, quarter, which, mean, inv):
    row = vec[pl.ds(shards(scal)[quarter], 1)][0]
    gain = row[2 * which + 2 : 2 * which + 3]
    bias = row[2 * which + 3 : 2 * which + 4]
    if which == 1:
        first = scal[I] == 0
        grow = 1.0 + jnp.where(first, row[8:9], row[10:11])
        gain, bias = gain * grow, bias * grow + jnp.where(first, row[9:10], row[11:12])
    slope = inv * gain
    return gain, slope, bias - mean * slope


def column_sums(first, second):
    rows = jnp.concatenate(
        [jnp.sum(first, axis=0, keepdims=True), jnp.sum(second, axis=0, keepdims=True)], axis=0
    )
    return jnp.concatenate([rows, jnp.zeros((6, rows.shape[1]), F32)], axis=0)


def shift_columns(total, left, right):
    col = lax.broadcasted_iota(jnp.int32, total.shape, 0) % COLS
    rows = total.shape[0]
    total = total + jnp.where(col > 0, pltpu.roll(left, 1, 0), 0.0)
    return total + jnp.where(col < COLS - 1, pltpu.roll(right, rows - 1, 0), 0.0)


def silu_slope(field):
    sigma = jax.nn.sigmoid(field)
    return sigma * (1.0 + field * (1.0 - sigma))


def masked_rows(scal, value, flag):
    return jnp.where(scal[flag] > 0, value, 0.0)


def input_sums_kernel(scal, field, vec, chunk, out, mine, theirs, both, *, blocks):
    i = scal[I]
    pix = mine.shape[0]
    mine[...] = field[pl.ds(i, 1)][0]
    theirs[...] = field[pl.ds(1 - i, 1)][0]
    both[0:pix] = theirs[...]
    both[pix:] = chunk[...]
    for image in range(2):
        value = field[image].astype(F32)
        sums = column_sums(value, value * value)[:2]
        sums = jnp.concatenate([sums, vec[2:]], axis=0)
        for target in range(blocks):
            out[4 * target + 2 * image] = sums
            out[4 * target + 2 * image + 1] = sums


def image_split_kernel(scal, field, mine, theirs):
    mine[...] = field[pl.ds(scal[I], 1)][0]
    theirs[...] = field[pl.ds(1 - scal[I], 1)][0]


def spread(out, sums):
    for target in range(out.shape[0]):
        out[target] = sums


def conv1_kernel(scal, own, oth, top, bot, sums, weight, out, out_sums, act_out, vec, act_scr, *, cells, size):
    pix = own.shape[0]
    vec[...] = sums[0:4]
    rows = pix + 2 * COLS
    for quarter in range(4):
        shard = shards(scal)[quarter]
        mean, inv = norm_stats(scal, sums, quarter, cells, size)
        gain, slope, offset = affine_of(scal, vec, quarter, 0, mean, inv)
        lanes = slice(quarter * LANES, (quarter + 1) * LANES)

        def active(field):
            pre = field.astype(F32) * slope + offset
            return pre * jax.nn.sigmoid(pre)

        half = own if quarter < 2 else oth
        main = active(half[:, part_of(quarter)]).astype(BF)
        above, below = active(top[:, lanes]), active(bot[:, lanes])
        act_scr[2 * COLS : 2 * COLS + pix, lanes_of(shard)] = main
        act_out[:, lanes_of(shard)] = main
        act_scr[0:COLS, lanes_of(shard)] = masked_rows(scal, above[:COLS], UP2).astype(BF)
        act_scr[COLS : 2 * COLS, lanes_of(shard)] = masked_rows(scal, above[COLS:], UP1).astype(BF)
        end = 2 * COLS + pix
        act_scr[end : end + COLS, lanes_of(shard)] = masked_rows(scal, below[:COLS], DOWN1).astype(BF)
        act_scr[end + COLS :, lanes_of(shard)] = masked_rows(scal, below[COLS:], DOWN2).astype(BF)
    result = convolve(act_scr, weight, rows)
    out[...] = result.astype(BF)
    inner = result[COLS : COLS + pix]
    spread(out_sums, column_sums(inner, inner * inner))


def convolve(act_scr, weight, rows):
    channels = act_scr.shape[1]
    parts = []
    for kx in range(3):
        acc = None
        for ky in range(3):
            tap = (ky * 3 + kx) * channels
            term = dot(act_scr[ky * COLS : ky * COLS + rows, :], weight[tap : tap + channels, :])
            acc = term if acc is None else acc + term
        parts.append(acc)
    return shift_columns(parts[1], parts[0], parts[2])


def conv2_kernel(scal, own, oth, sums, vec, weight, base, act_below, out_f, out_low, out_sums, act_first, act_out, edges, act_scr, *, cells, size):
    pix = base.shape[0]
    cut = act_first.shape[0]
    act_first[...] = act_below[0:cut]
    act_out[0 : pix - cut, :] = act_below[cut:]
    for quarter in range(4):
        shard = shards(scal)[quarter]
        mean, inv = norm_stats(scal, sums, quarter, cells, size)
        gain, slope, offset = affine_of(scal, vec, quarter, 1, mean, inv)
        half = own if quarter < 2 else oth
        pre = half[:, part_of(quarter)].astype(F32) * slope + offset
        act = pre * jax.nn.sigmoid(pre)
        main = act[COLS : COLS + pix].astype(BF)
        act_scr[COLS : COLS + pix, lanes_of(shard)] = main
        act_out[pix - cut :, lanes_of(shard)] = main
        act_scr[0:COLS, lanes_of(shard)] = masked_rows(scal, act[:COLS], UP1).astype(BF)
        act_scr[COLS + pix :, lanes_of(shard)] = masked_rows(scal, act[COLS + pix :], DOWN1).astype(BF)
    result = convolve(act_scr, weight, pix) + base[...].astype(F32)
    out_f[...] = result
    low = result.astype(BF)
    out_low[...] = low
    if edges.shape[1] < pix:
        edges[0], edges[1] = low[: edges.shape[1]], low[pix - edges.shape[1] :]
    else:
        edges[0], edges[1] = low, low
    spread(out_sums, column_sums(result, result * result))


def qkv_kernel(scal, own, oth, sums, vec, cot_own, cot_oth, weight, out, act_out, cot_out, edges, *, cells, size):
    rows = edges.shape[1]
    edges[0], edges[1] = cot_own[0:rows], cot_own[cot_own.shape[0] - rows :]
    for quarter in range(4):
        shard = shards(scal)[quarter]
        mean, inv = norm_stats(scal, sums, quarter, cells, size)
        gain, slope, offset = affine_of(scal, vec, quarter, 2, mean, inv)
        half = own if quarter < 2 else oth
        cot = cot_own if quarter < 2 else cot_oth
        field = half[:, part_of(quarter)].astype(F32)
        act_out[:, lanes_of(shard)] = (field * slope + offset).astype(BF)
        cot_out[:, lanes_of(shard)] = cot[:, part_of(quarter)]
    for head in range(4):
        columns = weight[:, head * HALF : (head + 1) * HALF]
        fwd = dot(act_out[...], columns)
        back = dot(cot_out[...], columns[:, LANES:])
        out[head, :, :LANES] = fwd[:, :LANES].astype(BF)
        lane = lax.broadcasted_iota(jnp.int32, back.shape, 1)
        out[head, :, LANES:] = jnp.where(lane < HEAD, fwd[:, LANES:], back).astype(BF)


def below_stats(scal, total, own, oth, sums, vec, out_own, out_oth, out_stats, which, cells, size):
    rows = total.shape[0]
    pix = rows - 2 * COLS if which == 1 else rows
    inner = slice(COLS, COLS + pix) if which == 1 else slice(0, pix)
    for quarter in range(4):
        shard = shards(scal)[quarter]
        mean, inv = norm_stats(scal, sums, quarter, cells, size)
        gain, slope, offset = affine_of(scal, vec, quarter, which, mean, inv)
        half = own if quarter < 2 else oth
        part = part_of(quarter)
        if quarter < 2:
            out_own[:, part] = total[:, lanes_of(shard)]
        else:
            out_oth[:, part] = total[:, lanes_of(shard)].astype(BF)
        grad = total[inner, lanes_of(shard)]
        field = half[inner, part].astype(F32)
        if which < 2:
            grad = grad * silu_slope(field * slope + offset)
        result = column_sums(grad, grad * ((field - mean) * inv))
        slot = scal[H] if quarter < 2 else 1 - scal[H]
        for target in range(out_stats.shape[0] // 2):
            out_stats[pl.ds(2 * target + slot, 1), :, part] = result[None]


def qkv_back_kernel(scal, grads, weight, own, oth, sums, vec, out_own, out_oth, out_stats, tot_scr, *, cells, size):
    total = None
    for head in range(4):
        columns = weight[:, head * HALF : (head + 1) * HALF]
        grad = grads[head]
        lane = lax.broadcasted_iota(jnp.int32, grad.shape, 1)
        term = dot_t(jnp.where(lane < 3 * HEAD, grad, jnp.zeros_like(grad)), columns)
        total = term if total is None else total + term
    tot_scr[...] = total
    below_stats(scal, tot_scr, own, oth, sums, vec, out_own, out_oth, out_stats, 2, cells, size)


def out_kernel(scal, grads, weight, act, cot, proj_own, proj_oth, keep, mine, send, tot_scr, wgrad):
    channels = act.shape[1]
    act_t = act[...].astype(F32).T.astype(BF)
    total = None
    for pair in range(2):
        slot = jnp.where(scal[I] == pair, 0, 1)
        parts, outs = [], []
        for head in (2 * pair, 2 * pair + 1):
            columns = weight[:, head * HALF + LANES : (head + 1) * HALF]
            grad = grads[head]
            low = grad[:, LANES:]
            lane = lax.broadcasted_iota(jnp.int32, low.shape, 1)
            term = dot_t(jnp.where(lane < HEAD, jnp.zeros_like(low), low), columns)
            total = term if total is None else total + term
            parts.append(dot(act_t, grad))
            outs.append(dot(low.astype(F32).T[HEAD:].astype(BF), cot[...]))
        first, second = parts
        pieces = [
            jnp.concatenate([first[:, LANES : LANES + HEAD], second[:, LANES : LANES + HEAD]], axis=1)
            * 0.125,
            jnp.concatenate([first[:, :HEAD], second[:, :HEAD]], axis=1),
            jnp.concatenate([first[:, HEAD:LANES], second[:, HEAD:LANES]], axis=1),
        ]
        both = jnp.concatenate(outs, axis=0)
        pieces += [both[:, n * LANES : (n + 1) * LANES] for n in range(channels // LANES)]
        wgrad[pl.ds(slot, 1)] = jnp.concatenate(pieces, axis=0)[None]
    keep[...] = wgrad[0].astype(BF)
    core, half = scal[B] % 2, mine.shape[0]
    mine[...] = wgrad[1, pl.ds(pl.multiple_of(core * half, half), half), :]
    send[...] = wgrad[1, pl.ds(pl.multiple_of((1 - core) * half, half), half), :].astype(BF)
    tot_scr[...] = total
    for quarter, shard in enumerate(shards(scal)):
        if quarter < 2:
            proj_own[:, part_of(quarter)] = tot_scr[:, lanes_of(shard)]
        else:
            proj_oth[:, part_of(quarter)] = tot_scr[:, lanes_of(shard)].astype(BF)


def total_stats(stats):
    total = stats[0]
    for source in range(1, stats.shape[0]):
        total = total + stats[source]
    return total


def norm_back(scal, quarter, sums, stats, vec, which, cells, size):
    mean, inv = norm_stats(scal, sums, quarter, cells, size)
    gain, slope, offset = affine_of(scal, vec, quarter, which, mean, inv)
    means = group_sum(total_stats(stats)[:, part_of(quarter)] * gain, size) / cells

    def back(grad, field):
        field = field.astype(F32)
        hat = (field - mean) * inv
        if which < 2:
            grad = grad * silu_slope(field * slope + offset)
        return (grad * gain - means[0:1] - hat * means[1:2]) * inv

    return back


def norm3_back_kernel(
    scal, part, recv, dtop, dbot, field, ftop, fbot, cot, ctop, cbot, sums, stats, vec, out_f, ext, away, *, cells, size
):
    pix = part.shape[0]
    end = 2 * COLS + pix
    for quarter in range(2):
        lanes = part_of(quarter)
        back = norm_back(scal, quarter, sums, stats, vec, 2, cells, size)
        main = back(part[:, lanes] + recv[:, lanes].astype(F32), field[:, lanes])
        main = main + cot[:, lanes].astype(F32)
        out_f[:, lanes] = main
        ext[2 * COLS : end, lanes] = main.astype(BF)
        head = back(dtop[:, lanes].astype(F32), ftop[:, lanes]) + ctop[:, lanes].astype(F32)
        tail = back(dbot[:, lanes].astype(F32), fbot[:, lanes]) + cbot[:, lanes].astype(F32)
        ext[0:COLS, lanes] = masked_rows(scal, head[:COLS], UP2).astype(BF)
        ext[COLS : 2 * COLS, lanes] = masked_rows(scal, head[COLS:], UP1).astype(BF)
        ext[end : end + COLS, lanes] = masked_rows(scal, tail[:COLS], DOWN1).astype(BF)
        ext[end + COLS :, lanes] = masked_rows(scal, tail[COLS:], DOWN2).astype(BF)
    away[...] = ext[COLS : end + COLS, lanes_of(1 - scal[I])]


def norm2_back_kernel(scal, part, recv, field, sums, stats, vec, ext, away, *, cells, size):
    rows = part.shape[0]
    for quarter in range(2):
        lanes = part_of(quarter)
        back = norm_back(scal, quarter, sums, stats, vec, 1, cells, size)
        main = back(part[:, lanes] + recv[:, lanes].astype(F32), field[:, lanes])
        ext[0:COLS, lanes] = masked_rows(scal, main[:COLS], UP1).astype(BF)
        ext[COLS : rows - COLS, lanes] = main[COLS : rows - COLS].astype(BF)
        ext[rows - COLS :, lanes] = masked_rows(scal, main[rows - COLS :], DOWN1).astype(BF)
    away[...] = ext[:, lanes_of(1 - scal[I])]


def conv_back_kernel(scal, ext, weight, own, oth, sums, vec, out_own, out_oth, out_stats, tot_scr, *, which, cells, size):
    rows, channels = tot_scr.shape
    parts = []
    for kx in range(3):
        acc = None
        for ky in range(3):
            tap = (ky * 3 + kx) * channels
            start = (2 - ky) * COLS
            term = dot_t(ext[start : start + rows, :], weight[tap : tap + channels, :])
            acc = term if acc is None else acc + term
        parts.append(acc)
    tot_scr[...] = shift_columns(parts[1], parts[2], parts[0])
    below_stats(scal, tot_scr, own, oth, sums, vec, out_own, out_oth, out_stats, which, cells, size)


def last_kernel(scal, part, recv, field, sums, stats, vec, resid_grad, keep, send, tot_scr, *, cells, size):
    i = scal[I]
    for quarter in range(2):
        lanes = part_of(quarter)
        back = norm_back(scal, quarter, sums, stats, vec, 0, cells, size)
        main = back(part[:, lanes] + recv[:, lanes].astype(F32), field[:, lanes])
        tot_scr[:, lanes] = main + resid_grad[:, lanes]
    keep[...] = tot_scr[:, lanes_of(i)]
    send[...] = tot_scr[:, lanes_of(1 - i)].astype(BF)


def weight_grads(scal, act_one, act_two, ext_one, ext_two, rhs_scr, out_scr):
    pix, channels = act_one.shape
    rows = ext_two.shape[0]
    first = (ext_one.shape[0] - rows) // 2
    own = ext_one[first : first + rows, lanes_of(scal[I])]
    products = []
    for act, wide in ((act_one, own), (act_two, ext_two[...])):
        wide = wide.astype(F32)
        col = lax.broadcasted_iota(jnp.int32, wide.shape, 0) % COLS
        for kx in range(3):
            if kx == 0:
                moved = jnp.where(col < COLS - 1, pltpu.roll(wide, rows - 1, 0), 0.0)
            elif kx == 2:
                moved = jnp.where(col > 0, pltpu.roll(wide, 1, 0), 0.0)
            else:
                moved = wide
            moved = moved.astype(BF)
            for ky in range(3):
                start = (2 - ky) * COLS
                tap = ky * 3 + kx
                lanes = slice(tap * LANES, (tap + 1) * LANES)
                rhs_scr[len(products), :, lanes] = moved[start : start + pix]
        products.append(act.astype(F32).T.astype(BF))
    for tap in range(9):
        lanes = slice(tap * LANES, (tap + 1) * LANES)
        total = dot(products[0], rhs_scr[0, :, lanes]) + dot(products[1], rhs_scr[1, :, lanes])
        out_scr[tap * channels : (tap + 1) * channels, :] = total


def weight_grad_one_kernel(
    scal, up, low, up_there, low_there, ext_one, ext_two, wp, wp_there, keep, send, rhs_scr, out_scr, wp_scr
):
    cut = up.shape[0]
    mine = jnp.concatenate([up[...], low[0:cut]], axis=0)
    theirs = jnp.concatenate([up_there[...], low_there[0:cut]], axis=0)
    weight_grads(scal, mine, theirs, ext_one, ext_two, rhs_scr, out_scr)
    core = scal[B] % 2
    half = wp_there.shape[0]
    at = lambda n, size: pl.ds(pl.multiple_of(n * size, size), size)
    wp_scr[...] = wp[...].astype(F32)
    wp_scr[at(core, half), :] += wp_there[...].astype(F32)
    for source, first in ((out_scr, 0), (wp_scr, out_scr.shape[0] // 8)):
        count = source.shape[0] // 2
        where = slice(first, first + count // 4)
        keep[:, where] = source[at(core, count), :].reshape(4, count // 4, LANES)
        send[:, where] = source[at(1 - core, count), :].astype(BF).reshape(4, count // 4, LANES)


def weight_grad_two_kernel(scal, act, act_there, ext_one, ext_two, out, rhs_scr, out_scr):
    cut = act.shape[0] // 3
    weight_grads(scal, act[cut:], act_there[cut:], ext_one, ext_two, rhs_scr, out_scr)
    out[...] = out_scr[...].astype(BF).reshape(out.shape)


def total_kernel(scal, own, parts, one, two, three, out):
    count = own.shape[0]
    first = own[...] + one[...].astype(F32) + two[...].astype(F32) + three[...].astype(F32)
    out[0:count] = first.astype(BF)
    second = parts[0].astype(F32)
    for source in range(1, parts.shape[0]):
        second = second + parts[source].astype(F32)
    out[count:] = second.astype(BF)


def scatter_kernel(scal, keep, recv, own, *sends):
    chip = scal[B] // 2
    for mask in range(4):
        chunk = pl.ds(chip ^ mask, 1)
        value = (keep[chunk] + recv[chunk].astype(F32))[0]
        if mask == 0:
            own[...] = value
        else:
            sends[mask - 1][...] = value.astype(BF)


def place_kernel(scal, *refs):
    pieces, (one, two, qkv, out) = refs[:8], refs[8:]
    core, chip = scal[B] % 2, scal[B] // 2
    count = one.shape[0] // 8
    rows = qkv.shape[0] // 6
    for n, piece in enumerate(pieces):
        half = core if n < 4 else 1 - core
        source = chip ^ (n % 4)
        at = lambda slot, size: pl.ds(pl.multiple_of(slot * size, size), size)
        slot = 4 * half + source
        one[at(slot, count), :] = piece[:count].astype(F32)
        two[at(2 * source + half, count), :] = piece[count + rows :].astype(F32)
        extra = piece[count : count + rows].astype(F32)

        @pl.when(slot < 6)
        def _(extra=extra, slot=slot):
            qkv[at(slot, rows), :] = extra

        @pl.when(slot >= 6)
        def _(extra=extra, slot=slot):
            for m in range(rows // LANES):
                column = (slot - 6) * (rows // LANES) + m
                out[:, lanes_of(column)] = extra[m * LANES : (m + 1) * LANES]


def merge_kernel(scal, mine, recv, rest, out):
    out[:, :LANES] = (mine[...] + recv[...].astype(F32)).astype(BF)
    out[:, LANES:] = rest[...]


def context_grad_kernel(scal, context, d_zero, d_one, d_two, d_three, out, tot_scr, *, split):
    rows = out.shape[0]
    turned = [context[image].astype(F32).T.astype(BF) for image in range(2)]
    pieces = (d_zero, d_one, d_two, d_three)
    for h in range(2):
        total = None
        for image in range(2):
            slot = (2 * image + h) ^ scal[Z]
            chosen = pieces[0][...]
            for n in range(1, 4):
                chosen = jnp.where(slot == n, pieces[n][...], chosen)
            term = dot(turned[image], chosen)
            total = term if total is None else total + term
        tot_scr[:, h * LANES : (h + 1) * LANES] = total
    part = scal[B] % split
    out[...] = tot_scr[pl.ds(pl.multiple_of(part * rows, rows), rows), :].astype(BF)


def context_place_kernel(scal, pieces, out, *, split):
    rows = pieces.shape[1]
    for part in range(split):
        for t in range(2):
            first, second = ((2 * t + n) * split + part for n in range(2))
            for h in range(2):
                for kind in range(2):
                    start = h * LANES + kind * HEAD
                    value = jnp.concatenate(
                        [pieces[n, :, start : start + HEAD] for n in (first, second)], axis=1
                    )
                    column = (4 * kind + h + 2 * t) * LANES
                    out[part * rows : (part + 1) * rows, column : column + LANES] = value.astype(F32)


def join_kernel(scal, own, *refs):
    pieces, out = refs[:8], refs[8]
    i, b = scal[I], scal[B]
    out[:, lanes_of(i)] = own[...]
    size = own.shape[0] // 8
    for core in range(2):
        for mask in range(4):
            source = b ^ (2 * mask + core)
            target = pl.ds(pl.multiple_of(source * size, size), size)
            out[target, lanes_of(1 - i)] = pieces[4 * core + mask][...]


def place_weight_kernel(scal, own, chunks, out, *, start, width):
    i = scal[I]
    rows = own.shape[0] // width
    size = own.shape[0] // chunks.shape[0]
    for n in range(width):
        out[:, lanes_of(i * width + n)] = own[n * rows : (n + 1) * rows]
    for source in range(chunks.shape[0]):
        n, first = divmod(source * size, rows)
        out[first : first + size, lanes_of((1 - i) * width + n)] = chunks[
            source, start : start + size
        ]


def attend_kernel(
    live, qd, kva, kvb, ctx, dqo, dkva, dkvb, dctx,
    kv_scr, kt_scr, vt_scr, s_scr, e_scr, acc_scr, *, chunk, unroll,
):
    step = pl.program_id(0)
    half_a, half_b, extra = kva.shape[0], kvb.shape[0], ctx.shape[0]
    keys = half_a + half_b
    total = keys + extra
    block = qd.shape[0]

    @pl.when(step == 0)
    def _():
        kv_scr[0:half_a, :] = kva[...]
        kv_scr[half_a:keys, :] = kvb[...]
        kv_scr[keys:total, :] = ctx[...]
        acc_scr[...] = jnp.zeros_like(acc_scr)

        def turn(rows):
            flipped = kv_scr[rows, :].astype(F32).T.astype(BF)
            kt_scr[:, rows] = flipped[:HEAD]
            vt_scr[0:HEAD, rows] = flipped[HEAD:]

        def turn_step(n, carry):
            turn(pl.ds(pl.multiple_of(n * 256, 256), 256))
            return carry

        lax.fori_loop(0, keys // 256, turn_step, 0)
        turn(slice(keys, total))
        vt_scr[HEAD:, :] = jnp.ones((16, total), BF)

    both = qd[...].astype(F32).T
    q_t = both[:HEAD].astype(BF)
    zero = jnp.zeros((HEAD, block), BF)
    q_side = jnp.concatenate([q_t, zero], axis=0)

    def score(rows, top, masked):
        s = dot(kv_scr[rows, :], q_side)
        if masked:
            index = lax.broadcasted_iota(jnp.int32, s.shape, 0)
            s = jnp.where(index < live[0], s, -1e30)
        s_scr[rows, :] = s
        return jnp.maximum(top, jnp.max(s.reshape(-1, 8, block), axis=0))

    def span(n):
        return pl.ds(pl.multiple_of(n * chunk, chunk), chunk)

    def over_keys(func, carry):
        return lax.fori_loop(
            0, keys // chunk, lambda n, c: func(span(n), c), carry, unroll=unroll
        )

    tail = pl.ds(keys, extra)
    top = score(tail, jnp.full((8, block), -1e30, F32), True)
    top = over_keys(lambda rows, c: score(rows, c, False), top)
    top = jnp.max(top, axis=0, keepdims=True)

    def weigh(rows, acc):
        e = jnp.exp(s_scr[rows, :] - top).astype(BF)
        e_scr[rows, :] = e
        return acc + dot(vt_scr[:, rows], e)

    out_t = weigh(tail, jnp.zeros((HEAD + 16, block), F32))
    out_t = over_keys(weigh, out_t)
    inv = 1.0 / out_t[HEAD : HEAD + 1]
    out_t = out_t[:HEAD] * inv
    d_t = both[HEAD:]
    delta = jnp.sum(d_t * out_t, axis=0, keepdims=True) * inv
    d_t = d_t * inv
    d_side = jnp.concatenate([zero, d_t.astype(BF)], axis=0)
    zero_q = jnp.zeros((block, HEAD), BF)
    rows_q = jnp.concatenate([qd[:, :HEAD], zero_q], axis=1)
    rows_d = jnp.concatenate([zero_q, d_t.T.astype(BF)], axis=1)
    right = jnp.concatenate([rows_q, rows_d], axis=0)

    def back(rows, acc):
        d_prob = dot(kv_scr[rows, :], d_side)
        e = e_scr[rows, :]
        d_score = (e.astype(F32) * (d_prob - delta)).astype(BF)
        acc_scr[rows, :] += dot(jnp.concatenate([d_score, e], axis=1), right)
        return acc + dot(kt_scr[:, rows], d_score)

    dq_t = back(tail, jnp.zeros((HEAD, block), F32))
    dq_t = over_keys(back, dq_t)
    dqo[...] = jnp.concatenate([dq_t, out_t], axis=0).T.astype(BF)

    @pl.when(step == pl.num_programs(0) - 1)
    def _():
        dkva[...] = acc_scr[0:half_a, :]
        dkvb[...] = acc_scr[half_a:keys, :].astype(BF)
        dctx[...] = acc_scr[keys:total, :]


def attend(live, recv, kva, kvb, ctx, deps):
    queries = recv.shape[0]
    block = min(512, queries)
    half_a, half_b, extra = recv.shape[0] if kva is recv else kva.shape[0], kvb.shape[0], ctx.shape[0]
    total = half_a + half_b + extra
    whole = lambda shape: pl.BlockSpec(shape, lambda n: (0, 0))
    kernel = functools.partial(attend_kernel, chunk=512, unroll=4)

    def inner(*refs):
        kernel(*refs[:5], *refs[5 + len(deps) :])

    return pl.pallas_call(
        inner,
        grid=(queries // block,),
        in_specs=[
            pl.BlockSpec(memory_space=pltpu.SMEM),
            pl.BlockSpec((block, LANES), lambda n: (n, 1)),
            whole((half_a, LANES)),
            whole((half_b, LANES)),
            whole((extra, LANES)),
        ]
        + [pl.BlockSpec(memory_space=pl.ANY)] * len(deps),
        out_specs=[
            pl.BlockSpec((block, LANES), lambda n: (n, 0)),
            whole((half_a, LANES)),
            whole((half_b, LANES)),
            whole((extra, LANES)),
        ],
        out_shape=[
            jax.ShapeDtypeStruct((queries, LANES), BF),
            jax.ShapeDtypeStruct((half_a, LANES), F32),
            jax.ShapeDtypeStruct((half_b, LANES), BF),
            jax.ShapeDtypeStruct((extra, LANES), F32),
        ],
        scratch_shapes=[
            pltpu.VMEM((total, LANES), BF),
            pltpu.VMEM((HEAD, total), BF),
            pltpu.VMEM((HEAD + 16, total), BF),
            pltpu.VMEM((total, block), F32),
            pltpu.VMEM((total, block), BF),
            pltpu.VMEM((total, LANES), F32),
        ],
        compiler_params=pltpu.CompilerParams(vmem_limit_bytes=VMEM_BYTES),
        cost_estimate=pl.CostEstimate(
            flops=int(38 * 1.15e9), bytes_accessed=1, transcendentals=0
        ),
    )(live, recv, kva, kvb, ctx, *deps)


def call(kernel, args, outs, scratch=(), deps=(), time=0.0):
    in_vmem = pl.BlockSpec(memory_space=pltpu.VMEM)
    in_smem = pl.BlockSpec(memory_space=pltpu.SMEM)
    anywhere = pl.BlockSpec(memory_space=pl.ANY)
    count = len(args)

    def inner(*refs):
        kernel(*refs[:count], *refs[count + len(deps) :])

    return pl.pallas_call(
        inner,
        in_specs=[in_smem] + [in_vmem] * (count - 1) + [anywhere] * len(deps),
        out_specs=[in_vmem] * len(outs),
        out_shape=[jax.ShapeDtypeStruct(s, d) for s, d in outs],
        scratch_shapes=[pltpu.VMEM(s, d) for s, d in scratch],
        compiler_params=pltpu.CompilerParams(vmem_limit_bytes=VMEM_BYTES),
        cost_estimate=pl.CostEstimate(
            flops=1 + int(time * 1.15e9), bytes_accessed=1, transcendentals=0
        ),
    )(*args, *deps)


def after(values, *deps):
    anywhere = pl.BlockSpec(memory_space=pl.ANY)
    count = len(values)

    def inner(*refs):
        pass

    return pl.pallas_call(
        inner,
        in_specs=[anywhere] * (count + len(deps)),
        out_specs=[anywhere] * count,
        out_shape=[jax.ShapeDtypeStruct(v.shape, v.dtype) for v in values],
        input_output_aliases={n: n for n in range(count)},
        cost_estimate=pl.CostEstimate(flops=1, bytes_accessed=1, transcendentals=0),
    )(*values, *deps)


def embed_features(timesteps, image_embed):
    half_width = image_embed.shape[1] // 2
    freqs = jnp.exp(-math.log(10000.0) * jnp.arange(half_width, dtype=F32) / half_width)
    angles = timesteps.astype(F32)[:, None] * freqs[None, :]
    return jax.nn.silu(jnp.concatenate([jnp.cos(angles), jnp.sin(angles)], axis=1) + image_embed)


def body(
    block_input,
    cotangent,
    image_embed,
    timesteps,
    text_len,
    context,
    conv1_weight,
    conv2_weight,
    embed_weight,
    embed_bias,
    norm1_gain,
    norm1_bias,
    norm2_gain,
    norm2_bias,
    norm3_gain,
    norm3_bias,
    qkv_weight,
    out_weight,
    ctx_weight,
):
    images, row_count, col_count, width = block_input.shape
    channels = qkv_weight.shape[0]
    size = channels // GROUPS
    blocks = lax.axis_size("blk")
    pix = row_count * col_count
    cells = float(pix * blocks * size)
    split = blocks // 4
    ctx_len = context.shape[1]
    b = lax.axis_index("blk")
    z = lax.axis_index("ch")
    h, i = z % 2, z // 2
    row, rows_all = b * row_count, blocks * row_count
    inside = [row >= 1, row + row_count < rows_all, row >= 2, row + row_count + 1 < rows_all]
    scal = jnp.stack([h, i] + [flag.astype(jnp.int32) for flag in inside] + [z, b]).astype(jnp.int32)


    def over_ch(value, mask):
        return lax.ppermute(value, "ch", [(n, n ^ mask) for n in range(4)])

    def over_blk(value, mask):
        return lax.ppermute(value, "blk", [(n, n ^ mask) for n in range(blocks)])

    def ring(value, step):
        return lax.ppermute(value, "blk", [(n, (n + step) % blocks) for n in range(blocks)])

    def halo(first, last):
        if row_count >= 2:
            return ring(last, 1), ring(first, -1)
        return (
            jnp.concatenate([ring(last, 2), ring(last, 1)], axis=0),
            jnp.concatenate([ring(first, -1), ring(first, -2)], axis=0),
        )

    pairs = [[n * 4 + 2 * m + k for n in range(blocks) for k in range(2)] for m in range(2)]

    def to_image(value):
        return lax.all_to_all(value, ("blk", "ch"), 0, 0, axis_index_groups=pairs)

    def by_image(first, second):
        return jnp.where(i == 0, first, second), jnp.where(i == 0, second, first)

    def plane(value):
        mine = [value] + [over_blk(value, 2 * mask) for mask in (1, 2, 3)]
        return mine + [over_blk(piece, 1) for piece in mine]

    w1_own = conv1_weight.reshape(-1, width)
    w2_own = conv2_weight.reshape(-1, width)
    heads = lambda v: v.reshape(channels, 2, HEAD)
    wp_own = jnp.stack(
        [
            jnp.concatenate([heads(qkv_weight[:, 1]), heads(qkv_weight[:, 2])], axis=2),
            jnp.concatenate([heads(qkv_weight[:, 0] * 0.125), heads(out_weight.T)], axis=2),
        ],
        axis=0,
    )
    wp_own = jnp.transpose(wp_own, (2, 0, 1, 3)).reshape(-1, LANES)
    w1_rows, w2_rows, wp_rows = (w.shape[0] // blocks for w in (w1_own, w2_own, wp_own))
    chunk_of = lambda w: lax.dynamic_slice_in_dim(w, b * (w.shape[0] // blocks), w.shape[0] // blocks, 0)
    w1_slice = chunk_of(w1_own)

    emb_act = embed_features(timesteps, image_embed).astype(BF)
    scale_shift = (
        jnp.einsum("ie,esc->isc", emb_act, embed_weight, preferred_element_type=F32) + embed_bias
    )
    local_vec = jnp.concatenate(
        [
            jnp.zeros((2, width), F32),
            jnp.stack([norm1_gain, norm1_bias, norm2_gain, norm2_bias, norm3_gain, norm3_bias]),
            scale_shift.reshape(4, width),
            jnp.zeros((4, width), F32),
        ],
        axis=0,
    )
    x_sums, x_mine, x_theirs, x_both = call(
        functools.partial(input_sums_kernel, blocks=blocks),
        [scal, block_input.reshape(images, pix, width), local_vec, w1_slice],
        [
            ((4 * blocks, 16, width), F32),
            ((pix, width), BF),
            ((pix, width), BF),
            ((pix + w1_rows, width), BF),
        ],
    )
    x_two = over_ch(x_both, 2)
    x_three, x_one = over_ch(x_theirs, 3), over_ch(x_mine, 1)
    sums1 = lax.all_to_all(x_sums, ("blk", "ch"), 0, 0)
    two_source = jnp.concatenate([chunk_of(w2_own), chunk_of(wp_own)], axis=0)
    x_one, x_two, x_three, two_source = after((x_one, x_two, x_three, two_source))
    two_chunk = over_ch(two_source, 2)
    x_two, w1_chunk = x_two[:pix], x_two[pix:]
    wide = dict(axis=1)
    x_own = jnp.concatenate(by_image(x_mine, x_two), **wide)
    x_oth = jnp.concatenate(by_image(x_one, x_three), **wide)
    edge = min(2 * COLS, pix)
    x_top, x_bot = halo(
        jnp.concatenate([x_own[:edge], x_oth[:edge]], **wide),
        jnp.concatenate([x_own[pix - edge :], x_oth[pix - edge :]], **wide),
    )
    if blocks == 8:
        w1_pieces = plane(w1_chunk)
        w1 = call(
            join_kernel, [scal, w1_own] + w1_pieces, [((w1_own.shape[0], HALF), BF)]
        )[0]
    else:
        w1_oth = lax.all_gather(w1_chunk, "blk", axis=0, tiled=True)
        w1 = jnp.concatenate(by_image(w1_own, w1_oth), **wide)
        w1_pieces = [w1_oth]
    (two_chunk,) = after((two_chunk,), *w1_pieces[1:4])
    two = lax.all_gather(two_chunk, "blk", axis=0)
    w2 = call(
        functools.partial(place_weight_kernel, start=0, width=1),
        [scal, w2_own, two],
        [((w2_own.shape[0], HALF), BF)],
    )[0]
    j = b // split
    ctx_rows = -(-ctx_len // 16) * 16
    ctx_w = jnp.stack(
        [
            lax.dynamic_slice_in_dim(
                ctx_weight, 128 * (hh + 2 * (j // 2)) + HEAD * (j % 2), HEAD, 2
            ).reshape(-1, 2 * HEAD)
            for hh in range(2)
        ]
    )
    ctx_term = jnp.einsum("itx,hxk->ihtk", context, ctx_w, preferred_element_type=F32)
    ctx_term = jnp.pad(
        ctx_term.astype(BF).reshape(4, ctx_len, 2 * HEAD),
        ((0, 0), (0, ctx_rows - ctx_len), (0, 0)),
    )
    ctx_kv = lax.psum_scatter(ctx_term, "ch", scatter_dimension=0)
    live = (CLIPTOK + jnp.where(i == 0, text_len[0], text_len[1])).astype(jnp.int32)[None]

    conv_flops = 2 * pix * 9 * channels * HALF
    kind = dict(cells=cells, size=size)
    ext = pix + 2 * COLS
    stat_shape = ((2 * blocks, 8, HALF), F32)

    hid_own, hid_stat, act1, vec = call(
        functools.partial(conv1_kernel, **kind),
        [scal, x_own, x_oth, x_top, x_bot, sums1, w1],
        [((ext, HALF), BF), stat_shape, ((pix, channels), BF), ((4, 16, LANES), F32)],
        [((ext + 2 * COLS, channels), BF)],
    )
    hid_oth = over_ch(hid_own, 1)
    sums2 = to_image(hid_stat)

    c_mine, c_theirs = call(
        image_split_kernel,
        [scal, cotangent.reshape(images, pix, width)],
        [((pix, width), BF)] * 2,
        deps=[x_two],
    )
    c_mine, c_theirs = after((c_mine, c_theirs), hid_oth, w2)
    c_one, c_two, c_three = over_ch(c_mine, 1), over_ch(c_theirs, 2), over_ch(c_theirs, 3)
    cot_own = jnp.concatenate(by_image(c_mine, c_two), **wide)
    cot_oth = jnp.concatenate(by_image(c_one, c_three), **wide)

    edges = ((2, edge, HALF), BF)
    res_f, res_own, res_stat, act_first, act_rest, res_edges = call(
        functools.partial(conv2_kernel, **kind),
        [scal, hid_own, hid_oth, sums2, vec, w2, x_own, act1],
        [
            ((pix, HALF), F32),
            ((pix, HALF), BF),
            stat_shape,
            ((pix // 2, channels), BF),
            ((pix + pix // 2, channels), BF),
            edges,
        ],
        [((ext, channels), BF)],
    )
    res_oth = over_ch(res_own, 1)
    sums3 = to_image(res_stat)
    wp = call(
        functools.partial(place_weight_kernel, start=w2_rows, width=4),
        [scal, wp_own, two],
        [((channels, 4 * HALF), BF)],
        deps=[res_own],
    )[0]
    packed, act3, cot_all, cot_edges = call(
        functools.partial(qkv_kernel, **kind),
        [scal, res_own, res_oth, sums3, vec, cot_own, cot_oth, wp],
        [((4, pix, HALF), BF), ((pix, channels), BF), ((pix, channels), BF), edges],
        deps=[ctx_kv],
    )
    recv = lax.all_to_all(packed.reshape(blocks, pix // split, HALF), "blk", 0, 0)
    res_edges, act_first = after((res_edges, act_first), packed)
    res_top, res_bot = halo(res_edges[0], res_edges[1])
    cot_top, cot_bot = halo(cot_edges[0], cot_edges[1])
    first_there = over_ch(act_first, 2)
    (recv,) = after((recv,), res_top, res_bot, cot_top, cot_bot, first_there)
    recv = recv.reshape(-1, HALF)
    rest_there = over_ch(act_rest, 2)
    if split == 2:
        kva, kvb = recv, over_blk(recv[:, :LANES], 1)
    else:
        groups = [[n * split + m for m in range(split)] for n in range(4)]
        kv_all = lax.all_gather(
            recv[:, :LANES], "blk", axis=0, tiled=True, axis_index_groups=groups
        )
        kva, kvb = kv_all[: kv_all.shape[0] // 2], kv_all[kv_all.shape[0] // 2 :]
    dqo, dkva, dkvb, dctx = attend(live, recv, kva, kvb, ctx_kv, [])
    if split == 2:
        d_ctx = dctx + over_blk(dctx, 1)
        back = call(
            merge_kernel,
            [scal, dkva, over_blk(dkvb, 1), dqo],
            [((dqo.shape[0], HALF), BF)],
            deps=[rest_there],
        )[0]
    else:
        d_ctx = lax.psum(dctx, "blk", axis_index_groups=groups)
        d_kv = lax.psum_scatter(
            jnp.concatenate([dkva, dkvb.astype(F32)], axis=0),
            "blk",
            scatter_dimension=0,
            axis_index_groups=groups,
            tiled=True,
        )
        back = jnp.concatenate([d_kv.astype(BF), dqo], axis=1)
    grads = lax.all_to_all(back.reshape(blocks, pix // split, HALF), "blk", 0, 0)
    grads = grads.reshape(4, pix, HALF)

    features = context.shape[2] // split
    d_ctx = d_ctx[:ctx_len].astype(BF)
    ctx_part = call(
        functools.partial(context_grad_kernel, split=split),
        [scal, context, d_ctx] + [over_ch(d_ctx, mask) for mask in (1, 2, 3)],
        [((features, HALF), BF)],
        [((context.shape[2], HALF), F32)],
    )[0]
    ctx_all = lax.all_gather(ctx_part, "blk", axis=0)

    def low_grad(rows):
        return [((rows, HALF), F32), ((rows, HALF), BF), stat_shape]

    p3_own, p3_oth, st3 = call(
        functools.partial(qkv_back_kernel, **kind),
        [scal, grads, wp, res_own, res_oth, sums3, vec],
        low_grad(pix),
        [((pix, channels), F32)],
        deps=[ctx_part],
    )
    r3 = over_ch(p3_oth, 1)
    stats3 = to_image(st3)
    proj_own, proj_oth, wp_keep, wp_mine, wp_send = call(
        out_kernel,
        [scal, grads, wp, act3, cot_all],
        [
            ((pix, HALF), F32),
            ((pix, HALF), BF),
            ((4 * channels, LANES), BF),
            ((2 * channels, LANES), F32),
            ((2 * channels, LANES), BF),
        ],
        [((pix, channels), F32), ((2, 4 * channels, LANES), F32)],
    )
    wp_half = (wp_mine + over_blk(wp_send, 1).astype(F32)).astype(BF)
    wp_there = over_ch(wp_half, 2)
    first3 = (p3_own[:edge] + r3[:edge].astype(F32)).astype(BF)
    last3 = (p3_own[pix - edge :] + r3[pix - edge :].astype(F32)).astype(BF)
    d_top3, d_bot3 = halo(first3, last3)
    d_resid, ext2, away2 = call(
        functools.partial(norm3_back_kernel, **kind),
        [
            scal, p3_own, r3, d_top3, d_bot3, res_own, res_top, res_bot, cot_own, cot_top, cot_bot,
            sums3, stats3, vec,
        ],
        [((pix, HALF), F32), ((ext + 2 * COLS, HALF), BF), ((ext, LANES), BF)],
        deps=[proj_own],
    )
    there2 = over_ch(away2, 2)
    p2_own, p2_oth, st2 = call(
        functools.partial(conv_back_kernel, which=1, **kind),
        [scal, ext2, w2, hid_own, hid_oth, sums2, vec],
        low_grad(ext),
        [((ext, channels), F32)],
        time=8.0,
    )
    r2 = over_ch(p2_oth, 1)
    stats2 = to_image(st2)
    conv_rows, both_rows = 9 * channels // blocks, 13 * channels // blocks
    part2 = call(
        weight_grad_two_kernel,
        [scal, act_rest, rest_there, ext2, there2],
        [((blocks, conv_rows, LANES), BF)],
        [((2, pix, 9 * LANES), BF), ((9 * channels, LANES), F32)],
        deps=[r2],
    )[0]
    ext1, away1 = call(
        functools.partial(norm2_back_kernel, **kind),
        [scal, p2_own, r2, hid_own, sums2, stats2, vec],
        [((ext, HALF), BF), ((ext, LANES), BF)],
        deps=[part2],
    )
    parts2 = lax.all_to_all(part2, "blk", 0, 0)
    there1 = over_ch(away1, 2)
    p1_own, p1_oth, st1 = call(
        functools.partial(conv_back_kernel, which=0, **kind),
        [scal, ext1, w1, x_own, x_oth, sums1, vec],
        low_grad(pix),
        [((pix, channels), F32)],
        time=8.0,
    )
    r1 = over_ch(p1_oth, 1)
    stats1 = to_image(st1)
    half_shape = (4, 13 * channels // 8, LANES)
    keep1, send1 = call(
        weight_grad_one_kernel,
        [scal, act_first, act_rest, first_there, rest_there, ext1, there1, wp_keep, wp_there],
        [(half_shape, F32), (half_shape, BF)],
        [
            ((2, pix, 9 * LANES), BF),
            ((9 * channels, LANES), F32),
            ((4 * channels, LANES), F32),
        ],
        deps=[p1_own],
    )
    if blocks == 8:
        own1, *sends = call(
            scatter_kernel,
            [scal, keep1, over_blk(send1, 1)],
            [((both_rows, LANES), F32)] + [((both_rows, LANES), BF)] * 3,
            deps=[parts2],
        )
    else:
        own1 = keep1
    in_keep, in_send = call(
        functools.partial(last_kernel, **kind),
        [scal, p1_own, r1, x_own, sums1, stats1, vec, d_resid],
        [((pix, width), F32), ((pix, width), BF)],
        [((pix, HALF), F32)],
        deps=[own1],
    )
    if blocks == 8:
        total = call(
            total_kernel,
            [scal, own1, parts2] + [over_blk(v, 2 * n + 2) for n, v in enumerate(sends)],
            [((both_rows + conv_rows, LANES), BF)],
        )[0]
        grad1, grad2, qkv_grad, out_grad = call(
            place_kernel,
            [scal] + plane(total),
            [((9 * channels, LANES), F32)] * 2
            + [((3 * channels, LANES), F32), ((LANES, channels), F32)],
        )
    else:
        total = in_send
        flip = lambda c: jnp.where(b % 2 == 0, *((keep1.astype(BF), send1)[:: 1 - 2 * c]))
        grad1 = lax.psum(jnp.concatenate([flip(0), flip(1)], axis=0), "blk").astype(F32)
        cut = 9 * channels // 8
        wp_grad = grad1[:, cut:].reshape(-1, LANES)
        grad1, grad2 = grad1[:, :cut], lax.psum(part2, "blk").astype(F32)
        qkv_grad, out_grad = wp_grad[: 3 * channels], wp_grad[3 * channels :]
        out_grad = jnp.concatenate(list(out_grad.reshape(-1, LANES, LANES)), axis=1)

    (proj_late,) = after((proj_oth,), own1)
    out_own = (res_f + proj_own + over_ch(proj_late, 1).astype(F32)).astype(BF)
    out_keep, out_send = by_image(out_own[:, :LANES], out_own[:, LANES:])
    out_recv, in_recv = after((over_ch(out_send, 2), over_ch(in_send, 2)), grad1)
    block_output = jnp.stack(by_image(out_keep, out_recv)).reshape(block_input.shape)
    input_grad = jnp.stack(by_image(in_keep, in_recv.astype(F32))).reshape(block_input.shape)
    qkv_grad = jnp.transpose(qkv_grad.reshape(3, channels, LANES), (1, 0, 2))

    def both_images(*stats):
        totals = jnp.concatenate([jnp.sum(st[:, :2], axis=0) for st in stats])
        mine, theirs = by_image(totals[:, :LANES], totals[:, LANES:])
        return jnp.stack(by_image(mine, over_ch(theirs, 2)))

    totals = both_images(*after((stats1, stats2, stats3), total))
    ab1, ab2, ab3 = totals[:, 0:2], totals[:, 2:4], totals[:, 4:6]
    grow = 1.0 + scale_shift[:, 0]
    d_shift = ab2[:, 0]
    d_scale = norm2_gain * ab2[:, 1] + norm2_bias * ab2[:, 0]
    d_scale_shift = jnp.stack((d_scale, d_shift), axis=1)
    emb_f = jnp.repeat(emb_act.astype(F32), 2, axis=1)
    odd = (jnp.arange(emb_f.shape[1]) % 2)[None]
    emb_rows = jnp.concatenate([emb_f * (1 - odd), emb_f * odd], axis=0)
    embed_weight_grad = lax.dot_general(
        emb_rows,
        jnp.concatenate([d_scale, d_shift], axis=0),
        (((0,), (0,)), ((), ())),
        precision=lax.Precision.HIGHEST,
        preferred_element_type=F32,
    )

    (ctx_all,) = after((ctx_all,), total)
    if blocks == 8:
        ctx_grad = call(
            functools.partial(context_place_kernel, split=split),
            [scal, ctx_all],
            [((context.shape[2], 2 * channels), F32)],
        )[0]
    else:
        ctx_grad = ctx_all.reshape(2, 2, split, features, 2, 2, HEAD)
        ctx_grad = jnp.transpose(ctx_grad, (2, 3, 5, 0, 4, 1, 6)).astype(F32)

    return (
        block_output,
        input_grad,
        grad1.reshape(conv1_weight.shape),
        grad2.reshape(conv2_weight.shape),
        embed_weight_grad.reshape(embed_weight.shape),
        jnp.sum(d_scale_shift, axis=0),
        jnp.sum(ab1[:, 1], axis=0),
        jnp.sum(ab1[:, 0], axis=0),
        jnp.sum(grow * ab2[:, 1], axis=0),
        jnp.sum(grow * ab2[:, 0], axis=0),
        jnp.sum(ab3[:, 1], axis=0),
        jnp.sum(ab3[:, 0], axis=0),
        qkv_grad,
        out_grad,
        ctx_grad.astype(F32).reshape(ctx_weight.shape),
    )


def solution(mesh):
    return jax.shard_map(
        body,
        mesh=mesh,
        in_specs=(
            P(None, "blk", None, "ch"),
            P(None, "blk", None, "ch"),
            P(),
            P(),
            P(),
            P(None, None, "ch"),
            P(None, None, None, "ch"),
            P(None, None, None, "ch"),
            P(None, None, "ch"),
            P(None, "ch"),
            P("ch"),
            P("ch"),
            P("ch"),
            P("ch"),
            P("ch"),
            P("ch"),
            P(None, None, "ch"),
            P("ch", None),
            P("ch", None, None),
        ),
        out_specs=(
            P(None, "blk", None, "ch"),
            P(None, "blk", None, "ch"),
            P(None, None, None, "ch"),
            P(None, None, None, "ch"),
            P(None, None, "ch"),
            P(None, "ch"),
            P("ch"),
            P("ch"),
            P("ch"),
            P("ch"),
            P("ch"),
            P("ch"),
            P(None, None, "ch"),
            P("ch", None),
            P("ch", None, None),
        ),
        check_vma=False,
    )
```

```python
import functools
import math

import jax
import jax.numpy as jnp
from jax import lax
from jax.experimental import pallas as pl
from jax.experimental.pallas import tpu as pltpu
from jax.sharding import PartitionSpec as P

HEAD = 64
GROUPS = 32
CLIPTOK = 4
LANES = 128
HALF = 256
COLS = 64
VMEM_BYTES = 56 * 2**20
BF = jnp.bfloat16
F32 = jnp.float32

H, I, UP1, DOWN1, UP2, DOWN2, Z, B = range(8)


def dot(a, b):
    return jnp.dot(a, b, preferred_element_type=F32)


def dot_t(a, b):
    return lax.dot_general(a, b, (((1,), (1,)), ((), ())), preferred_element_type=F32)


def group_sum(vec, size):
    lane = lax.broadcasted_iota(jnp.int32, vec.shape, 1)
    step = 1
    while step < size:
        low = pltpu.roll(vec, step, 1)
        high = pltpu.roll(vec, LANES - step, 1)
        vec = vec + jnp.where((lane & step) != 0, low, high)
        step *= 2
    return vec


def shards(scal):
    h = scal[H]
    return (h, h + 2, 1 - h, 3 - h)


def lanes_of(shard):
    return pl.ds(pl.multiple_of(shard * LANES, LANES), LANES)


def part_of(quarter):
    return slice((quarter % 2) * LANES, (quarter % 2 + 1) * LANES)


def norm_stats(scal, sums, quarter, cells, size):
    wide = sums.shape[2] == HALF
    kinds = 2 if wide else 4
    shard = shards(scal)[quarter]
    total = None
    for source in range(sums.shape[0] // kinds):
        row = source * kinds + (shard % 2 if wide else shard)
        piece = sums[pl.ds(row, 1)][0]
        total = piece if total is None else total + piece
    if wide:
        total = total[:, part_of(quarter)]
    total = group_sum(total, size)
    mean = total[0:1] / cells
    inv = lax.rsqrt(total[1:2] / cells - mean * mean + 1e-05)
    return mean, inv


def affine_of(scal, vec, quarter, which, mean, inv):
    row = vec[pl.ds(shards(scal)[quarter], 1)][0]
    gain = row[2 * which + 2 : 2 * which + 3]
    bias = row[2 * which + 3 : 2 * which + 4]
    if which == 1:
        first = scal[I] == 0
        grow = 1.0 + jnp.where(first, row[8:9], row[10:11])
        gain, bias = gain * grow, bias * grow + jnp.where(first, row[9:10], row[11:12])
    slope = inv * gain
    return gain, slope, bias - mean * slope


def column_sums(first, second):
    rows = jnp.concatenate(
        [jnp.sum(first, axis=0, keepdims=True), jnp.sum(second, axis=0, keepdims=True)], axis=0
    )
    return jnp.concatenate([rows, jnp.zeros((6, rows.shape[1]), F32)], axis=0)


def shift_columns(total, left, right):
    col = lax.broadcasted_iota(jnp.int32, total.shape, 0) % COLS
    rows = total.shape[0]
    total = total + jnp.where(col > 0, pltpu.roll(left, 1, 0), 0.0)
    return total + jnp.where(col < COLS - 1, pltpu.roll(right, rows - 1, 0), 0.0)


def silu_slope(field):
    sigma = jax.nn.sigmoid(field)
    return sigma * (1.0 + field * (1.0 - sigma))


def masked_rows(scal, value, flag):
    return jnp.where(scal[flag] > 0, value, 0.0)


def input_sums_kernel(scal, field, vec, out, *, blocks):
    for image in range(2):
        value = field[image].astype(F32)
        sums = column_sums(value, value * value)[:2]
        sums = jnp.concatenate([sums, vec[2:]], axis=0)
        for target in range(blocks):
            out[4 * target + 2 * image] = sums
            out[4 * target + 2 * image + 1] = sums


def image_split_kernel(scal, field, mine, theirs):
    mine[...] = field[pl.ds(scal[I], 1)][0]
    theirs[...] = field[pl.ds(1 - scal[I], 1)][0]


def spread(out, sums):
    for target in range(out.shape[0]):
        out[target] = sums


def conv1_kernel(scal, own, oth, top, bot, sums, weight, out, out_sums, act_out, vec, act_scr, *, cells, size):
    pix = own.shape[0]
    vec[...] = sums[0:4]
    rows = pix + 2 * COLS
    for quarter in range(4):
        shard = shards(scal)[quarter]
        mean, inv = norm_stats(scal, sums, quarter, cells, size)
        gain, slope, offset = affine_of(scal, vec, quarter, 0, mean, inv)
        lanes = slice(quarter * LANES, (quarter + 1) * LANES)

        def active(field):
            pre = field.astype(F32) * slope + offset
            return pre * jax.nn.sigmoid(pre)

        half = own if quarter < 2 else oth
        main = active(half[:, part_of(quarter)]).astype(BF)
        above, below = active(top[:, lanes]), active(bot[:, lanes])
        act_scr[2 * COLS : 2 * COLS + pix, lanes_of(shard)] = main
        act_out[:, lanes_of(shard)] = main
        act_scr[0:COLS, lanes_of(shard)] = masked_rows(scal, above[:COLS], UP2).astype(BF)
        act_scr[COLS : 2 * COLS, lanes_of(shard)] = masked_rows(scal, above[COLS:], UP1).astype(BF)
        end = 2 * COLS + pix
        act_scr[end : end + COLS, lanes_of(shard)] = masked_rows(scal, below[:COLS], DOWN1).astype(BF)
        act_scr[end + COLS :, lanes_of(shard)] = masked_rows(scal, below[COLS:], DOWN2).astype(BF)
    result = convolve(act_scr, weight, rows)
    out[...] = result.astype(BF)
    inner = result[COLS : COLS + pix]
    spread(out_sums, column_sums(inner, inner * inner))


def convolve(act_scr, weight, rows):
    channels = act_scr.shape[1]
    parts = []
    for kx in range(3):
        acc = None
        for ky in range(3):
            tap = (ky * 3 + kx) * channels
            term = dot(act_scr[ky * COLS : ky * COLS + rows, :], weight[tap : tap + channels, :])
            acc = term if acc is None else acc + term
        parts.append(acc)
    return shift_columns(parts[1], parts[0], parts[2])


def conv2_kernel(scal, own, oth, sums, vec, weight, base, act_below, out_f, out_low, out_sums, act_first, act_out, edges, act_scr, *, cells, size):
    pix = base.shape[0]
    cut = act_first.shape[0]
    act_first[...] = act_below[0:cut]
    act_out[0 : pix - cut, :] = act_below[cut:]
    for quarter in range(4):
        shard = shards(scal)[quarter]
        mean, inv = norm_stats(scal, sums, quarter, cells, size)
        gain, slope, offset = affine_of(scal, vec, quarter, 1, mean, inv)
        half = own if quarter < 2 else oth
        pre = half[:, part_of(quarter)].astype(F32) * slope + offset
        act = pre * jax.nn.sigmoid(pre)
        main = act[COLS : COLS + pix].astype(BF)
        act_scr[COLS : COLS + pix, lanes_of(shard)] = main
        act_out[pix - cut :, lanes_of(shard)] = main
        act_scr[0:COLS, lanes_of(shard)] = masked_rows(scal, act[:COLS], UP1).astype(BF)
        act_scr[COLS + pix :, lanes_of(shard)] = masked_rows(scal, act[COLS + pix :], DOWN1).astype(BF)
    result = convolve(act_scr, weight, pix) + base[...].astype(F32)
    out_f[...] = result
    low = result.astype(BF)
    out_low[...] = low
    if edges.shape[1] < pix:
        edges[0], edges[1] = low[: edges.shape[1]], low[pix - edges.shape[1] :]
    else:
        edges[0], edges[1] = low, low
    spread(out_sums, column_sums(result, result * result))


def qkv_kernel(scal, own, oth, sums, vec, cot_own, cot_oth, weight, out, act_out, cot_out, edges, *, cells, size):
    rows = edges.shape[1]
    edges[0], edges[1] = cot_own[0:rows], cot_own[cot_own.shape[0] - rows :]
    for quarter in range(4):
        shard = shards(scal)[quarter]
        mean, inv = norm_stats(scal, sums, quarter, cells, size)
        gain, slope, offset = affine_of(scal, vec, quarter, 2, mean, inv)
        half = own if quarter < 2 else oth
        cot = cot_own if quarter < 2 else cot_oth
        field = half[:, part_of(quarter)].astype(F32)
        act_out[:, lanes_of(shard)] = (field * slope + offset).astype(BF)
        cot_out[:, lanes_of(shard)] = cot[:, part_of(quarter)]
    for head in range(4):
        columns = weight[:, head * HALF : (head + 1) * HALF]
        fwd = dot(act_out[...], columns)
        back = dot(cot_out[...], columns[:, LANES:])
        out[head, :, :LANES] = fwd[:, :LANES].astype(BF)
        lane = lax.broadcasted_iota(jnp.int32, back.shape, 1)
        out[head, :, LANES:] = jnp.where(lane < HEAD, fwd[:, LANES:], back).astype(BF)


def below_stats(scal, total, own, oth, sums, vec, out_own, out_oth, out_stats, which, cells, size):
    rows = total.shape[0]
    pix = rows - 2 * COLS if which == 1 else rows
    inner = slice(COLS, COLS + pix) if which == 1 else slice(0, pix)
    for quarter in range(4):
        shard = shards(scal)[quarter]
        mean, inv = norm_stats(scal, sums, quarter, cells, size)
        gain, slope, offset = affine_of(scal, vec, quarter, which, mean, inv)
        half = own if quarter < 2 else oth
        part = part_of(quarter)
        if quarter < 2:
            out_own[:, part] = total[:, lanes_of(shard)]
        else:
            out_oth[:, part] = total[:, lanes_of(shard)].astype(BF)
        grad = total[inner, lanes_of(shard)]
        field = half[inner, part].astype(F32)
        if which < 2:
            grad = grad * silu_slope(field * slope + offset)
        result = column_sums(grad, grad * ((field - mean) * inv))
        slot = scal[H] if quarter < 2 else 1 - scal[H]
        for target in range(out_stats.shape[0] // 2):
            out_stats[pl.ds(2 * target + slot, 1), :, part] = result[None]


def qkv_back_kernel(scal, grads, weight, own, oth, sums, vec, out_own, out_oth, out_stats, tot_scr, *, cells, size):
    total = None
    for head in range(4):
        columns = weight[:, head * HALF : (head + 1) * HALF]
        grad = grads[head]
        lane = lax.broadcasted_iota(jnp.int32, grad.shape, 1)
        term = dot_t(jnp.where(lane < 3 * HEAD, grad, jnp.zeros_like(grad)), columns)
        total = term if total is None else total + term
    tot_scr[...] = total
    below_stats(scal, tot_scr, own, oth, sums, vec, out_own, out_oth, out_stats, 2, cells, size)


def out_kernel(scal, grads, weight, act, cot, proj_own, proj_oth, wgrad, tot_scr):
    channels = act.shape[1]
    act_t = act[...].astype(F32).T.astype(BF)
    total = None
    for pair in range(2):
        slot = jnp.where(scal[I] == pair, 0, 1)
        parts, outs = [], []
        for head in (2 * pair, 2 * pair + 1):
            columns = weight[:, head * HALF + LANES : (head + 1) * HALF]
            grad = grads[head]
            low = grad[:, LANES:]
            lane = lax.broadcasted_iota(jnp.int32, low.shape, 1)
            term = dot_t(jnp.where(lane < HEAD, jnp.zeros_like(low), low), columns)
            total = term if total is None else total + term
            parts.append(dot(act_t, grad))
            outs.append(dot(low.astype(F32).T[HEAD:].astype(BF), cot[...]))
        first, second = parts
        pieces = [
            jnp.concatenate([first[:, LANES : LANES + HEAD], second[:, LANES : LANES + HEAD]], axis=1)
            * 0.125,
            jnp.concatenate([first[:, :HEAD], second[:, :HEAD]], axis=1),
            jnp.concatenate([first[:, HEAD:LANES], second[:, HEAD:LANES]], axis=1),
        ]
        both = jnp.concatenate(outs, axis=0)
        pieces += [both[:, n * LANES : (n + 1) * LANES] for n in range(channels // LANES)]
        wgrad[pl.ds(slot, 1)] = jnp.concatenate(pieces, axis=0).astype(BF)[None]
    tot_scr[...] = total
    for quarter, shard in enumerate(shards(scal)):
        if quarter < 2:
            proj_own[:, part_of(quarter)] = tot_scr[:, lanes_of(shard)]
        else:
            proj_oth[:, part_of(quarter)] = tot_scr[:, lanes_of(shard)].astype(BF)


def total_stats(stats):
    total = stats[0]
    for source in range(1, stats.shape[0]):
        total = total + stats[source]
    return total


def norm_back(scal, quarter, sums, stats, vec, which, cells, size):
    mean, inv = norm_stats(scal, sums, quarter, cells, size)
    gain, slope, offset = affine_of(scal, vec, quarter, which, mean, inv)
    means = group_sum(total_stats(stats)[:, part_of(quarter)] * gain, size) / cells

    def back(grad, field):
        field = field.astype(F32)
        hat = (field - mean) * inv
        if which < 2:
            grad = grad * silu_slope(field * slope + offset)
        return (grad * gain - means[0:1] - hat * means[1:2]) * inv

    return back


def norm3_back_kernel(
    scal, part, recv, dtop, dbot, field, ftop, fbot, cot, ctop, cbot, sums, stats, vec, out_f, ext, away, *, cells, size
):
    pix = part.shape[0]
    end = 2 * COLS + pix
    for quarter in range(2):
        lanes = part_of(quarter)
        back = norm_back(scal, quarter, sums, stats, vec, 2, cells, size)
        main = back(part[:, lanes] + recv[:, lanes].astype(F32), field[:, lanes])
        main = main + cot[:, lanes].astype(F32)
        out_f[:, lanes] = main
        ext[2 * COLS : end, lanes] = main.astype(BF)
        head = back(dtop[:, lanes].astype(F32), ftop[:, lanes]) + ctop[:, lanes].astype(F32)
        tail = back(dbot[:, lanes].astype(F32), fbot[:, lanes]) + cbot[:, lanes].astype(F32)
        ext[0:COLS, lanes] = masked_rows(scal, head[:COLS], UP2).astype(BF)
        ext[COLS : 2 * COLS, lanes] = masked_rows(scal, head[COLS:], UP1).astype(BF)
        ext[end : end + COLS, lanes] = masked_rows(scal, tail[:COLS], DOWN1).astype(BF)
        ext[end + COLS :, lanes] = masked_rows(scal, tail[COLS:], DOWN2).astype(BF)
    away[...] = ext[COLS : end + COLS, lanes_of(1 - scal[I])]


def norm2_back_kernel(scal, part, recv, field, sums, stats, vec, ext, away, *, cells, size):
    rows = part.shape[0]
    for quarter in range(2):
        lanes = part_of(quarter)
        back = norm_back(scal, quarter, sums, stats, vec, 1, cells, size)
        main = back(part[:, lanes] + recv[:, lanes].astype(F32), field[:, lanes])
        ext[0:COLS, lanes] = masked_rows(scal, main[:COLS], UP1).astype(BF)
        ext[COLS : rows - COLS, lanes] = main[COLS : rows - COLS].astype(BF)
        ext[rows - COLS :, lanes] = masked_rows(scal, main[rows - COLS :], DOWN1).astype(BF)
    away[...] = ext[:, lanes_of(1 - scal[I])]


def conv_back_kernel(scal, ext, weight, own, oth, sums, vec, out_own, out_oth, out_stats, tot_scr, *, which, cells, size):
    rows, channels = tot_scr.shape
    parts = []
    for kx in range(3):
        acc = None
        for ky in range(3):
            tap = (ky * 3 + kx) * channels
            start = (2 - ky) * COLS
            term = dot_t(ext[start : start + rows, :], weight[tap : tap + channels, :])
            acc = term if acc is None else acc + term
        parts.append(acc)
    tot_scr[...] = shift_columns(parts[1], parts[2], parts[0])
    below_stats(scal, tot_scr, own, oth, sums, vec, out_own, out_oth, out_stats, which, cells, size)


def last_kernel(scal, part, recv, field, sums, stats, vec, resid_grad, keep, send, tot_scr, *, cells, size):
    i = scal[I]
    for quarter in range(2):
        lanes = part_of(quarter)
        back = norm_back(scal, quarter, sums, stats, vec, 0, cells, size)
        main = back(part[:, lanes] + recv[:, lanes].astype(F32), field[:, lanes])
        tot_scr[:, lanes] = main + resid_grad[:, lanes]
    keep[...] = tot_scr[:, lanes_of(i)]
    send[...] = tot_scr[:, lanes_of(1 - i)].astype(BF)


def weight_grads(scal, act_one, act_two, ext_one, ext_two, rhs_scr, out_scr):
    pix, channels = act_one.shape
    rows = ext_two.shape[0]
    first = (ext_one.shape[0] - rows) // 2
    own = ext_one[first : first + rows, lanes_of(scal[I])]
    products = []
    for act, wide in ((act_one, own), (act_two, ext_two[...])):
        wide = wide.astype(F32)
        col = lax.broadcasted_iota(jnp.int32, wide.shape, 0) % COLS
        for kx in range(3):
            if kx == 0:
                moved = jnp.where(col < COLS - 1, pltpu.roll(wide, rows - 1, 0), 0.0)
            elif kx == 2:
                moved = jnp.where(col > 0, pltpu.roll(wide, 1, 0), 0.0)
            else:
                moved = wide
            moved = moved.astype(BF)
            for ky in range(3):
                start = (2 - ky) * COLS
                tap = ky * 3 + kx
                lanes = slice(tap * LANES, (tap + 1) * LANES)
                rhs_scr[len(products), :, lanes] = moved[start : start + pix]
        products.append(act.astype(F32).T.astype(BF))
    for tap in range(9):
        lanes = slice(tap * LANES, (tap + 1) * LANES)
        total = dot(products[0], rhs_scr[0, :, lanes]) + dot(products[1], rhs_scr[1, :, lanes])
        out_scr[tap * channels : (tap + 1) * channels, :] = total


def weight_grad_one_kernel(
    scal, up, low, up_there, low_there, ext_one, ext_two, keep, send, rhs_scr, out_scr
):
    cut = up.shape[0]
    mine = jnp.concatenate([up[...], low[0:cut]], axis=0)
    theirs = jnp.concatenate([up_there[...], low_there[0:cut]], axis=0)
    weight_grads(scal, mine, theirs, ext_one, ext_two, rhs_scr, out_scr)
    core = scal[B] % 2
    count = out_scr.shape[0] // 2
    at = lambda n: pl.ds(pl.multiple_of(n * count, count), count)
    keep[...] = out_scr[at(core), :].reshape(keep.shape)
    send[...] = out_scr[at(1 - core), :].astype(BF).reshape(send.shape)


def weight_grad_two_kernel(scal, act, act_there, ext_one, ext_two, wp, out, rhs_scr, out_scr):
    cut = act.shape[0] // 3
    weight_grads(scal, act[cut:], act_there[cut:], ext_one, ext_two, rhs_scr, out_scr)
    blocks = out.shape[0]
    rows = out_scr.shape[0] // blocks
    extra = wp.shape[1] // blocks
    out[:, :rows] = out_scr[...].astype(BF).reshape(blocks, rows, LANES)
    for part in range(2):
        first = rows + part * extra
        out[:, first : first + extra] = wp[part].reshape(blocks, extra, LANES)


def other_sum_kernel(scal, parts, out):
    first = parts.shape[1] - out.shape[0]
    total = parts[0, first:].astype(F32)
    for source in range(1, parts.shape[0]):
        total = total + parts[source, first:].astype(F32)
    out[...] = total.astype(BF)


def total_kernel(scal, own, parts, other, one, two, three, out):
    count = own.shape[0]
    extra = other.shape[0]
    first = own[...] + one[...].astype(F32) + two[...].astype(F32) + three[...].astype(F32)
    out[0:count] = first.astype(BF)
    second = parts[0, : count + extra].astype(F32)
    for source in range(1, parts.shape[0]):
        second = second + parts[source, : count + extra].astype(F32)
    out[count : 2 * count] = second[:count].astype(BF)
    out[2 * count :] = (second[count:] + other[...].astype(F32)).astype(BF)


def scatter_kernel(scal, keep, recv, own, *sends):
    chip = scal[B] // 2
    for mask in range(4):
        chunk = pl.ds(chip ^ mask, 1)
        value = (keep[chunk] + recv[chunk].astype(F32))[0]
        if mask == 0:
            own[...] = value
        else:
            sends[mask - 1][...] = value.astype(BF)


def place_kernel(scal, *refs):
    pieces, (one, two, qkv, out) = refs[:8], refs[8:]
    core, chip = scal[B] % 2, scal[B] // 2
    count = one.shape[0] // 8
    rows = qkv.shape[0] // 6
    for n, piece in enumerate(pieces):
        half = core if n < 4 else 1 - core
        source = chip ^ (n % 4)
        at = lambda slot, size: pl.ds(pl.multiple_of(slot * size, size), size)
        slot = 2 * source + half
        one[at(4 * half + source, count), :] = piece[:count].astype(F32)
        two[at(slot, count), :] = piece[count : 2 * count].astype(F32)
        extra = piece[2 * count :].astype(F32)

        @pl.when(slot < 6)
        def _(extra=extra, slot=slot):
            qkv[at(slot, rows), :] = extra

        @pl.when(slot >= 6)
        def _(extra=extra, slot=slot):
            for m in range(rows // LANES):
                column = (slot - 6) * (rows // LANES) + m
                out[:, lanes_of(column)] = extra[m * LANES : (m + 1) * LANES]


def channel_sums_kernel(scal, one, two, three, mine, theirs):
    rows = jnp.concatenate([total_stats(stats)[0:2] for stats in (one, two, three)], axis=0)
    rows = jnp.concatenate([rows, jnp.zeros((2, rows.shape[1]), F32)], axis=0)
    first, second = rows[:, :LANES], rows[:, LANES:]
    here = scal[I] == 0
    mine[...] = jnp.where(here, first, second)
    theirs[...] = jnp.where(here, second, first)


def channel_grads_kernel(scal, mine, recv, vec, emb, bias_grad, *outs):
    here = scal[I] == 0
    images = (
        jnp.where(here, mine[...], recv[...]),
        jnp.where(here, recv[...], mine[...]),
    )
    gain, bias = vec[4:5], vec[5:6]
    scales = [gain * rows[3:4] + bias * rows[2:3] for rows in images]
    shifts = [rows[2:3] for rows in images]
    grown = [1.0 + vec[8:9], 1.0 + vec[10:11]]
    both = images[0] + images[1]
    bias_grad[0:1] = scales[0] + scales[1]
    bias_grad[1:2] = shifts[0] + shifts[1]
    values = [
        both[1:2],
        both[0:1],
        grown[0] * images[0][3:4] + grown[1] * images[1][3:4],
        grown[0] * images[0][2:3] + grown[1] * images[1][2:3],
        both[5:6],
        both[4:5],
    ]
    for out, value in zip(outs, values):
        out[...] = value
    weight_grad = outs[6]
    turned = emb[...].T
    total = None
    for n, row in enumerate(scales + shifts):
        term = turned[:, n : n + 1] * row
        total = term if total is None else total + term
    weight_grad[...] = total


def out_add_kernel(scal, resid, part, recv, keep, send):
    total = resid[...] + part[...] + recv[...].astype(F32)
    first, second = total[:, :LANES].astype(BF), total[:, LANES:].astype(BF)
    here = scal[I] == 0
    keep[...] = jnp.where(here, first, second)
    send[...] = jnp.where(here, second, first)


def by_images_kernel(scal, out_keep, out_recv, in_keep, in_recv, block_output, input_grad):
    i = scal[I]
    for keep, recv, out in ((out_keep, out_recv, block_output), (in_keep, in_recv, input_grad)):
        out[pl.ds(i, 1)] = keep[...][None]
        out[pl.ds(1 - i, 1)] = recv[...].astype(out.dtype)[None]


def merge_kernel(scal, mine, recv, rest, out):
    out[:, :LANES] = (mine[...] + recv[...].astype(F32)).astype(BF)
    out[:, LANES:] = rest[...]


def context_grad_kernel(scal, context, d_zero, d_one, d_two, d_three, out, tot_scr, *, split):
    rows = out.shape[0]
    turned = [context[image].astype(F32).T.astype(BF) for image in range(2)]
    pieces = (d_zero, d_one, d_two, d_three)
    for h in range(2):
        total = None
        for image in range(2):
            slot = (2 * image + h) ^ scal[Z]
            chosen = pieces[0][...]
            for n in range(1, 4):
                chosen = jnp.where(slot == n, pieces[n][...], chosen)
            term = dot(turned[image], chosen)
            total = term if total is None else total + term
        tot_scr[:, h * LANES : (h + 1) * LANES] = total
    part = scal[B] % split
    out[...] = tot_scr[pl.ds(pl.multiple_of(part * rows, rows), rows), :].astype(BF)


def context_place_kernel(scal, pieces, out, *, split):
    rows = pieces.shape[1]
    for part in range(split):
        for t in range(2):
            first, second = ((2 * t + n) * split + part for n in range(2))
            for h in range(2):
                for kind in range(2):
                    start = h * LANES + kind * HEAD
                    value = jnp.concatenate(
                        [pieces[n, :, start : start + HEAD] for n in (first, second)], axis=1
                    )
                    column = (h + 2 * t) * LANES
                    out[part * rows : (part + 1) * rows, kind, column : column + LANES] = (
                        value.astype(F32)
                    )


def join_kernel(scal, own, *refs):
    pieces, out = refs[:8], refs[8]
    i, b = scal[I], scal[B]
    out[:, lanes_of(i)] = own[...]
    size = own.shape[0] // 8
    for core in range(2):
        for mask in range(4):
            source = b ^ (2 * mask + core)
            target = pl.ds(pl.multiple_of(source * size, size), size)
            out[target, lanes_of(1 - i)] = pieces[4 * core + mask][...]


def place_weight_kernel(scal, own, chunks, out, *, start, width):
    i = scal[I]
    rows = own.shape[0] // width
    size = own.shape[0] // chunks.shape[0]
    for n in range(width):
        out[:, lanes_of(i * width + n)] = own[n * rows : (n + 1) * rows]
    for source in range(chunks.shape[0]):
        n, first = divmod(source * size, rows)
        out[first : first + size, lanes_of((1 - i) * width + n)] = chunks[
            source, start : start + size
        ]


def attend_kernel(
    live, qd, kva, kvb, ctx, dqo, dkva, dkvb, dctx,
    kv_scr, kt_scr, vt_scr, s_scr, e_scr, acc_scr, *, chunk, unroll,
):
    step = pl.program_id(0)
    half_a, half_b, extra = kva.shape[0], kvb.shape[0], ctx.shape[0]
    keys = half_a + half_b
    total = keys + extra
    block = qd.shape[0]

    @pl.when(step == 0)
    def _():
        kv_scr[0:half_a, :] = kva[...]
        kv_scr[half_a:keys, :] = kvb[...]
        kv_scr[keys:total, :] = ctx[...]
        acc_scr[...] = jnp.zeros_like(acc_scr)

        def turn(rows):
            flipped = kv_scr[rows, :].astype(F32).T.astype(BF)
            kt_scr[:, rows] = flipped[:HEAD]
            vt_scr[0:HEAD, rows] = flipped[HEAD:]

        def turn_step(n, carry):
            turn(pl.ds(pl.multiple_of(n * 256, 256), 256))
            return carry

        lax.fori_loop(0, keys // 256, turn_step, 0)
        turn(slice(keys, total))
        vt_scr[HEAD:, :] = jnp.ones((16, total), BF)

    both = qd[...].astype(F32).T
    q_t = both[:HEAD].astype(BF)
    zero = jnp.zeros((HEAD, block), BF)
    q_side = jnp.concatenate([q_t, zero], axis=0)

    def score(rows, top, masked):
        s = dot(kv_scr[rows, :], q_side)
        if masked:
            index = lax.broadcasted_iota(jnp.int32, s.shape, 0)
            s = jnp.where(index < live[0], s, -1e30)
        s_scr[rows, :] = s
        return jnp.maximum(top, jnp.max(s.reshape(-1, 8, block), axis=0))

    def span(n):
        return pl.ds(pl.multiple_of(n * chunk, chunk), chunk)

    def over_keys(func, carry):
        return lax.fori_loop(
            0, keys // chunk, lambda n, c: func(span(n), c), carry, unroll=unroll
        )

    tail = pl.ds(keys, extra)
    top = score(tail, jnp.full((8, block), -1e30, F32), True)
    top = over_keys(lambda rows, c: score(rows, c, False), top)
    top = jnp.max(top, axis=0, keepdims=True)

    def weigh(rows, acc):
        e = jnp.exp(s_scr[rows, :] - top).astype(BF)
        e_scr[rows, :] = e
        return acc + dot(vt_scr[:, rows], e)

    out_t = weigh(tail, jnp.zeros((HEAD + 16, block), F32))
    out_t = over_keys(weigh, out_t)
    inv = 1.0 / out_t[HEAD : HEAD + 1]
    out_t = out_t[:HEAD] * inv
    d_t = both[HEAD:]
    delta = jnp.sum(d_t * out_t, axis=0, keepdims=True) * inv
    d_t = d_t * inv
    d_side = jnp.concatenate([zero, d_t.astype(BF)], axis=0)
    zero_q = jnp.zeros((block, HEAD), BF)
    rows_q = jnp.concatenate([qd[:, :HEAD], zero_q], axis=1)
    rows_d = jnp.concatenate([zero_q, d_t.T.astype(BF)], axis=1)
    right = jnp.concatenate([rows_q, rows_d], axis=0)

    def back(rows, acc):
        d_prob = dot(kv_scr[rows, :], d_side)
        e = e_scr[rows, :]
        d_score = (e.astype(F32) * (d_prob - delta)).astype(BF)
        acc_scr[rows, :] += dot(jnp.concatenate([d_score, e], axis=1), right)
        return acc + dot(kt_scr[:, rows], d_score)

    dq_t = back(tail, jnp.zeros((HEAD, block), F32))
    dq_t = over_keys(back, dq_t)
    dqo[...] = jnp.concatenate([dq_t, out_t], axis=0).T.astype(BF)

    @pl.when(step == pl.num_programs(0) - 1)
    def _():
        dkva[...] = acc_scr[0:half_a, :]
        dkvb[...] = acc_scr[half_a:keys, :].astype(BF)
        dctx[...] = acc_scr[keys:total, :]


def attend(live, recv, kva, kvb, ctx, deps):
    queries = recv.shape[0]
    block = min(512, queries)
    half_a, half_b, extra = recv.shape[0] if kva is recv else kva.shape[0], kvb.shape[0], ctx.shape[0]
    total = half_a + half_b + extra
    whole = lambda shape: pl.BlockSpec(shape, lambda n: (0, 0))
    kernel = functools.partial(attend_kernel, chunk=512, unroll=4)

    def inner(*refs):
        kernel(*refs[:5], *refs[5 + len(deps) :])

    return pl.pallas_call(
        inner,
        grid=(queries // block,),
        in_specs=[
            pl.BlockSpec(memory_space=pltpu.SMEM),
            pl.BlockSpec((block, LANES), lambda n: (n, 1)),
            whole((half_a, LANES)),
            whole((half_b, LANES)),
            whole((extra, LANES)),
        ]
        + [pl.BlockSpec(memory_space=pl.ANY)] * len(deps),
        out_specs=[
            pl.BlockSpec((block, LANES), lambda n: (n, 0)),
            whole((half_a, LANES)),
            whole((half_b, LANES)),
            whole((extra, LANES)),
        ],
        out_shape=[
            jax.ShapeDtypeStruct((queries, LANES), BF),
            jax.ShapeDtypeStruct((half_a, LANES), F32),
            jax.ShapeDtypeStruct((half_b, LANES), BF),
            jax.ShapeDtypeStruct((extra, LANES), F32),
        ],
        scratch_shapes=[
            pltpu.VMEM((total, LANES), BF),
            pltpu.VMEM((HEAD, total), BF),
            pltpu.VMEM((HEAD + 16, total), BF),
            pltpu.VMEM((total, block), F32),
            pltpu.VMEM((total, block), BF),
            pltpu.VMEM((total, LANES), F32),
        ],
        compiler_params=pltpu.CompilerParams(vmem_limit_bytes=VMEM_BYTES),
        cost_estimate=pl.CostEstimate(
            flops=int(38 * 1.15e9), bytes_accessed=1, transcendentals=0
        ),
    )(live, recv, kva, kvb, ctx, *deps)


def call(kernel, args, outs, scratch=(), deps=(), time=0.0):
    in_vmem = pl.BlockSpec(memory_space=pltpu.VMEM)
    in_smem = pl.BlockSpec(memory_space=pltpu.SMEM)
    anywhere = pl.BlockSpec(memory_space=pl.ANY)
    count = len(args)

    def inner(*refs):
        kernel(*refs[:count], *refs[count + len(deps) :])

    return pl.pallas_call(
        inner,
        in_specs=[in_smem] + [in_vmem] * (count - 1) + [anywhere] * len(deps),
        out_specs=[in_vmem] * len(outs),
        out_shape=[jax.ShapeDtypeStruct(s, d) for s, d in outs],
        scratch_shapes=[pltpu.VMEM(s, d) for s, d in scratch],
        compiler_params=pltpu.CompilerParams(vmem_limit_bytes=VMEM_BYTES),
        cost_estimate=pl.CostEstimate(
            flops=1 + int(time * 1.15e9), bytes_accessed=1, transcendentals=0
        ),
    )(*args, *deps)


def after(values, *deps):
    anywhere = pl.BlockSpec(memory_space=pl.ANY)
    count = len(values)

    def inner(*refs):
        pass

    return pl.pallas_call(
        inner,
        in_specs=[anywhere] * (count + len(deps)),
        out_specs=[anywhere] * count,
        out_shape=[jax.ShapeDtypeStruct(v.shape, v.dtype) for v in values],
        input_output_aliases={n: n for n in range(count)},
        cost_estimate=pl.CostEstimate(flops=1, bytes_accessed=1, transcendentals=0),
    )(*values, *deps)


def embed_features(timesteps, image_embed):
    half_width = image_embed.shape[1] // 2
    freqs = jnp.exp(-math.log(10000.0) * jnp.arange(half_width, dtype=F32) / half_width)
    angles = timesteps.astype(F32)[:, None] * freqs[None, :]
    return jax.nn.silu(jnp.concatenate([jnp.cos(angles), jnp.sin(angles)], axis=1) + image_embed)


def body(
    block_input,
    cotangent,
    image_embed,
    timesteps,
    text_len,
    context,
    conv1_weight,
    conv2_weight,
    embed_weight,
    embed_bias,
    norm1_gain,
    norm1_bias,
    norm2_gain,
    norm2_bias,
    norm3_gain,
    norm3_bias,
    qkv_weight,
    out_weight,
    ctx_weight,
):
    images, row_count, col_count, width = block_input.shape
    channels = qkv_weight.shape[0]
    size = channels // GROUPS
    blocks = lax.axis_size("blk")
    pix = row_count * col_count
    cells = float(pix * blocks * size)
    split = blocks // 4
    ctx_len = context.shape[1]
    b = lax.axis_index("blk")
    z = lax.axis_index("ch")
    h, i = z % 2, z // 2
    row, rows_all = b * row_count, blocks * row_count
    inside = [row >= 1, row + row_count < rows_all, row >= 2, row + row_count + 1 < rows_all]
    scal = jnp.stack([h, i] + [flag.astype(jnp.int32) for flag in inside] + [z, b]).astype(jnp.int32)


    def over_ch(value, mask):
        return lax.ppermute(value, "ch", [(n, n ^ mask) for n in range(4)])

    def over_blk(value, mask):
        return lax.ppermute(value, "blk", [(n, n ^ mask) for n in range(blocks)])

    def ring(value, step):
        return lax.ppermute(value, "blk", [(n, (n + step) % blocks) for n in range(blocks)])

    def halo(first, last):
        if row_count >= 2:
            return ring(last, 1), ring(first, -1)
        return (
            jnp.concatenate([ring(last, 2), ring(last, 1)], axis=0),
            jnp.concatenate([ring(first, -1), ring(first, -2)], axis=0),
        )

    pairs = [[n * 4 + 2 * m + k for n in range(blocks) for k in range(2)] for m in range(2)]

    def to_image(value):
        return lax.all_to_all(value, ("blk", "ch"), 0, 0, axis_index_groups=pairs)

    def by_image(first, second):
        return jnp.where(i == 0, first, second), jnp.where(i == 0, second, first)

    def plane(value):
        mine = [value] + [over_blk(value, 2 * mask) for mask in (1, 2, 3)]
        return mine + [over_blk(piece, 1) for piece in mine]

    w1_own = conv1_weight.reshape(-1, width)
    w2_own = conv2_weight.reshape(-1, width)
    heads = lambda v: v.reshape(channels, 2, HEAD)
    wp_own = jnp.stack(
        [
            jnp.concatenate([heads(qkv_weight[:, 1]), heads(qkv_weight[:, 2])], axis=2),
            jnp.concatenate([heads(qkv_weight[:, 0] * 0.125), heads(out_weight.T)], axis=2),
        ],
        axis=0,
    )
    wp_own = jnp.transpose(wp_own, (2, 0, 1, 3)).reshape(-1, LANES)
    w1_rows, w2_rows, wp_rows = (w.shape[0] // blocks for w in (w1_own, w2_own, wp_own))
    chunk_of = lambda w: lax.dynamic_slice_in_dim(w, b * (w.shape[0] // blocks), w.shape[0] // blocks, 0)
    w1_slice = chunk_of(w1_own)

    emb_act = embed_features(timesteps, image_embed).astype(BF)
    scale_shift = (
        jnp.einsum("ie,esc->isc", emb_act, embed_weight, preferred_element_type=F32) + embed_bias
    )
    local_vec = jnp.concatenate(
        [
            jnp.zeros((2, width), F32),
            jnp.stack([norm1_gain, norm1_bias, norm2_gain, norm2_bias, norm3_gain, norm3_bias]),
            scale_shift.reshape(4, width),
            jnp.zeros((4, width), F32),
        ],
        axis=0,
    )
    x_mine, x_theirs = call(
        image_split_kernel,
        [scal, block_input.reshape(images, pix, width)],
        [((pix, width), BF)] * 2,
        deps=[w1_slice],
    )
    w1_chunk = over_ch(w1_slice, 2)
    x_two, x_one = over_ch(x_theirs, 2), over_ch(x_mine, 1)
    x_three = over_ch(x_two, 1)
    if blocks == 8:
        w1_pieces = plane(w1_chunk)
    else:
        w1_pieces = [lax.all_gather(w1_chunk, "blk", axis=0, tiled=True)]
    x_sums = call(
        functools.partial(input_sums_kernel, blocks=blocks),
        [scal, block_input.reshape(images, pix, width), local_vec],
        [((4 * blocks, 16, width), F32)],
        deps=[x_mine],
    )[0]
    sums1 = lax.all_to_all(x_sums, ("blk", "ch"), 0, 0)
    two_source = jnp.concatenate([chunk_of(w2_own), chunk_of(wp_own)], axis=0)
    (two_source,) = after((two_source,), x_two, x_one, x_sums)
    two_chunk = over_ch(two_source, 2)
    (two_chunk,) = after((two_chunk,), x_three, *w1_pieces[1:4])
    wide = dict(axis=1)
    x_own = jnp.concatenate(by_image(x_mine, x_two), **wide)
    x_oth = jnp.concatenate(by_image(x_one, x_three), **wide)
    edge = min(2 * COLS, pix)
    x_top, x_bot = halo(
        jnp.concatenate([x_own[:edge], x_oth[:edge]], **wide),
        jnp.concatenate([x_own[pix - edge :], x_oth[pix - edge :]], **wide),
    )
    if blocks == 8:
        w1 = call(join_kernel, [scal, w1_own] + w1_pieces, [((w1_own.shape[0], HALF), BF)])[0]
    else:
        w1_oth = w1_pieces[0]
        w1 = jnp.concatenate(by_image(w1_own, w1_oth), **wide)
    two = lax.all_gather(two_chunk, "blk", axis=0)
    w2 = call(
        functools.partial(place_weight_kernel, start=0, width=1),
        [scal, w2_own, two],
        [((w2_own.shape[0], HALF), BF)],
    )[0]
    j = b // split
    ctx_rows = -(-ctx_len // 16) * 16
    ctx_w = jnp.stack(
        [
            lax.dynamic_slice_in_dim(
                ctx_weight, 128 * (hh + 2 * (j // 2)) + HEAD * (j % 2), HEAD, 2
            ).reshape(-1, 2 * HEAD)
            for hh in range(2)
        ]
    )
    ctx_term = jnp.einsum("itx,hxk->ihtk", context, ctx_w, preferred_element_type=F32)
    ctx_term = jnp.pad(
        ctx_term.astype(BF).reshape(4, ctx_len, 2 * HEAD),
        ((0, 0), (0, ctx_rows - ctx_len), (0, 0)),
    )
    ctx_kv = lax.psum_scatter(ctx_term, "ch", scatter_dimension=0)
    live = (CLIPTOK + jnp.where(i == 0, text_len[0], text_len[1])).astype(jnp.int32)[None]

    emb_f = jnp.repeat(emb_act.astype(F32), 2, axis=1)
    odd = (jnp.arange(emb_f.shape[1]) % 2)[None]
    emb_rows = jnp.concatenate(
        [emb_f * (1 - odd), emb_f * odd, jnp.zeros((4, emb_f.shape[1]), F32)], axis=0
    )
    kind = dict(cells=cells, size=size)
    ext = pix + 2 * COLS
    stat_shape = ((2 * blocks, 8, HALF), F32)

    c_mine, c_theirs = call(
        image_split_kernel,
        [scal, cotangent.reshape(images, pix, width)],
        [((pix, width), BF)] * 2,
        deps=[x_sums],
    )

    hid_own, hid_stat, act1, vec = call(
        functools.partial(conv1_kernel, **kind),
        [scal, x_own, x_oth, x_top, x_bot, sums1, w1],
        [((ext, HALF), BF), stat_shape, ((pix, channels), BF), ((4, 16, LANES), F32)],
        [((ext + 2 * COLS, channels), BF)],
        deps=[ctx_term, c_mine, emb_rows, live],
    )
    hid_oth = over_ch(hid_own, 1)
    sums2 = to_image(hid_stat)

    c_mine, c_theirs = after((c_mine, c_theirs), hid_oth, w2)
    c_one, c_two = over_ch(c_mine, 1), over_ch(c_theirs, 2)
    c_three = over_ch(c_two, 1)
    cot_own = jnp.concatenate(by_image(c_mine, c_two), **wide)
    cot_oth = jnp.concatenate(by_image(c_one, c_three), **wide)

    edges = ((2, edge, HALF), BF)
    res_f, res_own, res_stat, act_first, act_rest, res_edges = call(
        functools.partial(conv2_kernel, **kind),
        [scal, hid_own, hid_oth, sums2, vec, w2, x_own, act1],
        [
            ((pix, HALF), F32),
            ((pix, HALF), BF),
            stat_shape,
            ((pix // 2, channels), BF),
            ((pix + pix // 2, channels), BF),
            edges,
        ],
        [((ext, channels), BF)],
    )
    res_oth = over_ch(res_own, 1)
    sums3 = to_image(res_stat)
    wp = call(
        functools.partial(place_weight_kernel, start=w2_rows, width=4),
        [scal, wp_own, two],
        [((channels, 4 * HALF), BF)],
        deps=[res_oth],
    )[0]
    packed, act3, cot_all, cot_edges = call(
        functools.partial(qkv_kernel, **kind),
        [scal, res_own, res_oth, sums3, vec, cot_own, cot_oth, wp],
        [((4, pix, HALF), BF), ((pix, channels), BF), ((pix, channels), BF), edges],
        deps=[ctx_kv],
    )
    recv = lax.all_to_all(packed.reshape(blocks, pix // split, HALF), "blk", 0, 0)
    res_edges, act_first = after((res_edges, act_first), packed)
    res_top, res_bot = halo(res_edges[0], res_edges[1])
    cot_top, cot_bot = halo(cot_edges[0], cot_edges[1])
    first_there = over_ch(act_first, 2)
    (recv,) = after((recv,), res_top, res_bot, cot_top, cot_bot, first_there)
    recv = recv.reshape(-1, HALF)
    rest_there = over_ch(act_rest, 2)
    if split == 2:
        kva, kvb = recv, over_blk(recv[:, :LANES], 1)
    else:
        groups = [[n * split + m for m in range(split)] for n in range(4)]
        kv_all = lax.all_gather(
            recv[:, :LANES], "blk", axis=0, tiled=True, axis_index_groups=groups
        )
        kva, kvb = kv_all[: kv_all.shape[0] // 2], kv_all[kv_all.shape[0] // 2 :]
    dqo, dkva, dkvb, dctx = attend(live, recv, kva, kvb, ctx_kv, [])
    if split == 2:
        d_ctx = dctx + over_blk(dctx, 1)
        back = call(
            merge_kernel,
            [scal, dkva, over_blk(dkvb, 1), dqo],
            [((dqo.shape[0], HALF), BF)],
            deps=[rest_there],
        )[0]
    else:
        d_ctx = lax.psum(dctx, "blk", axis_index_groups=groups)
        d_kv = lax.psum_scatter(
            jnp.concatenate([dkva, dkvb.astype(F32)], axis=0),
            "blk",
            scatter_dimension=0,
            axis_index_groups=groups,
            tiled=True,
        )
        back = jnp.concatenate([d_kv.astype(BF), dqo], axis=1)
    grads = lax.all_to_all(back.reshape(blocks, pix // split, HALF), "blk", 0, 0)
    grads = grads.reshape(4, pix, HALF)

    features = context.shape[2] // split
    d_ctx = d_ctx[:ctx_len].astype(BF)
    ctx_part = call(
        functools.partial(context_grad_kernel, split=split),
        [scal, context, d_ctx] + [over_ch(d_ctx, mask) for mask in (1, 2, 3)],
        [((features, HALF), BF)],
        [((context.shape[2], HALF), F32)],
    )[0]
    ctx_all = lax.all_gather(ctx_part, "blk", axis=0)

    def low_grad(rows):
        return [((rows, HALF), F32), ((rows, HALF), BF), stat_shape]

    p3_own, p3_oth, st3 = call(
        functools.partial(qkv_back_kernel, **kind),
        [scal, grads, wp, res_own, res_oth, sums3, vec],
        low_grad(pix),
        [((pix, channels), F32)],
        deps=[ctx_part],
    )
    r3 = over_ch(p3_oth, 1)
    stats3 = to_image(st3)
    proj_own, proj_oth, wp_part = call(
        out_kernel,
        [scal, grads, wp, act3, cot_all],
        [((pix, HALF), F32), ((pix, HALF), BF), ((2, 4 * channels, LANES), BF)],
        [((pix, channels), F32)],
        deps=[r3],
    )
    first3 = (p3_own[:edge] + r3[:edge].astype(F32)).astype(BF)
    last3 = (p3_own[pix - edge :] + r3[pix - edge :].astype(F32)).astype(BF)
    d_top3, d_bot3 = halo(first3, last3)
    d_resid, ext2, away2 = call(
        functools.partial(norm3_back_kernel, **kind),
        [
            scal, p3_own, r3, d_top3, d_bot3, res_own, res_top, res_bot, cot_own, cot_top, cot_bot,
            sums3, stats3, vec,
        ],
        [((pix, HALF), F32), ((ext + 2 * COLS, HALF), BF), ((ext, LANES), BF)],
        deps=[proj_own],
    )
    there2 = over_ch(away2, 2)
    p2_own, p2_oth, st2 = call(
        functools.partial(conv_back_kernel, which=1, **kind),
        [scal, ext2, w2, hid_own, hid_oth, sums2, vec],
        low_grad(ext),
        [((ext, channels), F32)],
        time=8.0,
    )
    r2 = over_ch(p2_oth, 1)
    (st2,) = after((st2,), there2)
    stats2 = to_image(st2)
    conv_rows, wp_rows = 9 * channels // blocks, 4 * channels // blocks
    part2 = call(
        weight_grad_two_kernel,
        [scal, act_rest, rest_there, ext2, there2, wp_part],
        [((blocks, conv_rows + 2 * wp_rows, LANES), BF)],
        [((2, pix, 9 * LANES), BF), ((9 * channels, LANES), F32)],
        deps=[r2],
    )[0]
    ext1, away1 = call(
        functools.partial(norm2_back_kernel, **kind),
        [scal, p2_own, r2, hid_own, sums2, stats2, vec],
        [((ext, HALF), BF), ((ext, LANES), BF)],
        deps=[part2, ctx_all],
    )
    parts2 = lax.all_to_all(part2, "blk", 0, 0)
    there1 = over_ch(away1, 2)
    p1_own, p1_oth, st1 = call(
        functools.partial(conv_back_kernel, which=0, **kind),
        [scal, ext1, w1, x_own, x_oth, sums1, vec],
        low_grad(pix),
        [((pix, channels), F32)],
        time=8.0,
    )
    (st1,) = after((st1,), there1, parts2)
    (proj_late,) = after((proj_oth,), there1)
    r1 = over_ch(p1_oth, 1)
    stats1 = to_image(st1)
    half_shape = (4, 9 * channels // 8, LANES)
    keep1, send1 = call(
        weight_grad_one_kernel,
        [scal, act_first, act_rest, first_there, rest_there, ext1, there1],
        [(half_shape, F32), (half_shape, BF)],
        [((2, pix, 9 * LANES), BF), ((9 * channels, LANES), F32)],
        deps=[p1_own],
        time=20.0,
    )
    if blocks == 8:
        own1, *sends = call(
            scatter_kernel,
            [scal, keep1, over_blk(send1, 1)],
            [((conv_rows, LANES), F32)] + [((conv_rows, LANES), BF)] * 3,
        )
    else:
        own1 = keep1
    if blocks == 8:
        other = call(other_sum_kernel, [scal, parts2], [((wp_rows, LANES), BF)], deps=[own1])[0]
        total = call(
            total_kernel,
            [scal, own1, parts2, over_ch(other, 2)]
            + [over_blk(v, 2 * n + 2) for n, v in enumerate(sends)],
            [((2 * conv_rows + wp_rows, LANES), BF)],
        )[0]
    else:
        total = own1
    out_keep, out_send = call(
        out_add_kernel,
        [scal, res_f, proj_own, over_ch(proj_late, 1)],
        [((pix, width), BF)] * 2,
        deps=[total],
    )
    in_keep, in_send = call(
        functools.partial(last_kernel, **kind),
        [scal, p1_own, r1, x_own, sums1, stats1, vec, d_resid],
        [((pix, width), F32), ((pix, width), BF)],
        [((pix, HALF), F32)],
        deps=[total],
        time=40.0,
    )
    sums_here, sums_away = call(
        channel_sums_kernel,
        [scal, stats1, stats2, stats3],
        [((8, LANES), F32)] * 2,
        deps=[total],
    )
    sums_recv = over_ch(sums_away, 2)
    out_recv, in_recv = over_ch(out_send, 2), over_ch(in_send, 2)
    bias_grad, *smalls, embed_weight_grad = call(
        channel_grads_kernel,
        [scal, sums_here, sums_recv, local_vec, emb_rows],
        [((2, LANES), F32)] + [((1, LANES), F32)] * 6 + [((emb_rows.shape[1], LANES), F32)],
        deps=[total],
        time=15.0,
    )
    block_output, input_grad = call(
        by_images_kernel,
        [scal, out_keep, out_recv, in_keep, in_recv],
        [((images, pix, width), BF), ((images, pix, width), F32)],
        deps=[total],
        time=10.0,
    )
    if blocks == 8:
        ctx_grad = call(
            functools.partial(context_place_kernel, split=split),
            [scal, ctx_all],
            [((context.shape[2], 2, channels), F32)],
            deps=[total],
            time=10.0,
        )[0]
        grad1, grad2, qkv_grad, out_grad = call(
            place_kernel,
            [scal] + plane(total),
            [((9 * channels, LANES), F32)] * 2
            + [((3 * channels, LANES), F32), ((LANES, channels), F32)],
            deps=[block_output, ctx_grad, bias_grad],
        )
    else:
        ctx_grad = ctx_all.reshape(2, 2, split, features, 2, 2, HEAD)
        ctx_grad = jnp.transpose(ctx_grad, (2, 3, 5, 0, 4, 1, 6)).astype(F32)
        flip = lambda c: jnp.where(b % 2 == 0, *((keep1.astype(BF), send1)[:: 1 - 2 * c]))
        grad1 = lax.psum(jnp.concatenate([flip(0), flip(1)], axis=0), "blk").astype(F32)
        sums = lax.psum(part2, "blk").astype(F32)
        cut = conv_rows + wp_rows
        grad2 = sums[:, :conv_rows]
        wp_grad = sums[:, conv_rows:cut] + over_ch(sums[:, cut:].astype(BF), 2).astype(F32)
        wp_grad = wp_grad.reshape(-1, LANES)
        qkv_grad, out_grad = wp_grad[: 3 * channels], wp_grad[3 * channels :]
        out_grad = jnp.concatenate(list(out_grad.reshape(-1, LANES, LANES)), axis=1)
    qkv_grad = jnp.transpose(qkv_grad.reshape(3, channels, LANES), (1, 0, 2))

    return (
        block_output.reshape(block_input.shape),
        input_grad.reshape(block_input.shape),
        grad1.reshape(conv1_weight.shape),
        grad2.reshape(conv2_weight.shape),
        embed_weight_grad.reshape(embed_weight.shape),
        bias_grad,
        *(value.reshape(width) for value in smalls),
        qkv_grad,
        out_grad,
        ctx_grad.reshape(ctx_weight.shape),
    )


def solution(mesh):
    return jax.shard_map(
        body,
        mesh=mesh,
        in_specs=(
            P(None, "blk", None, "ch"),
            P(None, "blk", None, "ch"),
            P(),
            P(),
            P(),
            P(None, None, "ch"),
            P(None, None, None, "ch"),
            P(None, None, None, "ch"),
            P(None, None, "ch"),
            P(None, "ch"),
            P("ch"),
            P("ch"),
            P("ch"),
            P("ch"),
            P("ch"),
            P("ch"),
            P(None, None, "ch"),
            P("ch", None),
            P("ch", None, None),
        ),
        out_specs=(
            P(None, "blk", None, "ch"),
            P(None, "blk", None, "ch"),
            P(None, None, None, "ch"),
            P(None, None, None, "ch"),
            P(None, None, "ch"),
            P(None, "ch"),
            P("ch"),
            P("ch"),
            P("ch"),
            P("ch"),
            P("ch"),
            P("ch"),
            P(None, None, "ch"),
            P("ch", None),
            P("ch", None, None),
        ),
        check_vma=False,
    )
```

```python
import functools
import math

import jax
import jax.numpy as jnp
from jax import lax
from jax.experimental import pallas as pl
from jax.experimental.pallas import tpu as pltpu
from jax.sharding import PartitionSpec as P

HEAD = 64
GROUPS = 32
CLIPTOK = 4
LANES = 128
HALF = 256
COLS = 64
VMEM_BYTES = 56 * 2**20
BF = jnp.bfloat16
F32 = jnp.float32

H, I, UP1, DOWN1, UP2, DOWN2, Z, B = range(8)


def dot(a, b):
    return jnp.dot(a, b, preferred_element_type=F32)


def dot_t(a, b):
    return lax.dot_general(a, b, (((1,), (1,)), ((), ())), preferred_element_type=F32)


def group_sum(vec, size):
    lane = lax.broadcasted_iota(jnp.int32, vec.shape, 1)
    step = 1
    while step < size:
        low = pltpu.roll(vec, step, 1)
        high = pltpu.roll(vec, LANES - step, 1)
        vec = vec + jnp.where((lane & step) != 0, low, high)
        step *= 2
    return vec


def shards(scal):
    h = scal[H]
    return (h, h + 2, 1 - h, 3 - h)


def lanes_of(shard):
    return pl.ds(pl.multiple_of(shard * LANES, LANES), LANES)


def part_of(quarter):
    return slice((quarter % 2) * LANES, (quarter % 2 + 1) * LANES)


def norm_stats(scal, sums, quarter, cells, size):
    wide = sums.shape[2] == HALF
    kinds = 2 if wide else 4
    shard = shards(scal)[quarter]
    total = None
    for source in range(sums.shape[0] // kinds):
        row = source * kinds + (shard % 2 if wide else shard)
        piece = sums[pl.ds(row, 1)][0]
        total = piece if total is None else total + piece
    if wide:
        total = total[:, part_of(quarter)]
    total = group_sum(total, size)
    mean = total[0:1] / cells
    inv = lax.rsqrt(total[1:2] / cells - mean * mean + 1e-05)
    return mean, inv


def affine_of(scal, vec, quarter, which, mean, inv):
    row = vec[pl.ds(shards(scal)[quarter], 1)][0]
    gain = row[2 * which + 2 : 2 * which + 3]
    bias = row[2 * which + 3 : 2 * which + 4]
    if which == 1:
        first = scal[I] == 0
        grow = 1.0 + jnp.where(first, row[8:9], row[10:11])
        gain, bias = gain * grow, bias * grow + jnp.where(first, row[9:10], row[11:12])
    slope = inv * gain
    return gain, slope, bias - mean * slope


def column_sums(first, second):
    rows = jnp.concatenate(
        [jnp.sum(first, axis=0, keepdims=True), jnp.sum(second, axis=0, keepdims=True)], axis=0
    )
    return jnp.concatenate([rows, jnp.zeros((6, rows.shape[1]), F32)], axis=0)


def shift_columns(total, left, right):
    col = lax.broadcasted_iota(jnp.int32, total.shape, 0) % COLS
    rows = total.shape[0]
    total = total + jnp.where(col > 0, pltpu.roll(left, 1, 0), 0.0)
    return total + jnp.where(col < COLS - 1, pltpu.roll(right, rows - 1, 0), 0.0)


def silu_slope(field):
    sigma = jax.nn.sigmoid(field)
    return sigma * (1.0 + field * (1.0 - sigma))


def masked_rows(scal, value, flag):
    return jnp.where(scal[flag] > 0, value, 0.0)


def input_sums_kernel(scal, field, vec, out, *, blocks):
    for image in range(2):
        value = field[image].astype(F32)
        sums = column_sums(value, value * value)[:2]
        sums = jnp.concatenate([sums, vec[2:]], axis=0)
        for target in range(blocks):
            out[4 * target + 2 * image] = sums
            out[4 * target + 2 * image + 1] = sums


def image_split_kernel(scal, field, mine, theirs):
    mine[...] = field[pl.ds(scal[I], 1)][0]
    theirs[...] = field[pl.ds(1 - scal[I], 1)][0]


def spread(out, sums):
    for target in range(out.shape[0]):
        out[target] = sums


def conv1_kernel(scal, own, oth, top, bot, sums, weight, out, out_sums, act_out, vec, act_scr, *, cells, size):
    pix = own.shape[0]
    vec[...] = sums[0:4]
    rows = pix + 2 * COLS
    for quarter in range(4):
        shard = shards(scal)[quarter]
        mean, inv = norm_stats(scal, sums, quarter, cells, size)
        gain, slope, offset = affine_of(scal, vec, quarter, 0, mean, inv)
        lanes = slice(quarter * LANES, (quarter + 1) * LANES)

        def active(field):
            pre = field.astype(F32) * slope + offset
            return pre * jax.nn.sigmoid(pre)

        half = own if quarter < 2 else oth
        main = active(half[:, part_of(quarter)]).astype(BF)
        above, below = active(top[:, lanes]), active(bot[:, lanes])
        act_scr[2 * COLS : 2 * COLS + pix, lanes_of(shard)] = main
        act_out[:, lanes_of(shard)] = main
        act_scr[0:COLS, lanes_of(shard)] = masked_rows(scal, above[:COLS], UP2).astype(BF)
        act_scr[COLS : 2 * COLS, lanes_of(shard)] = masked_rows(scal, above[COLS:], UP1).astype(BF)
        end = 2 * COLS + pix
        act_scr[end : end + COLS, lanes_of(shard)] = masked_rows(scal, below[:COLS], DOWN1).astype(BF)
        act_scr[end + COLS :, lanes_of(shard)] = masked_rows(scal, below[COLS:], DOWN2).astype(BF)
    result = convolve(act_scr, weight, rows)
    out[...] = result.astype(BF)
    inner = result[COLS : COLS + pix]
    spread(out_sums, column_sums(inner, inner * inner))


def convolve(act_scr, weight, rows):
    channels = act_scr.shape[1]
    parts = []
    for kx in range(3):
        acc = None
        for ky in range(3):
            tap = (ky * 3 + kx) * channels
            term = dot(act_scr[ky * COLS : ky * COLS + rows, :], weight[tap : tap + channels, :])
            acc = term if acc is None else acc + term
        parts.append(acc)
    return shift_columns(parts[1], parts[0], parts[2])


def conv2_kernel(scal, own, oth, sums, vec, weight, base, act_below, out_f, out_low, out_sums, act_first, act_out, edges, act_scr, *, cells, size):
    pix = base.shape[0]
    cut = act_first.shape[0]
    act_first[...] = act_below[0:cut]
    act_out[0 : pix - cut, :] = act_below[cut:]
    for quarter in range(4):
        shard = shards(scal)[quarter]
        mean, inv = norm_stats(scal, sums, quarter, cells, size)
        gain, slope, offset = affine_of(scal, vec, quarter, 1, mean, inv)
        half = own if quarter < 2 else oth
        pre = half[:, part_of(quarter)].astype(F32) * slope + offset
        act = pre * jax.nn.sigmoid(pre)
        main = act[COLS : COLS + pix].astype(BF)
        act_scr[COLS : COLS + pix, lanes_of(shard)] = main
        act_out[pix - cut :, lanes_of(shard)] = main
        act_scr[0:COLS, lanes_of(shard)] = masked_rows(scal, act[:COLS], UP1).astype(BF)
        act_scr[COLS + pix :, lanes_of(shard)] = masked_rows(scal, act[COLS + pix :], DOWN1).astype(BF)
    result = convolve(act_scr, weight, pix) + base[...].astype(F32)
    out_f[...] = result
    low = result.astype(BF)
    out_low[...] = low
    if edges.shape[1] < pix:
        edges[0], edges[1] = low[: edges.shape[1]], low[pix - edges.shape[1] :]
    else:
        edges[0], edges[1] = low, low
    spread(out_sums, column_sums(result, result * result))


def qkv_kernel(scal, own, oth, sums, vec, cot_own, cot_oth, weight, out, act_out, cot_out, edges, *, cells, size):
    rows = edges.shape[1]
    edges[0], edges[1] = cot_own[0:rows], cot_own[cot_own.shape[0] - rows :]
    for quarter in range(4):
        shard = shards(scal)[quarter]
        mean, inv = norm_stats(scal, sums, quarter, cells, size)
        gain, slope, offset = affine_of(scal, vec, quarter, 2, mean, inv)
        half = own if quarter < 2 else oth
        cot = cot_own if quarter < 2 else cot_oth
        field = half[:, part_of(quarter)].astype(F32)
        act_out[:, lanes_of(shard)] = (field * slope + offset).astype(BF)
        cot_out[:, lanes_of(shard)] = cot[:, part_of(quarter)]
    for head in range(4):
        columns = weight[:, head * HALF : (head + 1) * HALF]
        fwd = dot(act_out[...], columns)
        back = dot(cot_out[...], columns[:, LANES:])
        out[head, :, :LANES] = fwd[:, :LANES].astype(BF)
        lane = lax.broadcasted_iota(jnp.int32, back.shape, 1)
        out[head, :, LANES:] = jnp.where(lane < HEAD, fwd[:, LANES:], back).astype(BF)


def below_stats(scal, total, own, oth, sums, vec, out_own, out_oth, out_stats, which, cells, size):
    rows = total.shape[0]
    pix = rows - 2 * COLS if which == 1 else rows
    inner = slice(COLS, COLS + pix) if which == 1 else slice(0, pix)
    for quarter in range(4):
        shard = shards(scal)[quarter]
        mean, inv = norm_stats(scal, sums, quarter, cells, size)
        gain, slope, offset = affine_of(scal, vec, quarter, which, mean, inv)
        half = own if quarter < 2 else oth
        part = part_of(quarter)
        if quarter < 2:
            out_own[:, part] = total[:, lanes_of(shard)]
        else:
            out_oth[:, part] = total[:, lanes_of(shard)].astype(BF)
        grad = total[inner, lanes_of(shard)]
        field = half[inner, part].astype(F32)
        if which < 2:
            grad = grad * silu_slope(field * slope + offset)
        result = column_sums(grad, grad * ((field - mean) * inv))
        slot = scal[H] if quarter < 2 else 1 - scal[H]
        for target in range(out_stats.shape[0] // 2):
            out_stats[pl.ds(2 * target + slot, 1), :, part] = result[None]


def qkv_back_kernel(scal, grads, weight, own, oth, sums, vec, out_own, out_oth, out_stats, tot_scr, *, cells, size):
    total = None
    for head in range(4):
        columns = weight[:, head * HALF : (head + 1) * HALF]
        grad = grads[head]
        lane = lax.broadcasted_iota(jnp.int32, grad.shape, 1)
        term = dot_t(jnp.where(lane < 3 * HEAD, grad, jnp.zeros_like(grad)), columns)
        total = term if total is None else total + term
    tot_scr[...] = total
    below_stats(scal, tot_scr, own, oth, sums, vec, out_own, out_oth, out_stats, 2, cells, size)


def out_kernel(scal, grads, weight, act, cot, proj_own, proj_oth, wgrad, tot_scr):
    channels = act.shape[1]
    act_t = act[...].astype(F32).T.astype(BF)
    total = None
    for pair in range(2):
        slot = jnp.where(scal[I] == pair, 0, 1)
        parts, outs = [], []
        for head in (2 * pair, 2 * pair + 1):
            columns = weight[:, head * HALF + LANES : (head + 1) * HALF]
            grad = grads[head]
            low = grad[:, LANES:]
            lane = lax.broadcasted_iota(jnp.int32, low.shape, 1)
            term = dot_t(jnp.where(lane < HEAD, jnp.zeros_like(low), low), columns)
            total = term if total is None else total + term
            parts.append(dot(act_t, grad))
            outs.append(dot(low.astype(F32).T[HEAD:].astype(BF), cot[...]))
        first, second = parts
        pieces = [
            jnp.concatenate([first[:, LANES : LANES + HEAD], second[:, LANES : LANES + HEAD]], axis=1)
            * 0.125,
            jnp.concatenate([first[:, :HEAD], second[:, :HEAD]], axis=1),
            jnp.concatenate([first[:, HEAD:LANES], second[:, HEAD:LANES]], axis=1),
        ]
        both = jnp.concatenate(outs, axis=0)
        pieces += [both[:, n * LANES : (n + 1) * LANES] for n in range(channels // LANES)]
        wgrad[pl.ds(slot, 1)] = jnp.concatenate(pieces, axis=0).astype(BF)[None]
    tot_scr[...] = total
    for quarter, shard in enumerate(shards(scal)):
        if quarter < 2:
            proj_own[:, part_of(quarter)] = tot_scr[:, lanes_of(shard)]
        else:
            proj_oth[:, part_of(quarter)] = tot_scr[:, lanes_of(shard)].astype(BF)


def total_stats(stats):
    total = stats[0]
    for source in range(1, stats.shape[0]):
        total = total + stats[source]
    return total


def norm_back(scal, quarter, sums, stats, vec, which, cells, size):
    mean, inv = norm_stats(scal, sums, quarter, cells, size)
    gain, slope, offset = affine_of(scal, vec, quarter, which, mean, inv)
    means = group_sum(total_stats(stats)[:, part_of(quarter)] * gain, size) / cells

    def back(grad, field):
        field = field.astype(F32)
        hat = (field - mean) * inv
        if which < 2:
            grad = grad * silu_slope(field * slope + offset)
        return (grad * gain - means[0:1] - hat * means[1:2]) * inv

    return back


def norm3_back_kernel(
    scal, part, recv, dtop, dbot, field, ftop, fbot, cot, ctop, cbot, sums, stats, vec, out_f, ext, away, *, cells, size
):
    pix = part.shape[0]
    end = 2 * COLS + pix
    for quarter in range(2):
        lanes = part_of(quarter)
        back = norm_back(scal, quarter, sums, stats, vec, 2, cells, size)
        main = back(part[:, lanes] + recv[:, lanes].astype(F32), field[:, lanes])
        main = main + cot[:, lanes].astype(F32)
        out_f[:, lanes] = main
        ext[2 * COLS : end, lanes] = main.astype(BF)
        head = back(dtop[:, lanes].astype(F32), ftop[:, lanes]) + ctop[:, lanes].astype(F32)
        tail = back(dbot[:, lanes].astype(F32), fbot[:, lanes]) + cbot[:, lanes].astype(F32)
        ext[0:COLS, lanes] = masked_rows(scal, head[:COLS], UP2).astype(BF)
        ext[COLS : 2 * COLS, lanes] = masked_rows(scal, head[COLS:], UP1).astype(BF)
        ext[end : end + COLS, lanes] = masked_rows(scal, tail[:COLS], DOWN1).astype(BF)
        ext[end + COLS :, lanes] = masked_rows(scal, tail[COLS:], DOWN2).astype(BF)
    away[...] = ext[COLS : end + COLS, lanes_of(1 - scal[I])]


def norm2_back_kernel(scal, part, recv, field, sums, stats, vec, ext, away, *, cells, size):
    rows = part.shape[0]
    for quarter in range(2):
        lanes = part_of(quarter)
        back = norm_back(scal, quarter, sums, stats, vec, 1, cells, size)
        main = back(part[:, lanes] + recv[:, lanes].astype(F32), field[:, lanes])
        ext[0:COLS, lanes] = masked_rows(scal, main[:COLS], UP1).astype(BF)
        ext[COLS : rows - COLS, lanes] = main[COLS : rows - COLS].astype(BF)
        ext[rows - COLS :, lanes] = masked_rows(scal, main[rows - COLS :], DOWN1).astype(BF)
    away[...] = ext[:, lanes_of(1 - scal[I])]


def conv_back_kernel(scal, ext, weight, own, oth, sums, vec, out_own, out_oth, out_stats, tot_scr, *, which, cells, size):
    rows, channels = tot_scr.shape
    parts = []
    for kx in range(3):
        acc = None
        for ky in range(3):
            tap = (ky * 3 + kx) * channels
            start = (2 - ky) * COLS
            term = dot_t(ext[start : start + rows, :], weight[tap : tap + channels, :])
            acc = term if acc is None else acc + term
        parts.append(acc)
    tot_scr[...] = shift_columns(parts[1], parts[2], parts[0])
    below_stats(scal, tot_scr, own, oth, sums, vec, out_own, out_oth, out_stats, which, cells, size)


def last_kernel(scal, part, recv, field, sums, stats, vec, resid_grad, keep, send, tot_scr, *, cells, size):
    i = scal[I]
    for quarter in range(2):
        lanes = part_of(quarter)
        back = norm_back(scal, quarter, sums, stats, vec, 0, cells, size)
        main = back(part[:, lanes] + recv[:, lanes].astype(F32), field[:, lanes])
        tot_scr[:, lanes] = main + resid_grad[:, lanes]
    keep[...] = tot_scr[:, lanes_of(i)]
    send[...] = tot_scr[:, lanes_of(1 - i)].astype(BF)


def weight_grads(scal, act_one, act_two, ext_one, ext_two, rhs_scr, out_scr):
    pix, channels = act_one.shape
    rows = ext_two.shape[0]
    first = (ext_one.shape[0] - rows) // 2
    own = ext_one[first : first + rows, lanes_of(scal[I])]
    for image, wide in enumerate((own, ext_two[...])):
        wide = wide.astype(F32)
        col = lax.broadcasted_iota(jnp.int32, wide.shape, 0) % COLS
        for kx in range(3):
            if kx == 0:
                moved = jnp.where(col < COLS - 1, pltpu.roll(wide, rows - 1, 0), 0.0)
            elif kx == 2:
                moved = jnp.where(col > 0, pltpu.roll(wide, 1, 0), 0.0)
            else:
                moved = wide
            moved = moved.astype(BF)
            for ky in range(3):
                start = (2 - ky) * COLS
                tap = ky * 3 + kx
                lanes = slice(tap * LANES, (tap + 1) * LANES)
                rhs_scr[image * pix : (image + 1) * pix, lanes] = moved[start : start + pix]
    both = jnp.concatenate([act_one, act_two], axis=0)
    for tap in range(0, 9, 2):
        count = min(2, 9 - tap)
        total = lax.dot_general(
            both,
            rhs_scr[:, tap * LANES : (tap + count) * LANES],
            (((0,), (0,)), ((), ())),
            preferred_element_type=F32,
        )
        for n in range(count):
            out_scr[(tap + n) * channels : (tap + n + 1) * channels, :] = total[
                :, n * LANES : (n + 1) * LANES
            ]


def weight_grad_one_kernel(
    scal, up, low, up_there, low_there, ext_one, ext_two, keep, send, rhs_scr, out_scr
):
    cut = up.shape[0]
    mine = jnp.concatenate([up[...], low[0:cut]], axis=0)
    theirs = jnp.concatenate([up_there[...], low_there[0:cut]], axis=0)
    weight_grads(scal, mine, theirs, ext_one, ext_two, rhs_scr, out_scr)
    core = scal[B] % 2
    count = out_scr.shape[0] // 2
    at = lambda n: pl.ds(pl.multiple_of(n * count, count), count)
    keep[...] = out_scr[at(core), :].reshape(keep.shape)
    send[...] = out_scr[at(1 - core), :].astype(BF).reshape(send.shape)


def weight_grad_two_kernel(scal, act, act_there, ext_one, ext_two, wp, out, rhs_scr, out_scr):
    cut = act.shape[0] // 3
    weight_grads(scal, act[cut:], act_there[cut:], ext_one, ext_two, rhs_scr, out_scr)
    blocks = out.shape[0]
    rows = out_scr.shape[0] // blocks
    extra = wp.shape[1] // blocks
    out[:, :rows] = out_scr[...].astype(BF).reshape(blocks, rows, LANES)
    for part in range(2):
        first = rows + part * extra
        out[:, first : first + extra] = wp[part].reshape(blocks, extra, LANES)


def other_sum_kernel(scal, parts, out):
    first = parts.shape[1] - out.shape[0]
    total = parts[0, first:].astype(F32)
    for source in range(1, parts.shape[0]):
        total = total + parts[source, first:].astype(F32)
    out[...] = total.astype(BF)


def total_kernel(scal, own, parts, other, one, two, three, out):
    count = own.shape[0]
    extra = other.shape[0]
    first = own[...] + one[...].astype(F32) + two[...].astype(F32) + three[...].astype(F32)
    out[0:count] = first.astype(BF)
    second = parts[0, : count + extra].astype(F32)
    for source in range(1, parts.shape[0]):
        second = second + parts[source, : count + extra].astype(F32)
    out[count : 2 * count] = second[:count].astype(BF)
    out[2 * count :] = (second[count:] + other[...].astype(F32)).astype(BF)


def scatter_kernel(scal, keep, recv, own, *sends):
    chip = scal[B] // 2
    for mask in range(4):
        chunk = pl.ds(chip ^ mask, 1)
        value = (keep[chunk] + recv[chunk].astype(F32))[0]
        if mask == 0:
            own[...] = value
        else:
            sends[mask - 1][...] = value.astype(BF)


def place_kernel(scal, *refs):
    pieces, (one, two, qkv, out) = refs[:8], refs[8:]
    core, chip = scal[B] % 2, scal[B] // 2
    count = one.shape[0] // 8
    rows = qkv.shape[0] // 6
    for n, piece in enumerate(pieces):
        half = core if n < 4 else 1 - core
        source = chip ^ (n % 4)
        at = lambda slot, size: pl.ds(pl.multiple_of(slot * size, size), size)
        slot = 2 * source + half
        one[at(4 * half + source, count), :] = piece[:count].astype(F32)
        two[at(slot, count), :] = piece[count : 2 * count].astype(F32)
        extra = piece[2 * count :].astype(F32)

        @pl.when(slot < 6)
        def _(extra=extra, slot=slot):
            qkv[at(slot, rows), :] = extra

        @pl.when(slot >= 6)
        def _(extra=extra, slot=slot):
            for m in range(rows // LANES):
                column = (slot - 6) * (rows // LANES) + m
                out[:, lanes_of(column)] = extra[m * LANES : (m + 1) * LANES]


def channel_sums_kernel(scal, one, two, three, mine, theirs):
    rows = jnp.concatenate([total_stats(stats)[0:2] for stats in (one, two, three)], axis=0)
    rows = jnp.concatenate([rows, jnp.zeros((2, rows.shape[1]), F32)], axis=0)
    first, second = rows[:, :LANES], rows[:, LANES:]
    here = scal[I] == 0
    mine[...] = jnp.where(here, first, second)
    theirs[...] = jnp.where(here, second, first)


def channel_grads_kernel(scal, mine, recv, vec, emb, bias_grad, *outs):
    here = scal[I] == 0
    images = (
        jnp.where(here, mine[...], recv[...]),
        jnp.where(here, recv[...], mine[...]),
    )
    gain, bias = vec[4:5], vec[5:6]
    scales = [gain * rows[3:4] + bias * rows[2:3] for rows in images]
    shifts = [rows[2:3] for rows in images]
    grown = [1.0 + vec[8:9], 1.0 + vec[10:11]]
    both = images[0] + images[1]
    bias_grad[0:1] = scales[0] + scales[1]
    bias_grad[1:2] = shifts[0] + shifts[1]
    values = [
        both[1:2],
        both[0:1],
        grown[0] * images[0][3:4] + grown[1] * images[1][3:4],
        grown[0] * images[0][2:3] + grown[1] * images[1][2:3],
        both[5:6],
        both[4:5],
    ]
    for out, value in zip(outs, values):
        out[...] = value
    weight_grad = outs[6]
    turned = emb[...].T
    total = None
    for n, row in enumerate(scales + shifts):
        term = turned[:, n : n + 1] * row
        total = term if total is None else total + term
    weight_grad[...] = total


def out_add_kernel(scal, resid, part, recv, keep, send):
    total = resid[...] + part[...] + recv[...].astype(F32)
    first, second = total[:, :LANES].astype(BF), total[:, LANES:].astype(BF)
    here = scal[I] == 0
    keep[...] = jnp.where(here, first, second)
    send[...] = jnp.where(here, second, first)


def by_images_kernel(scal, out_keep, out_recv, in_keep, in_recv, block_output, input_grad):
    i = scal[I]
    for keep, recv, out in ((out_keep, out_recv, block_output), (in_keep, in_recv, input_grad)):
        out[pl.ds(i, 1)] = keep[...][None]
        out[pl.ds(1 - i, 1)] = recv[...].astype(out.dtype)[None]


def merge_kernel(scal, mine, recv, rest, out):
    out[:, :LANES] = (mine[...] + recv[...].astype(F32)).astype(BF)
    out[:, LANES:] = rest[...]


def context_grad_kernel(scal, context, d_zero, d_one, d_two, d_three, out, tot_scr, *, split):
    rows = out.shape[0]
    turned = [context[image].astype(F32).T.astype(BF) for image in range(2)]
    pieces = (d_zero, d_one, d_two, d_three)
    for h in range(2):
        total = None
        for image in range(2):
            slot = (2 * image + h) ^ scal[Z]
            chosen = pieces[0][...]
            for n in range(1, 4):
                chosen = jnp.where(slot == n, pieces[n][...], chosen)
            term = dot(turned[image], chosen)
            total = term if total is None else total + term
        tot_scr[:, h * LANES : (h + 1) * LANES] = total
    part = scal[B] % split
    out[...] = tot_scr[pl.ds(pl.multiple_of(part * rows, rows), rows), :].astype(BF)


def context_place_kernel(scal, pieces, out, *, split):
    rows = pieces.shape[1]
    for part in range(split):
        for t in range(2):
            first, second = ((2 * t + n) * split + part for n in range(2))
            for h in range(2):
                for kind in range(2):
                    start = h * LANES + kind * HEAD
                    value = jnp.concatenate(
                        [pieces[n, :, start : start + HEAD] for n in (first, second)], axis=1
                    )
                    column = (h + 2 * t) * LANES
                    out[part * rows : (part + 1) * rows, kind, column : column + LANES] = (
                        value.astype(F32)
                    )


def join_kernel(scal, own, *refs):
    pieces, out = refs[:8], refs[8]
    i, b = scal[I], scal[B]
    out[:, lanes_of(i)] = own[...]
    size = own.shape[0] // 8
    for core in range(2):
        for mask in range(4):
            source = b ^ (2 * mask + core)
            target = pl.ds(pl.multiple_of(source * size, size), size)
            out[target, lanes_of(1 - i)] = pieces[4 * core + mask][...]


def place_weight_kernel(scal, own, chunks, out, *, start, width):
    i = scal[I]
    rows = own.shape[0] // width
    size = own.shape[0] // chunks.shape[0]
    for n in range(width):
        out[:, lanes_of(i * width + n)] = own[n * rows : (n + 1) * rows]
    for source in range(chunks.shape[0]):
        n, first = divmod(source * size, rows)
        out[first : first + size, lanes_of((1 - i) * width + n)] = chunks[
            source, start : start + size
        ]


def attend_kernel(
    live, qd, kva, kvb, ctx, dqo, dkva, dkvb, dctx,
    kv_scr, kt_scr, vt_scr, s_scr, e_scr, acc_scr, *, chunk, unroll,
):
    step = pl.program_id(0)
    half_a, half_b, extra = kva.shape[0], kvb.shape[0], ctx.shape[0]
    keys = half_a + half_b
    total = keys + extra
    block = qd.shape[0]

    @pl.when(step == 0)
    def _():
        kv_scr[0:half_a, :] = kva[...]
        kv_scr[half_a:keys, :] = kvb[...]
        kv_scr[keys:total, :] = ctx[...]
        acc_scr[...] = jnp.zeros_like(acc_scr)

        def turn(rows):
            flipped = kv_scr[rows, :].astype(F32).T.astype(BF)
            kt_scr[:, rows] = flipped[:HEAD]
            vt_scr[0:HEAD, rows] = flipped[HEAD:]

        def turn_step(n, carry):
            turn(pl.ds(pl.multiple_of(n * 256, 256), 256))
            return carry

        lax.fori_loop(0, keys // 256, turn_step, 0)
        turn(slice(keys, total))
        vt_scr[HEAD:, :] = jnp.ones((16, total), BF)

    both = qd[...].astype(F32).T
    q_t = both[:HEAD].astype(BF)
    zero = jnp.zeros((HEAD, block), BF)
    q_side = jnp.concatenate([q_t, zero], axis=0)

    def score(rows, top, masked):
        s = dot(kv_scr[rows, :], q_side)
        if masked:
            index = lax.broadcasted_iota(jnp.int32, s.shape, 0)
            s = jnp.where(index < live[0], s, -1e30)
        s_scr[rows, :] = s
        return jnp.maximum(top, jnp.max(s.reshape(-1, 8, block), axis=0))

    def span(n):
        return pl.ds(pl.multiple_of(n * chunk, chunk), chunk)

    def over_keys(func, carry):
        return lax.fori_loop(
            0, keys // chunk, lambda n, c: func(span(n), c), carry, unroll=unroll
        )

    tail = pl.ds(keys, extra)
    top = score(tail, jnp.full((8, block), -1e30, F32), True)
    top = over_keys(lambda rows, c: score(rows, c, False), top)
    top = jnp.max(top, axis=0, keepdims=True)

    def weigh(rows, acc):
        e = jnp.exp(s_scr[rows, :] - top).astype(BF)
        e_scr[rows, :] = e
        return acc + dot(vt_scr[:, rows], e)

    out_t = weigh(tail, jnp.zeros((HEAD + 16, block), F32))
    out_t = over_keys(weigh, out_t)
    inv = 1.0 / out_t[HEAD : HEAD + 1]
    out_t = out_t[:HEAD] * inv
    d_t = both[HEAD:]
    delta = jnp.sum(d_t * out_t, axis=0, keepdims=True) * inv
    d_t = d_t * inv
    d_low = d_t.astype(BF)
    d_side = jnp.concatenate([zero, d_low], axis=0)

    def back(rows, acc):
        d_prob = dot(kv_scr[rows, :], d_side)
        e = e_scr[rows, :]
        d_score = (e.astype(F32) * (d_prob - delta)).astype(BF)
        acc_scr[0:HEAD, rows] += dot_t(q_t, d_score)
        acc_scr[HEAD:, rows] += dot_t(d_low, e)
        return acc + dot(kt_scr[:, rows], d_score)

    dq_t = back(tail, jnp.zeros((HEAD, block), F32))
    dq_t = over_keys(back, dq_t)
    dqo[...] = jnp.concatenate([dq_t, out_t], axis=0).T.astype(BF)

    @pl.when(step == pl.num_programs(0) - 1)
    def _():
        dkva[...] = acc_scr[:, 0:half_a].T
        dkvb[...] = acc_scr[:, half_a:keys].T.astype(BF)
        dctx[...] = acc_scr[:, keys:total].T


def attend(live, recv, kva, kvb, ctx, deps):
    queries = recv.shape[0]
    block = min(1024, queries)
    half_a, half_b, extra = recv.shape[0] if kva is recv else kva.shape[0], kvb.shape[0], ctx.shape[0]
    total = half_a + half_b + extra
    whole = lambda shape: pl.BlockSpec(shape, lambda n: (0, 0))
    kernel = functools.partial(attend_kernel, chunk=512, unroll=8)

    def inner(*refs):
        kernel(*refs[:5], *refs[5 + len(deps) :])

    return pl.pallas_call(
        inner,
        grid=(queries // block,),
        in_specs=[
            pl.BlockSpec(memory_space=pltpu.SMEM),
            pl.BlockSpec((block, LANES), lambda n: (n, 1)),
            whole((half_a, LANES)),
            whole((half_b, LANES)),
            whole((extra, LANES)),
        ]
        + [pl.BlockSpec(memory_space=pl.ANY)] * len(deps),
        out_specs=[
            pl.BlockSpec((block, LANES), lambda n: (n, 0)),
            whole((half_a, LANES)),
            whole((half_b, LANES)),
            whole((extra, LANES)),
        ],
        out_shape=[
            jax.ShapeDtypeStruct((queries, LANES), BF),
            jax.ShapeDtypeStruct((half_a, LANES), F32),
            jax.ShapeDtypeStruct((half_b, LANES), BF),
            jax.ShapeDtypeStruct((extra, LANES), F32),
        ],
        scratch_shapes=[
            pltpu.VMEM((total, LANES), BF),
            pltpu.VMEM((HEAD, total), BF),
            pltpu.VMEM((HEAD + 16, total), BF),
            pltpu.VMEM((total, block), F32),
            pltpu.VMEM((total, block), BF),
            pltpu.VMEM((LANES, total), F32),
        ],
        compiler_params=pltpu.CompilerParams(vmem_limit_bytes=VMEM_BYTES),
        cost_estimate=pl.CostEstimate(
            flops=int(38 * 1.15e9), bytes_accessed=1, transcendentals=0
        ),
    )(live, recv, kva, kvb, ctx, *deps)


def call(kernel, args, outs, scratch=(), deps=(), time=0.0):
    in_vmem = pl.BlockSpec(memory_space=pltpu.VMEM)
    in_smem = pl.BlockSpec(memory_space=pltpu.SMEM)
    anywhere = pl.BlockSpec(memory_space=pl.ANY)
    count = len(args)

    def inner(*refs):
        kernel(*refs[:count], *refs[count + len(deps) :])

    return pl.pallas_call(
        inner,
        in_specs=[in_smem] + [in_vmem] * (count - 1) + [anywhere] * len(deps),
        out_specs=[in_vmem] * len(outs),
        out_shape=[jax.ShapeDtypeStruct(s, d) for s, d in outs],
        scratch_shapes=[pltpu.VMEM(s, d) for s, d in scratch],
        compiler_params=pltpu.CompilerParams(vmem_limit_bytes=VMEM_BYTES),
        cost_estimate=pl.CostEstimate(
            flops=1 + int(time * 1.15e9), bytes_accessed=1, transcendentals=0
        ),
    )(*args, *deps)


def after(values, *deps):
    anywhere = pl.BlockSpec(memory_space=pl.ANY)
    count = len(values)

    def inner(*refs):
        pass

    return pl.pallas_call(
        inner,
        in_specs=[anywhere] * (count + len(deps)),
        out_specs=[anywhere] * count,
        out_shape=[jax.ShapeDtypeStruct(v.shape, v.dtype) for v in values],
        input_output_aliases={n: n for n in range(count)},
        cost_estimate=pl.CostEstimate(flops=1, bytes_accessed=1, transcendentals=0),
    )(*values, *deps)


def embed_features(timesteps, image_embed):
    half_width = image_embed.shape[1] // 2
    freqs = jnp.exp(-math.log(10000.0) * jnp.arange(half_width, dtype=F32) / half_width)
    angles = timesteps.astype(F32)[:, None] * freqs[None, :]
    return jax.nn.silu(jnp.concatenate([jnp.cos(angles), jnp.sin(angles)], axis=1) + image_embed)


def body(
    block_input,
    cotangent,
    image_embed,
    timesteps,
    text_len,
    context,
    conv1_weight,
    conv2_weight,
    embed_weight,
    embed_bias,
    norm1_gain,
    norm1_bias,
    norm2_gain,
    norm2_bias,
    norm3_gain,
    norm3_bias,
    qkv_weight,
    out_weight,
    ctx_weight,
):
    images, row_count, col_count, width = block_input.shape
    channels = qkv_weight.shape[0]
    size = channels // GROUPS
    blocks = lax.axis_size("blk")
    pix = row_count * col_count
    cells = float(pix * blocks * size)
    split = blocks // 4
    ctx_len = context.shape[1]
    b = lax.axis_index("blk")
    z = lax.axis_index("ch")
    h, i = z % 2, z // 2
    row, rows_all = b * row_count, blocks * row_count
    inside = [row >= 1, row + row_count < rows_all, row >= 2, row + row_count + 1 < rows_all]
    scal = jnp.stack([h, i] + [flag.astype(jnp.int32) for flag in inside] + [z, b]).astype(jnp.int32)


    def over_ch(value, mask):
        return lax.ppermute(value, "ch", [(n, n ^ mask) for n in range(4)])

    def over_blk(value, mask):
        return lax.ppermute(value, "blk", [(n, n ^ mask) for n in range(blocks)])

    def ring(value, step):
        return lax.ppermute(value, "blk", [(n, (n + step) % blocks) for n in range(blocks)])

    def halo(first, last):
        if row_count >= 2:
            return ring(last, 1), ring(first, -1)
        return (
            jnp.concatenate([ring(last, 2), ring(last, 1)], axis=0),
            jnp.concatenate([ring(first, -1), ring(first, -2)], axis=0),
        )

    pairs = [[n * 4 + 2 * m + k for n in range(blocks) for k in range(2)] for m in range(2)]

    def to_image(value):
        return lax.all_to_all(value, ("blk", "ch"), 0, 0, axis_index_groups=pairs)

    def by_image(first, second):
        return jnp.where(i == 0, first, second), jnp.where(i == 0, second, first)

    def plane(value):
        mine = [value] + [over_blk(value, 2 * mask) for mask in (1, 2, 3)]
        return mine + [over_blk(piece, 1) for piece in mine]

    w1_own = conv1_weight.reshape(-1, width)
    w2_own = conv2_weight.reshape(-1, width)
    heads = lambda v: v.reshape(channels, 2, HEAD)
    wp_own = jnp.stack(
        [
            jnp.concatenate([heads(qkv_weight[:, 1]), heads(qkv_weight[:, 2])], axis=2),
            jnp.concatenate([heads(qkv_weight[:, 0] * 0.125), heads(out_weight.T)], axis=2),
        ],
        axis=0,
    )
    wp_own = jnp.transpose(wp_own, (2, 0, 1, 3)).reshape(-1, LANES)
    w1_rows, w2_rows, wp_rows = (w.shape[0] // blocks for w in (w1_own, w2_own, wp_own))
    chunk_of = lambda w: lax.dynamic_slice_in_dim(w, b * (w.shape[0] // blocks), w.shape[0] // blocks, 0)
    w1_slice = chunk_of(w1_own)

    emb_act = embed_features(timesteps, image_embed).astype(BF)
    scale_shift = (
        jnp.einsum("ie,esc->isc", emb_act, embed_weight, preferred_element_type=F32) + embed_bias
    )
    local_vec = jnp.concatenate(
        [
            jnp.zeros((2, width), F32),
            jnp.stack([norm1_gain, norm1_bias, norm2_gain, norm2_bias, norm3_gain, norm3_bias]),
            scale_shift.reshape(4, width),
            jnp.zeros((4, width), F32),
        ],
        axis=0,
    )
    x_mine, x_theirs = call(
        image_split_kernel,
        [scal, block_input.reshape(images, pix, width)],
        [((pix, width), BF)] * 2,
        deps=[w1_slice],
    )
    w1_chunk = over_ch(w1_slice, 2)
    x_two, x_one = over_ch(x_theirs, 2), over_ch(x_mine, 1)
    x_three = over_ch(x_two, 1)
    if blocks == 8:
        w1_pieces = plane(w1_chunk)
    else:
        w1_pieces = [lax.all_gather(w1_chunk, "blk", axis=0, tiled=True)]
    x_sums = call(
        functools.partial(input_sums_kernel, blocks=blocks),
        [scal, block_input.reshape(images, pix, width), local_vec],
        [((4 * blocks, 16, width), F32)],
        deps=[x_mine],
    )[0]
    sums1 = lax.all_to_all(x_sums, ("blk", "ch"), 0, 0)
    two_source = jnp.concatenate([chunk_of(w2_own), chunk_of(wp_own)], axis=0)
    (two_source,) = after((two_source,), x_two, x_one, x_sums)
    two_chunk = over_ch(two_source, 2)
    (two_chunk,) = after((two_chunk,), x_three, *w1_pieces[1:4])
    wide = dict(axis=1)
    x_own = jnp.concatenate(by_image(x_mine, x_two), **wide)
    x_oth = jnp.concatenate(by_image(x_one, x_three), **wide)
    edge = min(2 * COLS, pix)
    x_top, x_bot = halo(
        jnp.concatenate([x_own[:edge], x_oth[:edge]], **wide),
        jnp.concatenate([x_own[pix - edge :], x_oth[pix - edge :]], **wide),
    )
    if blocks == 8:
        w1 = call(join_kernel, [scal, w1_own] + w1_pieces, [((w1_own.shape[0], HALF), BF)])[0]
    else:
        w1_oth = w1_pieces[0]
        w1 = jnp.concatenate(by_image(w1_own, w1_oth), **wide)
    two = lax.all_gather(two_chunk, "blk", axis=0)
    w2 = call(
        functools.partial(place_weight_kernel, start=0, width=1),
        [scal, w2_own, two],
        [((w2_own.shape[0], HALF), BF)],
    )[0]
    j = b // split
    ctx_rows = -(-ctx_len // 16) * 16
    ctx_w = jnp.stack(
        [
            lax.dynamic_slice_in_dim(
                ctx_weight, 128 * (hh + 2 * (j // 2)) + HEAD * (j % 2), HEAD, 2
            ).reshape(-1, 2 * HEAD)
            for hh in range(2)
        ]
    )
    ctx_term = jnp.einsum("itx,hxk->ihtk", context, ctx_w, preferred_element_type=F32)
    ctx_term = jnp.pad(
        ctx_term.astype(BF).reshape(4, ctx_len, 2 * HEAD),
        ((0, 0), (0, ctx_rows - ctx_len), (0, 0)),
    )
    ctx_kv = lax.psum_scatter(ctx_term, "ch", scatter_dimension=0)
    live = (CLIPTOK + jnp.where(i == 0, text_len[0], text_len[1])).astype(jnp.int32)[None]

    emb_f = jnp.repeat(emb_act.astype(F32), 2, axis=1)
    odd = (jnp.arange(emb_f.shape[1]) % 2)[None]
    emb_rows = jnp.concatenate(
        [emb_f * (1 - odd), emb_f * odd, jnp.zeros((4, emb_f.shape[1]), F32)], axis=0
    )
    kind = dict(cells=cells, size=size)
    ext = pix + 2 * COLS
    stat_shape = ((2 * blocks, 8, HALF), F32)

    c_mine, c_theirs = call(
        image_split_kernel,
        [scal, cotangent.reshape(images, pix, width)],
        [((pix, width), BF)] * 2,
        deps=[x_sums],
    )

    hid_own, hid_stat, act1, vec = call(
        functools.partial(conv1_kernel, **kind),
        [scal, x_own, x_oth, x_top, x_bot, sums1, w1],
        [((ext, HALF), BF), stat_shape, ((pix, channels), BF), ((4, 16, LANES), F32)],
        [((ext + 2 * COLS, channels), BF)],
        deps=[ctx_term, c_mine, emb_rows, live],
    )
    hid_oth = over_ch(hid_own, 1)
    sums2 = to_image(hid_stat)

    c_mine, c_theirs = after((c_mine, c_theirs), hid_oth, w2)
    c_one, c_two = over_ch(c_mine, 1), over_ch(c_theirs, 2)
    c_three = over_ch(c_two, 1)
    cot_own = jnp.concatenate(by_image(c_mine, c_two), **wide)
    cot_oth = jnp.concatenate(by_image(c_one, c_three), **wide)

    edges = ((2, edge, HALF), BF)
    res_f, res_own, res_stat, act_first, act_rest, res_edges = call(
        functools.partial(conv2_kernel, **kind),
        [scal, hid_own, hid_oth, sums2, vec, w2, x_own, act1],
        [
            ((pix, HALF), F32),
            ((pix, HALF), BF),
            stat_shape,
            ((pix // 2, channels), BF),
            ((pix + pix // 2, channels), BF),
            edges,
        ],
        [((ext, channels), BF)],
    )
    res_oth = over_ch(res_own, 1)
    sums3 = to_image(res_stat)
    wp = call(
        functools.partial(place_weight_kernel, start=w2_rows, width=4),
        [scal, wp_own, two],
        [((channels, 4 * HALF), BF)],
        deps=[res_oth],
    )[0]
    packed, act3, cot_all, cot_edges = call(
        functools.partial(qkv_kernel, **kind),
        [scal, res_own, res_oth, sums3, vec, cot_own, cot_oth, wp],
        [((4, pix, HALF), BF), ((pix, channels), BF), ((pix, channels), BF), edges],
        deps=[ctx_kv],
    )
    recv = lax.all_to_all(packed.reshape(blocks, pix // split, HALF), "blk", 0, 0)
    res_edges, act_first = after((res_edges, act_first), packed)
    res_top, res_bot = halo(res_edges[0], res_edges[1])
    cot_top, cot_bot = halo(cot_edges[0], cot_edges[1])
    first_there = over_ch(act_first, 2)
    (recv,) = after((recv,), res_top, res_bot, cot_top, cot_bot, first_there)
    recv = recv.reshape(-1, HALF)
    rest_there = over_ch(act_rest, 2)
    if split == 2:
        kva, kvb = recv, over_blk(recv[:, :LANES], 1)
    else:
        groups = [[n * split + m for m in range(split)] for n in range(4)]
        kv_all = lax.all_gather(
            recv[:, :LANES], "blk", axis=0, tiled=True, axis_index_groups=groups
        )
        kva, kvb = kv_all[: kv_all.shape[0] // 2], kv_all[kv_all.shape[0] // 2 :]
    dqo, dkva, dkvb, dctx = attend(live, recv, kva, kvb, ctx_kv, [])
    if split == 2:
        d_ctx = dctx + over_blk(dctx, 1)
        back = call(
            merge_kernel,
            [scal, dkva, over_blk(dkvb, 1), dqo],
            [((dqo.shape[0], HALF), BF)],
            deps=[rest_there],
        )[0]
    else:
        d_ctx = lax.psum(dctx, "blk", axis_index_groups=groups)
        d_kv = lax.psum_scatter(
            jnp.concatenate([dkva, dkvb.astype(F32)], axis=0),
            "blk",
            scatter_dimension=0,
            axis_index_groups=groups,
            tiled=True,
        )
        back = jnp.concatenate([d_kv.astype(BF), dqo], axis=1)
    grads = lax.all_to_all(back.reshape(blocks, pix // split, HALF), "blk", 0, 0)
    grads = grads.reshape(4, pix, HALF)

    features = context.shape[2] // split
    d_ctx = d_ctx[:ctx_len].astype(BF)
    ctx_part = call(
        functools.partial(context_grad_kernel, split=split),
        [scal, context, d_ctx] + [over_ch(d_ctx, mask) for mask in (1, 2, 3)],
        [((features, HALF), BF)],
        [((context.shape[2], HALF), F32)],
    )[0]
    ctx_all = lax.all_gather(ctx_part, "blk", axis=0)

    def low_grad(rows):
        return [((rows, HALF), F32), ((rows, HALF), BF), stat_shape]

    p3_own, p3_oth, st3 = call(
        functools.partial(qkv_back_kernel, **kind),
        [scal, grads, wp, res_own, res_oth, sums3, vec],
        low_grad(pix),
        [((pix, channels), F32)],
        deps=[ctx_part],
    )
    r3 = over_ch(p3_oth, 1)
    stats3 = to_image(st3)
    proj_own, proj_oth, wp_part = call(
        out_kernel,
        [scal, grads, wp, act3, cot_all],
        [((pix, HALF), F32), ((pix, HALF), BF), ((2, 4 * channels, LANES), BF)],
        [((pix, channels), F32)],
        deps=[r3],
    )
    first3 = (p3_own[:edge] + r3[:edge].astype(F32)).astype(BF)
    last3 = (p3_own[pix - edge :] + r3[pix - edge :].astype(F32)).astype(BF)
    d_top3, d_bot3 = halo(first3, last3)
    d_resid, ext2, away2 = call(
        functools.partial(norm3_back_kernel, **kind),
        [
            scal, p3_own, r3, d_top3, d_bot3, res_own, res_top, res_bot, cot_own, cot_top, cot_bot,
            sums3, stats3, vec,
        ],
        [((pix, HALF), F32), ((ext + 2 * COLS, HALF), BF), ((ext, LANES), BF)],
        deps=[proj_own],
    )
    there2 = over_ch(away2, 2)
    p2_own, p2_oth, st2 = call(
        functools.partial(conv_back_kernel, which=1, **kind),
        [scal, ext2, w2, hid_own, hid_oth, sums2, vec],
        low_grad(ext),
        [((ext, channels), F32)],
        time=8.0,
    )
    r2 = over_ch(p2_oth, 1)
    (st2,) = after((st2,), there2)
    stats2 = to_image(st2)
    conv_rows, wp_rows = 9 * channels // blocks, 4 * channels // blocks
    part2 = call(
        weight_grad_two_kernel,
        [scal, act_rest, rest_there, ext2, there2, wp_part],
        [((blocks, conv_rows + 2 * wp_rows, LANES), BF)],
        [((2 * pix, 9 * LANES), BF), ((9 * channels, LANES), F32)],
        deps=[r2],
    )[0]
    ext1, away1 = call(
        functools.partial(norm2_back_kernel, **kind),
        [scal, p2_own, r2, hid_own, sums2, stats2, vec],
        [((ext, HALF), BF), ((ext, LANES), BF)],
        deps=[part2, ctx_all],
    )
    parts2 = lax.all_to_all(part2, "blk", 0, 0)
    there1 = over_ch(away1, 2)
    p1_own, p1_oth, st1 = call(
        functools.partial(conv_back_kernel, which=0, **kind),
        [scal, ext1, w1, x_own, x_oth, sums1, vec],
        low_grad(pix),
        [((pix, channels), F32)],
        time=8.0,
    )
    (st1,) = after((st1,), there1, parts2)
    (proj_late,) = after((proj_oth,), there1)
    r1 = over_ch(p1_oth, 1)
    stats1 = to_image(st1)
    half_shape = (4, 9 * channels // 8, LANES)
    keep1, send1 = call(
        weight_grad_one_kernel,
        [scal, act_first, act_rest, first_there, rest_there, ext1, there1],
        [(half_shape, F32), (half_shape, BF)],
        [((2 * pix, 9 * LANES), BF), ((9 * channels, LANES), F32)],
        deps=[p1_own],
        time=20.0,
    )
    if blocks == 8:
        own1, *sends = call(
            scatter_kernel,
            [scal, keep1, over_blk(send1, 1)],
            [((conv_rows, LANES), F32)] + [((conv_rows, LANES), BF)] * 3,
        )
    else:
        own1 = keep1
    if blocks == 8:
        other = call(other_sum_kernel, [scal, parts2], [((wp_rows, LANES), BF)], deps=[own1])[0]
        total = call(
            total_kernel,
            [scal, own1, parts2, over_ch(other, 2)]
            + [over_blk(v, 2 * n + 2) for n, v in enumerate(sends)],
            [((2 * conv_rows + wp_rows, LANES), BF)],
        )[0]
    else:
        total = own1
    out_keep, out_send = call(
        out_add_kernel,
        [scal, res_f, proj_own, over_ch(proj_late, 1)],
        [((pix, width), BF)] * 2,
        deps=[total],
    )
    in_keep, in_send = call(
        functools.partial(last_kernel, **kind),
        [scal, p1_own, r1, x_own, sums1, stats1, vec, d_resid],
        [((pix, width), F32), ((pix, width), BF)],
        [((pix, HALF), F32)],
        deps=[total],
        time=40.0,
    )
    sums_here, sums_away = call(
        channel_sums_kernel,
        [scal, stats1, stats2, stats3],
        [((8, LANES), F32)] * 2,
        deps=[total],
    )
    sums_recv = over_ch(sums_away, 2)
    out_recv, in_recv = over_ch(out_send, 2), over_ch(in_send, 2)
    bias_grad, *smalls, embed_weight_grad = call(
        channel_grads_kernel,
        [scal, sums_here, sums_recv, local_vec, emb_rows],
        [((2, LANES), F32)] + [((1, LANES), F32)] * 6 + [((emb_rows.shape[1], LANES), F32)],
        deps=[total],
        time=15.0,
    )
    block_output, input_grad = call(
        by_images_kernel,
        [scal, out_keep, out_recv, in_keep, in_recv],
        [((images, pix, width), BF), ((images, pix, width), F32)],
        deps=[total],
        time=10.0,
    )
    if blocks == 8:
        ctx_grad = call(
            functools.partial(context_place_kernel, split=split),
            [scal, ctx_all],
            [((context.shape[2], 2, channels), F32)],
            deps=[total],
            time=10.0,
        )[0]
        grad1, grad2, qkv_grad, out_grad = call(
            place_kernel,
            [scal] + plane(total),
            [((9 * channels, LANES), F32)] * 2
            + [((3 * channels, LANES), F32), ((LANES, channels), F32)],
            deps=[block_output, ctx_grad, bias_grad],
        )
    else:
        ctx_grad = ctx_all.reshape(2, 2, split, features, 2, 2, HEAD)
        ctx_grad = jnp.transpose(ctx_grad, (2, 3, 5, 0, 4, 1, 6)).astype(F32)
        flip = lambda c: jnp.where(b % 2 == 0, *((keep1.astype(BF), send1)[:: 1 - 2 * c]))
        grad1 = lax.psum(jnp.concatenate([flip(0), flip(1)], axis=0), "blk").astype(F32)
        sums = lax.psum(part2, "blk").astype(F32)
        cut = conv_rows + wp_rows
        grad2 = sums[:, :conv_rows]
        wp_grad = sums[:, conv_rows:cut] + over_ch(sums[:, cut:].astype(BF), 2).astype(F32)
        wp_grad = wp_grad.reshape(-1, LANES)
        qkv_grad, out_grad = wp_grad[: 3 * channels], wp_grad[3 * channels :]
        out_grad = jnp.concatenate(list(out_grad.reshape(-1, LANES, LANES)), axis=1)
    qkv_grad = jnp.transpose(qkv_grad.reshape(3, channels, LANES), (1, 0, 2))

    return (
        block_output.reshape(block_input.shape),
        input_grad.reshape(block_input.shape),
        grad1.reshape(conv1_weight.shape),
        grad2.reshape(conv2_weight.shape),
        embed_weight_grad.reshape(embed_weight.shape),
        bias_grad,
        *(value.reshape(width) for value in smalls),
        qkv_grad,
        out_grad,
        ctx_grad.reshape(ctx_weight.shape),
    )


def solution(mesh):
    return jax.shard_map(
        body,
        mesh=mesh,
        in_specs=(
            P(None, "blk", None, "ch"),
            P(None, "blk", None, "ch"),
            P(),
            P(),
            P(),
            P(None, None, "ch"),
            P(None, None, None, "ch"),
            P(None, None, None, "ch"),
            P(None, None, "ch"),
            P(None, "ch"),
            P("ch"),
            P("ch"),
            P("ch"),
            P("ch"),
            P("ch"),
            P("ch"),
            P(None, None, "ch"),
            P("ch", None),
            P("ch", None, None),
        ),
        out_specs=(
            P(None, "blk", None, "ch"),
            P(None, "blk", None, "ch"),
            P(None, None, None, "ch"),
            P(None, None, None, "ch"),
            P(None, None, "ch"),
            P(None, "ch"),
            P("ch"),
            P("ch"),
            P("ch"),
            P("ch"),
            P("ch"),
            P("ch"),
            P(None, None, "ch"),
            P("ch", None),
            P("ch", None, None),
        ),
        check_vma=False,
    )
```

```python
import functools
import math

import jax
import jax.numpy as jnp
from jax import lax
from jax.experimental import pallas as pl
from jax.experimental.pallas import tpu as pltpu
from jax.sharding import PartitionSpec as P

HEAD = 64
GROUPS = 32
CLIPTOK = 4
LANES = 128
HALF = 256
COLS = 64
VMEM_BYTES = 56 * 2**20
BF = jnp.bfloat16
F32 = jnp.float32

H, I, UP1, DOWN1, UP2, DOWN2, Z, B = range(8)


def dot(a, b):
    return jnp.dot(a, b, preferred_element_type=F32)


def dot_t(a, b):
    return lax.dot_general(a, b, (((1,), (1,)), ((), ())), preferred_element_type=F32)


def group_sum(vec, size):
    lane = lax.broadcasted_iota(jnp.int32, vec.shape, 1)
    step = 1
    while step < size:
        low = pltpu.roll(vec, step, 1)
        high = pltpu.roll(vec, LANES - step, 1)
        vec = vec + jnp.where((lane & step) != 0, low, high)
        step *= 2
    return vec


def shards(scal):
    h = scal[H]
    return (h, h + 2, 1 - h, 3 - h)


def lanes_of(shard):
    return pl.ds(pl.multiple_of(shard * LANES, LANES), LANES)


def part_of(quarter):
    return slice((quarter % 2) * LANES, (quarter % 2 + 1) * LANES)


def norm_stats(scal, sums, quarter, cells, size):
    wide = sums.shape[2] == HALF
    kinds = 2 if wide else 4
    shard = shards(scal)[quarter]
    total = None
    for source in range(sums.shape[0] // kinds):
        row = source * kinds + (shard % 2 if wide else shard)
        piece = sums[pl.ds(row, 1)][0]
        total = piece if total is None else total + piece
    if wide:
        total = total[:, part_of(quarter)]
    total = group_sum(total, size)
    mean = total[0:1] / cells
    inv = lax.rsqrt(total[1:2] / cells - mean * mean + 1e-05)
    return mean, inv


def affine_of(scal, vec, quarter, which, mean, inv):
    row = vec[pl.ds(shards(scal)[quarter], 1)][0]
    gain = row[2 * which + 2 : 2 * which + 3]
    bias = row[2 * which + 3 : 2 * which + 4]
    if which == 1:
        first = scal[I] == 0
        grow = 1.0 + jnp.where(first, row[8:9], row[10:11])
        gain, bias = gain * grow, bias * grow + jnp.where(first, row[9:10], row[11:12])
    slope = inv * gain
    return gain, slope, bias - mean * slope


def column_sums(first, second):
    rows = jnp.concatenate(
        [jnp.sum(first, axis=0, keepdims=True), jnp.sum(second, axis=0, keepdims=True)], axis=0
    )
    return jnp.concatenate([rows, jnp.zeros((6, rows.shape[1]), F32)], axis=0)


def shift_columns(total, left, right):
    col = lax.broadcasted_iota(jnp.int32, total.shape, 0) % COLS
    rows = total.shape[0]
    total = total + jnp.where(col > 0, pltpu.roll(left, 1, 0), 0.0)
    return total + jnp.where(col < COLS - 1, pltpu.roll(right, rows - 1, 0), 0.0)


def silu_slope(field):
    sigma = jax.nn.sigmoid(field)
    return sigma * (1.0 + field * (1.0 - sigma))


def masked_rows(scal, value, flag):
    return jnp.where(scal[flag] > 0, value, 0.0)


def input_sums_kernel(scal, field, vec, out, *, blocks):
    for image in range(2):
        value = field[image].astype(F32)
        sums = column_sums(value, value * value)[:2]
        sums = jnp.concatenate([sums, vec[2:]], axis=0)
        for target in range(blocks):
            out[4 * target + 2 * image] = sums
            out[4 * target + 2 * image + 1] = sums


def image_split_kernel(scal, field, mine, theirs):
    mine[...] = field[pl.ds(scal[I], 1)][0]
    theirs[...] = field[pl.ds(1 - scal[I], 1)][0]


def spread(out, sums):
    for target in range(out.shape[0]):
        out[target] = sums


def conv1_kernel(scal, own, oth, top, bot, sums, weight, out, out_sums, act_out, vec, act_scr, *, cells, size):
    pix = own.shape[0]
    vec[...] = sums[0:4]
    rows = pix + 2 * COLS
    for quarter in range(4):
        shard = shards(scal)[quarter]
        mean, inv = norm_stats(scal, sums, quarter, cells, size)
        gain, slope, offset = affine_of(scal, vec, quarter, 0, mean, inv)
        lanes = slice(quarter * LANES, (quarter + 1) * LANES)

        def active(field):
            pre = field.astype(F32) * slope + offset
            return pre * jax.nn.sigmoid(pre)

        half = own if quarter < 2 else oth
        main = active(half[:, part_of(quarter)]).astype(BF)
        above, below = active(top[:, lanes]), active(bot[:, lanes])
        act_scr[2 * COLS : 2 * COLS + pix, lanes_of(shard)] = main
        act_out[:, lanes_of(shard)] = main
        act_scr[0:COLS, lanes_of(shard)] = masked_rows(scal, above[:COLS], UP2).astype(BF)
        act_scr[COLS : 2 * COLS, lanes_of(shard)] = masked_rows(scal, above[COLS:], UP1).astype(BF)
        end = 2 * COLS + pix
        act_scr[end : end + COLS, lanes_of(shard)] = masked_rows(scal, below[:COLS], DOWN1).astype(BF)
        act_scr[end + COLS :, lanes_of(shard)] = masked_rows(scal, below[COLS:], DOWN2).astype(BF)
    result = convolve(act_scr, weight, rows)
    out[...] = result.astype(BF)
    inner = result[COLS : COLS + pix]
    spread(out_sums, column_sums(inner, inner * inner))


def convolve(act_scr, weight, rows):
    channels = act_scr.shape[1]
    parts = []
    for kx in range(3):
        acc = None
        for ky in range(3):
            tap = (ky * 3 + kx) * channels
            term = dot(act_scr[ky * COLS : ky * COLS + rows, :], weight[tap : tap + channels, :])
            acc = term if acc is None else acc + term
        parts.append(acc)
    return shift_columns(parts[1], parts[0], parts[2])


def conv2_kernel(scal, own, oth, sums, vec, weight, base, act_below, out_f, out_low, out_sums, act_first, act_out, edges, act_scr, *, cells, size):
    pix = base.shape[0]
    cut = act_first.shape[0]
    act_first[...] = act_below[0:cut]
    act_out[0 : pix - cut, :] = act_below[cut:]
    for quarter in range(4):
        shard = shards(scal)[quarter]
        mean, inv = norm_stats(scal, sums, quarter, cells, size)
        gain, slope, offset = affine_of(scal, vec, quarter, 1, mean, inv)
        half = own if quarter < 2 else oth
        pre = half[:, part_of(quarter)].astype(F32) * slope + offset
        act = pre * jax.nn.sigmoid(pre)
        main = act[COLS : COLS + pix].astype(BF)
        act_scr[COLS : COLS + pix, lanes_of(shard)] = main
        act_out[pix - cut :, lanes_of(shard)] = main
        act_scr[0:COLS, lanes_of(shard)] = masked_rows(scal, act[:COLS], UP1).astype(BF)
        act_scr[COLS + pix :, lanes_of(shard)] = masked_rows(scal, act[COLS + pix :], DOWN1).astype(BF)
    result = convolve(act_scr, weight, pix) + base[...].astype(F32)
    out_f[...] = result
    low = result.astype(BF)
    out_low[...] = low
    if edges.shape[1] < pix:
        edges[0], edges[1] = low[: edges.shape[1]], low[pix - edges.shape[1] :]
    else:
        edges[0], edges[1] = low, low
    spread(out_sums, column_sums(result, result * result))


def qkv_kernel(scal, own, oth, sums, vec, cot_own, cot_oth, weight, out, act_out, cot_out, edges, *, cells, size):
    rows = edges.shape[1]
    edges[0], edges[1] = cot_own[0:rows], cot_own[cot_own.shape[0] - rows :]
    for quarter in range(4):
        shard = shards(scal)[quarter]
        mean, inv = norm_stats(scal, sums, quarter, cells, size)
        gain, slope, offset = affine_of(scal, vec, quarter, 2, mean, inv)
        half = own if quarter < 2 else oth
        cot = cot_own if quarter < 2 else cot_oth
        field = half[:, part_of(quarter)].astype(F32)
        act_out[:, lanes_of(shard)] = (field * slope + offset).astype(BF)
        cot_out[:, lanes_of(shard)] = cot[:, part_of(quarter)]
    for head in range(4):
        columns = weight[:, head * HALF : (head + 1) * HALF]
        fwd = dot(act_out[...], columns)
        back = dot(cot_out[...], columns[:, LANES:])
        out[head, :, :LANES] = fwd[:, :LANES].astype(BF)
        lane = lax.broadcasted_iota(jnp.int32, back.shape, 1)
        out[head, :, LANES:] = jnp.where(lane < HEAD, fwd[:, LANES:], back).astype(BF)


def below_stats(scal, total, own, oth, sums, vec, out_own, out_oth, out_stats, which, cells, size):
    rows = total.shape[0]
    pix = rows - 2 * COLS if which == 1 else rows
    inner = slice(COLS, COLS + pix) if which == 1 else slice(0, pix)
    for quarter in range(4):
        shard = shards(scal)[quarter]
        mean, inv = norm_stats(scal, sums, quarter, cells, size)
        gain, slope, offset = affine_of(scal, vec, quarter, which, mean, inv)
        half = own if quarter < 2 else oth
        part = part_of(quarter)
        if quarter < 2:
            out_own[:, part] = total[:, lanes_of(shard)]
        else:
            out_oth[:, part] = total[:, lanes_of(shard)].astype(BF)
        grad = total[inner, lanes_of(shard)]
        field = half[inner, part].astype(F32)
        if which < 2:
            grad = grad * silu_slope(field * slope + offset)
        result = column_sums(grad, grad * ((field - mean) * inv))
        slot = scal[H] if quarter < 2 else 1 - scal[H]
        for target in range(out_stats.shape[0] // 2):
            out_stats[pl.ds(2 * target + slot, 1), :, part] = result[None]


def qkv_back_kernel(scal, grads, weight, own, oth, sums, vec, out_own, out_oth, out_stats, tot_scr, *, cells, size):
    total = None
    for head in range(4):
        columns = weight[:, head * HALF : (head + 1) * HALF]
        grad = grads[head]
        lane = lax.broadcasted_iota(jnp.int32, grad.shape, 1)
        term = dot_t(jnp.where(lane < 3 * HEAD, grad, jnp.zeros_like(grad)), columns)
        total = term if total is None else total + term
    tot_scr[...] = total
    below_stats(scal, tot_scr, own, oth, sums, vec, out_own, out_oth, out_stats, 2, cells, size)


def out_kernel(scal, grads, weight, act, cot, proj_own, proj_oth, wgrad, tot_scr):
    channels = act.shape[1]
    act_t = act[...].astype(F32).T.astype(BF)
    total = None
    for pair in range(2):
        slot = jnp.where(scal[I] == pair, 0, 1)
        parts, outs = [], []
        for head in (2 * pair, 2 * pair + 1):
            columns = weight[:, head * HALF + LANES : (head + 1) * HALF]
            grad = grads[head]
            low = grad[:, LANES:]
            lane = lax.broadcasted_iota(jnp.int32, low.shape, 1)
            term = dot_t(jnp.where(lane < HEAD, jnp.zeros_like(low), low), columns)
            total = term if total is None else total + term
            parts.append(dot(act_t, grad))
            outs.append(dot(low.astype(F32).T[HEAD:].astype(BF), cot[...]))
        first, second = parts
        pieces = [
            jnp.concatenate([first[:, LANES : LANES + HEAD], second[:, LANES : LANES + HEAD]], axis=1)
            * 0.125,
            jnp.concatenate([first[:, :HEAD], second[:, :HEAD]], axis=1),
            jnp.concatenate([first[:, HEAD:LANES], second[:, HEAD:LANES]], axis=1),
        ]
        both = jnp.concatenate(outs, axis=0)
        pieces += [both[:, n * LANES : (n + 1) * LANES] for n in range(channels // LANES)]
        wgrad[pl.ds(slot, 1)] = jnp.concatenate(pieces, axis=0).astype(BF)[None]
    tot_scr[...] = total
    for quarter, shard in enumerate(shards(scal)):
        if quarter < 2:
            proj_own[:, part_of(quarter)] = tot_scr[:, lanes_of(shard)]
        else:
            proj_oth[:, part_of(quarter)] = tot_scr[:, lanes_of(shard)].astype(BF)


def total_stats(stats):
    total = stats[0]
    for source in range(1, stats.shape[0]):
        total = total + stats[source]
    return total


def norm_back(scal, quarter, sums, stats, vec, which, cells, size):
    mean, inv = norm_stats(scal, sums, quarter, cells, size)
    gain, slope, offset = affine_of(scal, vec, quarter, which, mean, inv)
    means = group_sum(total_stats(stats)[:, part_of(quarter)] * gain, size) / cells

    def back(grad, field):
        field = field.astype(F32)
        hat = (field - mean) * inv
        if which < 2:
            grad = grad * silu_slope(field * slope + offset)
        return (grad * gain - means[0:1] - hat * means[1:2]) * inv

    return back


def norm3_back_kernel(
    scal, part, recv, dtop, dbot, field, ftop, fbot, cot, ctop, cbot, sums, stats, vec, out_f, ext, away, *, cells, size
):
    pix = part.shape[0]
    end = 2 * COLS + pix
    for quarter in range(2):
        lanes = part_of(quarter)
        back = norm_back(scal, quarter, sums, stats, vec, 2, cells, size)
        main = back(part[:, lanes] + recv[:, lanes].astype(F32), field[:, lanes])
        main = main + cot[:, lanes].astype(F32)
        out_f[:, lanes] = main
        ext[2 * COLS : end, lanes] = main.astype(BF)
        head = back(dtop[:, lanes].astype(F32), ftop[:, lanes]) + ctop[:, lanes].astype(F32)
        tail = back(dbot[:, lanes].astype(F32), fbot[:, lanes]) + cbot[:, lanes].astype(F32)
        ext[0:COLS, lanes] = masked_rows(scal, head[:COLS], UP2).astype(BF)
        ext[COLS : 2 * COLS, lanes] = masked_rows(scal, head[COLS:], UP1).astype(BF)
        ext[end : end + COLS, lanes] = masked_rows(scal, tail[:COLS], DOWN1).astype(BF)
        ext[end + COLS :, lanes] = masked_rows(scal, tail[COLS:], DOWN2).astype(BF)
    away[...] = ext[COLS : end + COLS, lanes_of(1 - scal[I])]


def norm2_back_kernel(scal, part, recv, field, sums, stats, vec, ext, away, *, cells, size):
    rows = part.shape[0]
    for quarter in range(2):
        lanes = part_of(quarter)
        back = norm_back(scal, quarter, sums, stats, vec, 1, cells, size)
        main = back(part[:, lanes] + recv[:, lanes].astype(F32), field[:, lanes])
        ext[0:COLS, lanes] = masked_rows(scal, main[:COLS], UP1).astype(BF)
        ext[COLS : rows - COLS, lanes] = main[COLS : rows - COLS].astype(BF)
        ext[rows - COLS :, lanes] = masked_rows(scal, main[rows - COLS :], DOWN1).astype(BF)
    away[...] = ext[:, lanes_of(1 - scal[I])]


def conv_back_kernel(scal, ext, weight, own, oth, sums, vec, out_own, out_oth, out_stats, tot_scr, *, which, cells, size):
    rows, channels = tot_scr.shape
    parts = []
    for kx in range(3):
        acc = None
        for ky in range(3):
            tap = (ky * 3 + kx) * channels
            start = (2 - ky) * COLS
            term = dot_t(ext[start : start + rows, :], weight[tap : tap + channels, :])
            acc = term if acc is None else acc + term
        parts.append(acc)
    tot_scr[...] = shift_columns(parts[1], parts[2], parts[0])
    below_stats(scal, tot_scr, own, oth, sums, vec, out_own, out_oth, out_stats, which, cells, size)


def last_kernel(scal, part, recv, field, sums, stats, vec, resid_grad, keep, send, tot_scr, *, cells, size):
    i = scal[I]
    for quarter in range(2):
        lanes = part_of(quarter)
        back = norm_back(scal, quarter, sums, stats, vec, 0, cells, size)
        main = back(part[:, lanes] + recv[:, lanes].astype(F32), field[:, lanes])
        tot_scr[:, lanes] = main + resid_grad[:, lanes]
    keep[...] = tot_scr[:, lanes_of(i)]
    send[...] = tot_scr[:, lanes_of(1 - i)].astype(BF)


def weight_grads(scal, act_one, act_two, ext_one, ext_two, rhs_scr, out_scr):
    pix, channels = act_one.shape
    rows = ext_two.shape[0]
    first = (ext_one.shape[0] - rows) // 2
    own = ext_one[first : first + rows, lanes_of(scal[I])]
    for image, wide in enumerate((own, ext_two[...])):
        wide = wide.astype(F32)
        col = lax.broadcasted_iota(jnp.int32, wide.shape, 0) % COLS
        for kx in range(3):
            if kx == 0:
                moved = jnp.where(col < COLS - 1, pltpu.roll(wide, rows - 1, 0), 0.0)
            elif kx == 2:
                moved = jnp.where(col > 0, pltpu.roll(wide, 1, 0), 0.0)
            else:
                moved = wide
            moved = moved.astype(BF)
            for ky in range(3):
                start = (2 - ky) * COLS
                tap = ky * 3 + kx
                lanes = slice(tap * LANES, (tap + 1) * LANES)
                rhs_scr[image * pix : (image + 1) * pix, lanes] = moved[start : start + pix]
    both = jnp.concatenate([act_one, act_two], axis=0)
    for tap in range(0, 9, 2):
        count = min(2, 9 - tap)
        total = lax.dot_general(
            both,
            rhs_scr[:, tap * LANES : (tap + count) * LANES],
            (((0,), (0,)), ((), ())),
            preferred_element_type=F32,
        )
        for n in range(count):
            out_scr[(tap + n) * channels : (tap + n + 1) * channels, :] = total[
                :, n * LANES : (n + 1) * LANES
            ]


def weight_grad_one_kernel(
    scal, up, low, up_there, low_there, ext_one, ext_two, keep, send, rhs_scr, out_scr
):
    cut = up.shape[0]
    mine = jnp.concatenate([up[...], low[0:cut]], axis=0)
    theirs = jnp.concatenate([up_there[...], low_there[0:cut]], axis=0)
    weight_grads(scal, mine, theirs, ext_one, ext_two, rhs_scr, out_scr)
    core = scal[B] % 2
    count = out_scr.shape[0] // 2
    at = lambda n: pl.ds(pl.multiple_of(n * count, count), count)
    keep[...] = out_scr[at(core), :].reshape(keep.shape)
    send[...] = out_scr[at(1 - core), :].astype(BF).reshape(send.shape)


def weight_grad_two_kernel(scal, act, act_there, ext_one, ext_two, wp, out, rhs_scr, out_scr):
    cut = act.shape[0] // 3
    weight_grads(scal, act[cut:], act_there[cut:], ext_one, ext_two, rhs_scr, out_scr)
    blocks = out.shape[0]
    rows = out_scr.shape[0] // blocks
    extra = wp.shape[1] // blocks
    out[:, :rows] = out_scr[...].astype(BF).reshape(blocks, rows, LANES)
    for part in range(2):
        first = rows + part * extra
        out[:, first : first + extra] = wp[part].reshape(blocks, extra, LANES)


def other_sum_kernel(scal, parts, out):
    first = parts.shape[1] - out.shape[0]
    total = parts[0, first:].astype(F32)
    for source in range(1, parts.shape[0]):
        total = total + parts[source, first:].astype(F32)
    out[...] = total.astype(BF)


def total_kernel(scal, own, parts, other, one, two, three, out):
    count = own.shape[0]
    extra = other.shape[0]
    first = own[...] + one[...].astype(F32) + two[...].astype(F32) + three[...].astype(F32)
    out[0:count] = first.astype(BF)
    second = parts[0, : count + extra].astype(F32)
    for source in range(1, parts.shape[0]):
        second = second + parts[source, : count + extra].astype(F32)
    out[count : 2 * count] = second[:count].astype(BF)
    out[2 * count :] = (second[count:] + other[...].astype(F32)).astype(BF)


def scatter_kernel(scal, keep, recv, own, *sends):
    chip = scal[B] // 2
    for mask in range(4):
        chunk = pl.ds(chip ^ mask, 1)
        value = (keep[chunk] + recv[chunk].astype(F32))[0]
        if mask == 0:
            own[...] = value
        else:
            sends[mask - 1][...] = value.astype(BF)


def place_kernel(scal, *refs):
    pieces, (one, two, qkv, out) = refs[:8], refs[8:]
    core, chip = scal[B] % 2, scal[B] // 2
    count = one.shape[0] // 8
    rows = qkv.shape[0] // 6
    for n, piece in enumerate(pieces):
        half = core if n < 4 else 1 - core
        source = chip ^ (n % 4)
        at = lambda slot, size: pl.ds(pl.multiple_of(slot * size, size), size)
        slot = 2 * source + half
        one[at(4 * half + source, count), :] = piece[:count].astype(F32)
        two[at(slot, count), :] = piece[count : 2 * count].astype(F32)
        extra = piece[2 * count :].astype(F32)

        @pl.when(slot < 6)
        def _(extra=extra, slot=slot):
            qkv[at(slot, rows), :] = extra

        @pl.when(slot >= 6)
        def _(extra=extra, slot=slot):
            for m in range(rows // LANES):
                column = (slot - 6) * (rows // LANES) + m
                out[:, lanes_of(column)] = extra[m * LANES : (m + 1) * LANES]


def channel_sums_kernel(scal, one, two, three, mine, theirs):
    rows = jnp.concatenate([total_stats(stats)[0:2] for stats in (one, two, three)], axis=0)
    rows = jnp.concatenate([rows, jnp.zeros((2, rows.shape[1]), F32)], axis=0)
    first, second = rows[:, :LANES], rows[:, LANES:]
    here = scal[I] == 0
    mine[...] = jnp.where(here, first, second)
    theirs[...] = jnp.where(here, second, first)


def channel_grads_kernel(scal, mine, recv, vec, emb, bias_grad, *outs):
    here = scal[I] == 0
    images = (
        jnp.where(here, mine[...], recv[...]),
        jnp.where(here, recv[...], mine[...]),
    )
    gain, bias = vec[4:5], vec[5:6]
    scales = [gain * rows[3:4] + bias * rows[2:3] for rows in images]
    shifts = [rows[2:3] for rows in images]
    grown = [1.0 + vec[8:9], 1.0 + vec[10:11]]
    both = images[0] + images[1]
    bias_grad[0:1] = scales[0] + scales[1]
    bias_grad[1:2] = shifts[0] + shifts[1]
    values = [
        both[1:2],
        both[0:1],
        grown[0] * images[0][3:4] + grown[1] * images[1][3:4],
        grown[0] * images[0][2:3] + grown[1] * images[1][2:3],
        both[5:6],
        both[4:5],
    ]
    for out, value in zip(outs, values):
        out[...] = value
    weight_grad = outs[6]
    turned = emb[...].T
    total = None
    for n, row in enumerate(scales + shifts):
        term = turned[:, n : n + 1] * row
        total = term if total is None else total + term
    weight_grad[...] = total


def out_add_kernel(scal, resid, part, recv, keep, send):
    total = resid[...] + part[...] + recv[...].astype(F32)
    first, second = total[:, :LANES].astype(BF), total[:, LANES:].astype(BF)
    here = scal[I] == 0
    keep[...] = jnp.where(here, first, second)
    send[...] = jnp.where(here, second, first)


def by_images_kernel(scal, out_keep, out_recv, in_keep, in_recv, block_output, input_grad):
    i = scal[I]
    for keep, recv, out in ((out_keep, out_recv, block_output), (in_keep, in_recv, input_grad)):
        out[pl.ds(i, 1)] = keep[...][None]
        out[pl.ds(1 - i, 1)] = recv[...].astype(out.dtype)[None]


def merge_kernel(scal, mine, recv, rest, out):
    out[:, :LANES] = (mine[...] + recv[...].astype(F32)).astype(BF)
    out[:, LANES:] = rest[...]


def context_grad_kernel(scal, context, d_zero, d_one, d_two, d_three, out, tot_scr, *, split):
    rows = out.shape[0]
    turned = [context[image].astype(F32).T.astype(BF) for image in range(2)]
    pieces = (d_zero, d_one, d_two, d_three)
    for h in range(2):
        total = None
        for image in range(2):
            slot = (2 * image + h) ^ scal[Z]
            chosen = pieces[0][...]
            for n in range(1, 4):
                chosen = jnp.where(slot == n, pieces[n][...], chosen)
            term = dot(turned[image], chosen)
            total = term if total is None else total + term
        tot_scr[:, h * LANES : (h + 1) * LANES] = total
    part = scal[B] % split
    out[...] = tot_scr[pl.ds(pl.multiple_of(part * rows, rows), rows), :].astype(BF)


def context_place_kernel(scal, pieces, out, *, split):
    rows = pieces.shape[1]
    for part in range(split):
        for t in range(2):
            first, second = ((2 * t + n) * split + part for n in range(2))
            for h in range(2):
                for kind in range(2):
                    start = h * LANES + kind * HEAD
                    value = jnp.concatenate(
                        [pieces[n, :, start : start + HEAD] for n in (first, second)], axis=1
                    )
                    column = (h + 2 * t) * LANES
                    out[part * rows : (part + 1) * rows, kind, column : column + LANES] = (
                        value.astype(F32)
                    )


def join_kernel(scal, own, *refs):
    pieces, out = refs[:8], refs[8]
    i, b = scal[I], scal[B]
    out[:, lanes_of(i)] = own[...]
    size = own.shape[0] // 8
    for core in range(2):
        for mask in range(4):
            source = b ^ (2 * mask + core)
            target = pl.ds(pl.multiple_of(source * size, size), size)
            out[target, lanes_of(1 - i)] = pieces[4 * core + mask][...]


def place_weight_kernel(scal, own, chunks, out, *, start, width):
    i = scal[I]
    rows = own.shape[0] // width
    size = own.shape[0] // chunks.shape[0]
    for n in range(width):
        out[:, lanes_of(i * width + n)] = own[n * rows : (n + 1) * rows]
    for source in range(chunks.shape[0]):
        n, first = divmod(source * size, rows)
        out[first : first + size, lanes_of((1 - i) * width + n)] = chunks[
            source, start : start + size
        ]


def attend_kernel(
    live, qd, kva, kvb, ctx, dqo, dkva, dkvb, dctx,
    kv_scr, kt_scr, vt_scr, s_scr, e_scr, acc_scr, *, chunk, unroll,
):
    step = pl.program_id(0)
    half_a, half_b, extra = kva.shape[0], kvb.shape[0], ctx.shape[0]
    keys = half_a + half_b
    total = keys + extra
    block = qd.shape[0]

    @pl.when(step == 0)
    def _():
        kv_scr[0:half_a, :] = kva[...]
        kv_scr[half_a:keys, :] = kvb[...]
        kv_scr[keys:total, :] = ctx[...]
        acc_scr[...] = jnp.zeros_like(acc_scr)

        def turn(rows):
            flipped = kv_scr[rows, :].astype(F32).T.astype(BF)
            kt_scr[:, rows] = flipped[:HEAD]
            vt_scr[0:HEAD, rows] = flipped[HEAD:]

        def turn_step(n, carry):
            turn(pl.ds(pl.multiple_of(n * 256, 256), 256))
            return carry

        lax.fori_loop(0, keys // 256, turn_step, 0)
        turn(slice(keys, total))
        vt_scr[HEAD:, :] = jnp.ones((16, total), BF)

    both = qd[...].astype(F32).T
    q_t = both[:HEAD].astype(BF)
    zero = jnp.zeros((HEAD, block), BF)
    q_side = jnp.concatenate([q_t, zero], axis=0)

    def score(rows, top, masked):
        s = dot(kv_scr[rows, :], q_side)
        if masked:
            index = lax.broadcasted_iota(jnp.int32, s.shape, 0)
            s = jnp.where(index < live[0], s, -1e30)
        s_scr[rows, :] = s
        return jnp.maximum(top, jnp.max(s.reshape(-1, 8, block), axis=0))

    def span(n):
        return pl.ds(pl.multiple_of(n * chunk, chunk), chunk)

    def over_keys(func, carry):
        return lax.fori_loop(
            0, keys // chunk, lambda n, c: func(span(n), c), carry, unroll=unroll
        )

    tail = pl.ds(keys, extra)
    top = score(tail, jnp.full((8, block), -1e30, F32), True)
    top = over_keys(lambda rows, c: score(rows, c, False), top)
    top = jnp.max(top, axis=0, keepdims=True)

    def weigh(rows, acc):
        e = jnp.exp(s_scr[rows, :] - top).astype(BF)
        e_scr[rows, :] = e
        return acc + dot(vt_scr[:, rows], e)

    out_t = weigh(tail, jnp.zeros((HEAD + 16, block), F32))
    out_t = over_keys(weigh, out_t)
    inv = 1.0 / out_t[HEAD : HEAD + 1]
    out_t = out_t[:HEAD] * inv
    d_t = both[HEAD:]
    delta = jnp.sum(d_t * out_t, axis=0, keepdims=True) * inv
    d_t = d_t * inv
    d_low = d_t.astype(BF)
    d_side = jnp.concatenate([zero, d_low], axis=0)

    def back(rows, acc):
        d_prob = dot(kv_scr[rows, :], d_side)
        e = e_scr[rows, :]
        d_score = (e.astype(F32) * (d_prob - delta)).astype(BF)
        acc_scr[0:HEAD, rows] += dot_t(q_t, d_score)
        acc_scr[HEAD:, rows] += dot_t(d_low, e)
        return acc + dot(kt_scr[:, rows], d_score)

    dq_t = back(tail, jnp.zeros((HEAD, block), F32))
    dq_t = over_keys(back, dq_t)
    dqo[...] = jnp.concatenate([dq_t, out_t], axis=0).T.astype(BF)

    @pl.when(step == pl.num_programs(0) - 1)
    def _():
        dkva[...] = acc_scr[:, 0:half_a].T
        dkvb[...] = acc_scr[:, half_a:keys].T.astype(BF)
        dctx[...] = acc_scr[:, keys:total].T


def attend(live, recv, kva, kvb, ctx, deps):
    queries = recv.shape[0]
    block = min(1024, queries)
    half_a, half_b, extra = recv.shape[0] if kva is recv else kva.shape[0], kvb.shape[0], ctx.shape[0]
    total = half_a + half_b + extra
    whole = lambda shape: pl.BlockSpec(shape, lambda n: (0, 0))
    kernel = functools.partial(attend_kernel, chunk=512, unroll=8)

    def inner(*refs):
        kernel(*refs[:5], *refs[5 + len(deps) :])

    return pl.pallas_call(
        inner,
        grid=(queries // block,),
        in_specs=[
            pl.BlockSpec(memory_space=pltpu.SMEM),
            pl.BlockSpec((block, LANES), lambda n: (n, 1)),
            whole((half_a, LANES)),
            whole((half_b, LANES)),
            whole((extra, LANES)),
        ]
        + [pl.BlockSpec(memory_space=pl.ANY)] * len(deps),
        out_specs=[
            pl.BlockSpec((block, LANES), lambda n: (n, 0)),
            whole((half_a, LANES)),
            whole((half_b, LANES)),
            whole((extra, LANES)),
        ],
        out_shape=[
            jax.ShapeDtypeStruct((queries, LANES), BF),
            jax.ShapeDtypeStruct((half_a, LANES), F32),
            jax.ShapeDtypeStruct((half_b, LANES), BF),
            jax.ShapeDtypeStruct((extra, LANES), F32),
        ],
        scratch_shapes=[
            pltpu.VMEM((total, LANES), BF),
            pltpu.VMEM((HEAD, total), BF),
            pltpu.VMEM((HEAD + 16, total), BF),
            pltpu.VMEM((total, block), F32),
            pltpu.VMEM((total, block), BF),
            pltpu.VMEM((LANES, total), F32),
        ],
        compiler_params=pltpu.CompilerParams(vmem_limit_bytes=VMEM_BYTES),
        cost_estimate=pl.CostEstimate(
            flops=int(38 * 1.15e9), bytes_accessed=1, transcendentals=0
        ),
    )(live, recv, kva, kvb, ctx, *deps)


def call(kernel, args, outs, scratch=(), deps=(), time=0.0):
    in_vmem = pl.BlockSpec(memory_space=pltpu.VMEM)
    in_smem = pl.BlockSpec(memory_space=pltpu.SMEM)
    anywhere = pl.BlockSpec(memory_space=pl.ANY)
    count = len(args)

    def inner(*refs):
        kernel(*refs[:count], *refs[count + len(deps) :])

    return pl.pallas_call(
        inner,
        in_specs=[in_smem] + [in_vmem] * (count - 1) + [anywhere] * len(deps),
        out_specs=[in_vmem] * len(outs),
        out_shape=[jax.ShapeDtypeStruct(s, d) for s, d in outs],
        scratch_shapes=[pltpu.VMEM(s, d) for s, d in scratch],
        compiler_params=pltpu.CompilerParams(vmem_limit_bytes=VMEM_BYTES),
        cost_estimate=pl.CostEstimate(
            flops=1 + int(time * 1.15e9), bytes_accessed=1, transcendentals=0
        ),
    )(*args, *deps)


def after(values, *deps):
    anywhere = pl.BlockSpec(memory_space=pl.ANY)
    count = len(values)

    def inner(*refs):
        pass

    return pl.pallas_call(
        inner,
        in_specs=[anywhere] * (count + len(deps)),
        out_specs=[anywhere] * count,
        out_shape=[jax.ShapeDtypeStruct(v.shape, v.dtype) for v in values],
        input_output_aliases={n: n for n in range(count)},
        cost_estimate=pl.CostEstimate(flops=1, bytes_accessed=1, transcendentals=0),
    )(*values, *deps)


def embed_features(timesteps, image_embed):
    half_width = image_embed.shape[1] // 2
    freqs = jnp.exp(-math.log(10000.0) * jnp.arange(half_width, dtype=F32) / half_width)
    angles = timesteps.astype(F32)[:, None] * freqs[None, :]
    return jax.nn.silu(jnp.concatenate([jnp.cos(angles), jnp.sin(angles)], axis=1) + image_embed)


def body(
    block_input,
    cotangent,
    image_embed,
    timesteps,
    text_len,
    context,
    conv1_weight,
    conv2_weight,
    embed_weight,
    embed_bias,
    norm1_gain,
    norm1_bias,
    norm2_gain,
    norm2_bias,
    norm3_gain,
    norm3_bias,
    qkv_weight,
    out_weight,
    ctx_weight,
):
    images, row_count, col_count, width = block_input.shape
    channels = qkv_weight.shape[0]
    size = channels // GROUPS
    blocks = lax.axis_size("blk")
    pix = row_count * col_count
    cells = float(pix * blocks * size)
    split = blocks // 4
    ctx_len = context.shape[1]
    b = lax.axis_index("blk")
    z = lax.axis_index("ch")
    h, i = z % 2, z // 2
    row, rows_all = b * row_count, blocks * row_count
    inside = [row >= 1, row + row_count < rows_all, row >= 2, row + row_count + 1 < rows_all]
    scal = jnp.stack([h, i] + [flag.astype(jnp.int32) for flag in inside] + [z, b]).astype(jnp.int32)


    def over_ch(value, mask):
        return lax.ppermute(value, "ch", [(n, n ^ mask) for n in range(4)])

    def over_blk(value, mask):
        return lax.ppermute(value, "blk", [(n, n ^ mask) for n in range(blocks)])

    def ring(value, step):
        return lax.ppermute(value, "blk", [(n, (n + step) % blocks) for n in range(blocks)])

    def halo(first, last):
        if row_count >= 2:
            return ring(last, 1), ring(first, -1)
        return (
            jnp.concatenate([ring(last, 2), ring(last, 1)], axis=0),
            jnp.concatenate([ring(first, -1), ring(first, -2)], axis=0),
        )

    pairs = [[n * 4 + 2 * m + k for n in range(blocks) for k in range(2)] for m in range(2)]

    def to_image(value):
        return lax.all_to_all(value, ("blk", "ch"), 0, 0, axis_index_groups=pairs)

    def by_image(first, second):
        return jnp.where(i == 0, first, second), jnp.where(i == 0, second, first)

    def plane(value):
        mine = [value] + [over_blk(value, 2 * mask) for mask in (1, 2, 3)]
        return mine + [over_blk(piece, 1) for piece in mine]

    w1_own = conv1_weight.reshape(-1, width)
    w2_own = conv2_weight.reshape(-1, width)
    heads = lambda v: v.reshape(channels, 2, HEAD)
    wp_own = jnp.stack(
        [
            jnp.concatenate([heads(qkv_weight[:, 1]), heads(qkv_weight[:, 2])], axis=2),
            jnp.concatenate([heads(qkv_weight[:, 0] * 0.125), heads(out_weight.T)], axis=2),
        ],
        axis=0,
    )
    wp_own = jnp.transpose(wp_own, (2, 0, 1, 3)).reshape(-1, LANES)
    w1_rows, w2_rows, wp_rows = (w.shape[0] // blocks for w in (w1_own, w2_own, wp_own))
    chunk_of = lambda w: lax.dynamic_slice_in_dim(w, b * (w.shape[0] // blocks), w.shape[0] // blocks, 0)
    w1_slice = chunk_of(w1_own)

    emb_act = embed_features(timesteps, image_embed).astype(BF)
    scale_shift = (
        jnp.einsum("ie,esc->isc", emb_act, embed_weight, preferred_element_type=F32) + embed_bias
    )
    local_vec = jnp.concatenate(
        [
            jnp.zeros((2, width), F32),
            jnp.stack([norm1_gain, norm1_bias, norm2_gain, norm2_bias, norm3_gain, norm3_bias]),
            scale_shift.reshape(4, width),
            jnp.zeros((4, width), F32),
        ],
        axis=0,
    )
    x_mine, x_theirs = call(
        image_split_kernel,
        [scal, block_input.reshape(images, pix, width)],
        [((pix, width), BF)] * 2,
        deps=[w1_slice],
    )
    w1_chunk = over_ch(w1_slice, 2)
    x_two, x_one = over_ch(x_theirs, 2), over_ch(x_mine, 1)
    x_three = over_ch(x_two, 1)
    if blocks == 8:
        w1_pieces = plane(w1_chunk)
    else:
        w1_pieces = [lax.all_gather(w1_chunk, "blk", axis=0, tiled=True)]
    x_sums = call(
        functools.partial(input_sums_kernel, blocks=blocks),
        [scal, block_input.reshape(images, pix, width), local_vec],
        [((4 * blocks, 16, width), F32)],
        deps=[x_mine],
    )[0]
    sums1 = lax.all_to_all(x_sums, ("blk", "ch"), 0, 0)
    two_source = jnp.concatenate([chunk_of(w2_own), chunk_of(wp_own)], axis=0)
    two_chunk = over_ch(two_source, 2)
    (two_chunk,) = after((two_chunk,), x_one, x_sums, x_three, *w1_pieces[1:4])
    wide = dict(axis=1)
    x_own = jnp.concatenate(by_image(x_mine, x_two), **wide)
    x_oth = jnp.concatenate(by_image(x_one, x_three), **wide)
    edge = min(2 * COLS, pix)
    x_top, x_bot = halo(
        jnp.concatenate([x_own[:edge], x_oth[:edge]], **wide),
        jnp.concatenate([x_own[pix - edge :], x_oth[pix - edge :]], **wide),
    )
    if blocks == 8:
        w1 = call(join_kernel, [scal, w1_own] + w1_pieces, [((w1_own.shape[0], HALF), BF)])[0]
    else:
        w1_oth = w1_pieces[0]
        w1 = jnp.concatenate(by_image(w1_own, w1_oth), **wide)
    two = lax.all_gather(two_chunk, "blk", axis=0)
    w2 = call(
        functools.partial(place_weight_kernel, start=0, width=1),
        [scal, w2_own, two],
        [((w2_own.shape[0], HALF), BF)],
    )[0]
    j = b // split
    ctx_rows = -(-ctx_len // 16) * 16
    ctx_w = jnp.stack(
        [
            lax.dynamic_slice_in_dim(
                ctx_weight, 128 * (hh + 2 * (j // 2)) + HEAD * (j % 2), HEAD, 2
            ).reshape(-1, 2 * HEAD)
            for hh in range(2)
        ]
    )
    ctx_term = jnp.einsum("itx,hxk->ihtk", context, ctx_w, preferred_element_type=F32)
    ctx_term = jnp.pad(
        ctx_term.astype(BF).reshape(4, ctx_len, 2 * HEAD),
        ((0, 0), (0, ctx_rows - ctx_len), (0, 0)),
    )
    ctx_kv = lax.psum_scatter(ctx_term, "ch", scatter_dimension=0)
    live = (CLIPTOK + jnp.where(i == 0, text_len[0], text_len[1])).astype(jnp.int32)[None]

    emb_f = jnp.repeat(emb_act.astype(F32), 2, axis=1)
    odd = (jnp.arange(emb_f.shape[1]) % 2)[None]
    emb_rows = jnp.concatenate(
        [emb_f * (1 - odd), emb_f * odd, jnp.zeros((4, emb_f.shape[1]), F32)], axis=0
    )
    kind = dict(cells=cells, size=size)
    ext = pix + 2 * COLS
    stat_shape = ((2 * blocks, 8, HALF), F32)

    c_mine, c_theirs = call(
        image_split_kernel,
        [scal, cotangent.reshape(images, pix, width)],
        [((pix, width), BF)] * 2,
        deps=[x_sums],
    )

    hid_own, hid_stat, act1, vec = call(
        functools.partial(conv1_kernel, **kind),
        [scal, x_own, x_oth, x_top, x_bot, sums1, w1],
        [((ext, HALF), BF), stat_shape, ((pix, channels), BF), ((4, 16, LANES), F32)],
        [((ext + 2 * COLS, channels), BF)],
        deps=[ctx_term, c_mine, emb_rows, live],
    )
    hid_oth = over_ch(hid_own, 1)
    sums2 = to_image(hid_stat)

    c_mine, c_theirs = after((c_mine, c_theirs), hid_oth, w2)
    c_one, c_two = over_ch(c_mine, 1), over_ch(c_theirs, 2)
    c_three = over_ch(c_two, 1)
    cot_own = jnp.concatenate(by_image(c_mine, c_two), **wide)
    cot_oth = jnp.concatenate(by_image(c_one, c_three), **wide)

    edges = ((2, edge, HALF), BF)
    res_f, res_own, res_stat, act_first, act_rest, res_edges = call(
        functools.partial(conv2_kernel, **kind),
        [scal, hid_own, hid_oth, sums2, vec, w2, x_own, act1],
        [
            ((pix, HALF), F32),
            ((pix, HALF), BF),
            stat_shape,
            ((pix // 2, channels), BF),
            ((pix + pix // 2, channels), BF),
            edges,
        ],
        [((ext, channels), BF)],
    )
    res_oth = over_ch(res_own, 1)
    sums3 = to_image(res_stat)
    wp = call(
        functools.partial(place_weight_kernel, start=w2_rows, width=4),
        [scal, wp_own, two],
        [((channels, 4 * HALF), BF)],
        deps=[res_oth],
    )[0]
    packed, act3, cot_all, cot_edges = call(
        functools.partial(qkv_kernel, **kind),
        [scal, res_own, res_oth, sums3, vec, cot_own, cot_oth, wp],
        [((4, pix, HALF), BF), ((pix, channels), BF), ((pix, channels), BF), edges],
        deps=[ctx_kv],
    )
    recv = lax.all_to_all(packed.reshape(blocks, pix // split, HALF), "blk", 0, 0)
    res_edges, act_first = after((res_edges, act_first), packed)
    res_top, res_bot = halo(res_edges[0], res_edges[1])
    cot_top, cot_bot = halo(cot_edges[0], cot_edges[1])
    first_there = over_ch(act_first, 2)
    (recv,) = after((recv,), res_top, res_bot, cot_top, cot_bot, first_there)
    recv = recv.reshape(-1, HALF)
    rest_there = over_ch(act_rest, 2)
    if split == 2:
        kva, kvb = recv, over_blk(recv[:, :LANES], 1)
    else:
        groups = [[n * split + m for m in range(split)] for n in range(4)]
        kv_all = lax.all_gather(
            recv[:, :LANES], "blk", axis=0, tiled=True, axis_index_groups=groups
        )
        kva, kvb = kv_all[: kv_all.shape[0] // 2], kv_all[kv_all.shape[0] // 2 :]
    dqo, dkva, dkvb, dctx = attend(live, recv, kva, kvb, ctx_kv, [])
    if split == 2:
        d_ctx = dctx + over_blk(dctx, 1)
        back = call(
            merge_kernel,
            [scal, dkva, over_blk(dkvb, 1), dqo],
            [((dqo.shape[0], HALF), BF)],
            deps=[rest_there],
        )[0]
    else:
        d_ctx = lax.psum(dctx, "blk", axis_index_groups=groups)
        d_kv = lax.psum_scatter(
            jnp.concatenate([dkva, dkvb.astype(F32)], axis=0),
            "blk",
            scatter_dimension=0,
            axis_index_groups=groups,
            tiled=True,
        )
        back = jnp.concatenate([d_kv.astype(BF), dqo], axis=1)
    grads = lax.all_to_all(back.reshape(blocks, pix // split, HALF), "blk", 0, 0)
    grads = grads.reshape(4, pix, HALF)

    features = context.shape[2] // split
    d_ctx = d_ctx[:ctx_len].astype(BF)
    ctx_part = call(
        functools.partial(context_grad_kernel, split=split),
        [scal, context, d_ctx] + [over_ch(d_ctx, mask) for mask in (1, 2, 3)],
        [((features, HALF), BF)],
        [((context.shape[2], HALF), F32)],
    )[0]
    ctx_all = lax.all_gather(ctx_part, "blk", axis=0)

    def low_grad(rows):
        return [((rows, HALF), F32), ((rows, HALF), BF), stat_shape]

    p3_own, p3_oth, st3 = call(
        functools.partial(qkv_back_kernel, **kind),
        [scal, grads, wp, res_own, res_oth, sums3, vec],
        low_grad(pix),
        [((pix, channels), F32)],
        deps=[ctx_part],
    )
    r3 = over_ch(p3_oth, 1)
    stats3 = to_image(st3)
    proj_own, proj_oth, wp_part = call(
        out_kernel,
        [scal, grads, wp, act3, cot_all],
        [((pix, HALF), F32), ((pix, HALF), BF), ((2, 4 * channels, LANES), BF)],
        [((pix, channels), F32)],
        deps=[r3],
    )
    first3 = (p3_own[:edge] + r3[:edge].astype(F32)).astype(BF)
    last3 = (p3_own[pix - edge :] + r3[pix - edge :].astype(F32)).astype(BF)
    d_top3, d_bot3 = halo(first3, last3)
    d_resid, ext2, away2 = call(
        functools.partial(norm3_back_kernel, **kind),
        [
            scal, p3_own, r3, d_top3, d_bot3, res_own, res_top, res_bot, cot_own, cot_top, cot_bot,
            sums3, stats3, vec,
        ],
        [((pix, HALF), F32), ((ext + 2 * COLS, HALF), BF), ((ext, LANES), BF)],
        deps=[proj_own],
    )
    there2 = over_ch(away2, 2)
    p2_own, p2_oth, st2 = call(
        functools.partial(conv_back_kernel, which=1, **kind),
        [scal, ext2, w2, hid_own, hid_oth, sums2, vec],
        low_grad(ext),
        [((ext, channels), F32)],
        time=8.0,
    )
    r2 = over_ch(p2_oth, 1)
    (st2,) = after((st2,), there2)
    stats2 = to_image(st2)
    conv_rows, wp_rows = 9 * channels // blocks, 4 * channels // blocks
    part2 = call(
        weight_grad_two_kernel,
        [scal, act_rest, rest_there, ext2, there2, wp_part],
        [((blocks, conv_rows + 2 * wp_rows, LANES), BF)],
        [((2 * pix, 9 * LANES), BF), ((9 * channels, LANES), F32)],
        deps=[r2],
    )[0]
    ext1, away1 = call(
        functools.partial(norm2_back_kernel, **kind),
        [scal, p2_own, r2, hid_own, sums2, stats2, vec],
        [((ext, HALF), BF), ((ext, LANES), BF)],
        deps=[part2, ctx_all],
    )
    parts2 = lax.all_to_all(part2, "blk", 0, 0)
    there1 = over_ch(away1, 2)
    p1_own, p1_oth, st1 = call(
        functools.partial(conv_back_kernel, which=0, **kind),
        [scal, ext1, w1, x_own, x_oth, sums1, vec],
        low_grad(pix),
        [((pix, channels), F32)],
        time=8.0,
    )
    (st1,) = after((st1,), there1, parts2)
    (proj_late,) = after((proj_oth,), there1)
    r1 = over_ch(p1_oth, 1)
    stats1 = to_image(st1)
    half_shape = (4, 9 * channels // 8, LANES)
    keep1, send1 = call(
        weight_grad_one_kernel,
        [scal, act_first, act_rest, first_there, rest_there, ext1, there1],
        [(half_shape, F32), (half_shape, BF)],
        [((2 * pix, 9 * LANES), BF), ((9 * channels, LANES), F32)],
        deps=[p1_own],
        time=20.0,
    )
    if blocks == 8:
        own1, *sends = call(
            scatter_kernel,
            [scal, keep1, over_blk(send1, 1)],
            [((conv_rows, LANES), F32)] + [((conv_rows, LANES), BF)] * 3,
        )
    else:
        own1 = keep1
    if blocks == 8:
        other = call(other_sum_kernel, [scal, parts2], [((wp_rows, LANES), BF)], deps=[own1])[0]
        total = call(
            total_kernel,
            [scal, own1, parts2, over_ch(other, 2)]
            + [over_blk(v, 2 * n + 2) for n, v in enumerate(sends)],
            [((2 * conv_rows + wp_rows, LANES), BF)],
        )[0]
    else:
        total = own1
    out_keep, out_send = call(
        out_add_kernel,
        [scal, res_f, proj_own, over_ch(proj_late, 1)],
        [((pix, width), BF)] * 2,
        deps=[total],
    )
    in_keep, in_send = call(
        functools.partial(last_kernel, **kind),
        [scal, p1_own, r1, x_own, sums1, stats1, vec, d_resid],
        [((pix, width), F32), ((pix, width), BF)],
        [((pix, HALF), F32)],
        deps=[total],
        time=40.0,
    )
    sums_here, sums_away = call(
        channel_sums_kernel,
        [scal, stats1, stats2, stats3],
        [((8, LANES), F32)] * 2,
        deps=[total],
    )
    sums_recv = over_ch(sums_away, 2)
    out_recv, in_recv = over_ch(out_send, 2), over_ch(in_send, 2)
    bias_grad, *smalls, embed_weight_grad = call(
        channel_grads_kernel,
        [scal, sums_here, sums_recv, local_vec, emb_rows],
        [((2, LANES), F32)] + [((1, LANES), F32)] * 6 + [((emb_rows.shape[1], LANES), F32)],
        deps=[total],
        time=15.0,
    )
    block_output, input_grad = call(
        by_images_kernel,
        [scal, out_keep, out_recv, in_keep, in_recv],
        [((images, pix, width), BF), ((images, pix, width), F32)],
        deps=[total],
        time=10.0,
    )
    if blocks == 8:
        ctx_grad = call(
            functools.partial(context_place_kernel, split=split),
            [scal, ctx_all],
            [((context.shape[2], 2, channels), F32)],
            deps=[total],
            time=10.0,
        )[0]
        grad1, grad2, qkv_grad, out_grad = call(
            place_kernel,
            [scal] + plane(total),
            [((9 * channels, LANES), F32)] * 2
            + [((3 * channels, LANES), F32), ((LANES, channels), F32)],
            deps=[block_output, ctx_grad, bias_grad],
        )
    else:
        ctx_grad = ctx_all.reshape(2, 2, split, features, 2, 2, HEAD)
        ctx_grad = jnp.transpose(ctx_grad, (2, 3, 5, 0, 4, 1, 6)).astype(F32)
        flip = lambda c: jnp.where(b % 2 == 0, *((keep1.astype(BF), send1)[:: 1 - 2 * c]))
        grad1 = lax.psum(jnp.concatenate([flip(0), flip(1)], axis=0), "blk").astype(F32)
        sums = lax.psum(part2, "blk").astype(F32)
        cut = conv_rows + wp_rows
        grad2 = sums[:, :conv_rows]
        wp_grad = sums[:, conv_rows:cut] + over_ch(sums[:, cut:].astype(BF), 2).astype(F32)
        wp_grad = wp_grad.reshape(-1, LANES)
        qkv_grad, out_grad = wp_grad[: 3 * channels], wp_grad[3 * channels :]
        out_grad = jnp.concatenate(list(out_grad.reshape(-1, LANES, LANES)), axis=1)
    qkv_grad = jnp.transpose(qkv_grad.reshape(3, channels, LANES), (1, 0, 2))

    return (
        block_output.reshape(block_input.shape),
        input_grad.reshape(block_input.shape),
        grad1.reshape(conv1_weight.shape),
        grad2.reshape(conv2_weight.shape),
        embed_weight_grad.reshape(embed_weight.shape),
        bias_grad,
        *(value.reshape(width) for value in smalls),
        qkv_grad,
        out_grad,
        ctx_grad.reshape(ctx_weight.shape),
    )


def solution(mesh):
    return jax.shard_map(
        body,
        mesh=mesh,
        in_specs=(
            P(None, "blk", None, "ch"),
            P(None, "blk", None, "ch"),
            P(),
            P(),
            P(),
            P(None, None, "ch"),
            P(None, None, None, "ch"),
            P(None, None, None, "ch"),
            P(None, None, "ch"),
            P(None, "ch"),
            P("ch"),
            P("ch"),
            P("ch"),
            P("ch"),
            P("ch"),
            P("ch"),
            P(None, None, "ch"),
            P("ch", None),
            P("ch", None, None),
        ),
        out_specs=(
            P(None, "blk", None, "ch"),
            P(None, "blk", None, "ch"),
            P(None, None, None, "ch"),
            P(None, None, None, "ch"),
            P(None, None, "ch"),
            P(None, "ch"),
            P("ch"),
            P("ch"),
            P("ch"),
            P("ch"),
            P("ch"),
            P("ch"),
            P(None, None, "ch"),
            P("ch", None),
            P("ch", None, None),
        ),
        check_vma=False,
    )
```

```python
import functools
import math

import jax
import jax.numpy as jnp
from jax import lax
from jax.experimental import pallas as pl
from jax.experimental.pallas import tpu as pltpu
from jax.sharding import PartitionSpec as P

HEAD = 64
GROUPS = 32
CLIPTOK = 4
LANES = 128
HALF = 256
COLS = 64
VMEM_BYTES = 56 * 2**20
BF = jnp.bfloat16
F32 = jnp.float32

H, I, UP1, DOWN1, UP2, DOWN2, Z, B = range(8)


def dot(a, b):
    return jnp.dot(a, b, preferred_element_type=F32)


def dot_t(a, b):
    return lax.dot_general(a, b, (((1,), (1,)), ((), ())), preferred_element_type=F32)


def group_sum(vec, size):
    lane = lax.broadcasted_iota(jnp.int32, vec.shape, 1)
    step = 1
    while step < size:
        low = pltpu.roll(vec, step, 1)
        high = pltpu.roll(vec, LANES - step, 1)
        vec = vec + jnp.where((lane & step) != 0, low, high)
        step *= 2
    return vec


def shards(scal):
    h = scal[H]
    return (h, h + 2, 1 - h, 3 - h)


def lanes_of(shard):
    return pl.ds(pl.multiple_of(shard * LANES, LANES), LANES)


def part_of(quarter):
    return slice((quarter % 2) * LANES, (quarter % 2 + 1) * LANES)


def norm_stats(scal, sums, quarter, cells, size):
    wide = sums.shape[2] == HALF
    kinds = 2 if wide else 4
    shard = shards(scal)[quarter]
    total = None
    for source in range(sums.shape[0] // kinds):
        row = source * kinds + (shard % 2 if wide else shard)
        piece = sums[pl.ds(row, 1)][0]
        total = piece if total is None else total + piece
    if wide:
        total = total[:, part_of(quarter)]
    total = group_sum(total, size)
    mean = total[0:1] / cells
    inv = lax.rsqrt(total[1:2] / cells - mean * mean + 1e-05)
    return mean, inv


def affine_of(scal, vec, quarter, which, mean, inv):
    row = vec[pl.ds(shards(scal)[quarter], 1)][0]
    gain = row[2 * which + 2 : 2 * which + 3]
    bias = row[2 * which + 3 : 2 * which + 4]
    if which == 1:
        first = scal[I] == 0
        grow = 1.0 + jnp.where(first, row[8:9], row[10:11])
        gain, bias = gain * grow, bias * grow + jnp.where(first, row[9:10], row[11:12])
    slope = inv * gain
    return gain, slope, bias - mean * slope


def column_sums(first, second):
    rows = jnp.concatenate(
        [jnp.sum(first, axis=0, keepdims=True), jnp.sum(second, axis=0, keepdims=True)], axis=0
    )
    return jnp.concatenate([rows, jnp.zeros((6, rows.shape[1]), F32)], axis=0)


def shift_columns(total, left, right):
    col = lax.broadcasted_iota(jnp.int32, total.shape, 0) % COLS
    rows = total.shape[0]
    total = total + jnp.where(col > 0, pltpu.roll(left, 1, 0), 0.0)
    return total + jnp.where(col < COLS - 1, pltpu.roll(right, rows - 1, 0), 0.0)


def silu_slope(field):
    sigma = jax.nn.sigmoid(field)
    return sigma * (1.0 + field * (1.0 - sigma))


def masked_rows(scal, value, flag):
    return jnp.where(scal[flag] > 0, value, 0.0)


def input_sums_kernel(scal, field, vec, out, *, blocks):
    for image in range(2):
        value = field[image].astype(F32)
        sums = column_sums(value, value * value)[:2]
        sums = jnp.concatenate([sums, vec[2:]], axis=0)
        for target in range(blocks):
            out[4 * target + 2 * image] = sums
            out[4 * target + 2 * image + 1] = sums


def image_split_kernel(scal, field, mine, theirs):
    mine[...] = field[pl.ds(scal[I], 1)][0]
    theirs[...] = field[pl.ds(1 - scal[I], 1)][0]


def spread(out, sums):
    for target in range(out.shape[0]):
        out[target] = sums


def conv1_kernel(scal, own, oth, top, bot, sums, weight, out, out_sums, act_out, vec, act_scr, *, cells, size):
    pix = own.shape[0]
    vec[...] = sums[0:4]
    rows = pix + 2 * COLS
    for quarter in range(4):
        shard = shards(scal)[quarter]
        mean, inv = norm_stats(scal, sums, quarter, cells, size)
        gain, slope, offset = affine_of(scal, vec, quarter, 0, mean, inv)
        lanes = slice(quarter * LANES, (quarter + 1) * LANES)

        def active(field):
            pre = field.astype(F32) * slope + offset
            return pre * jax.nn.sigmoid(pre)

        half = own if quarter < 2 else oth
        main = active(half[:, part_of(quarter)]).astype(BF)
        above, below = active(top[:, lanes]), active(bot[:, lanes])
        act_scr[2 * COLS : 2 * COLS + pix, lanes_of(shard)] = main
        act_out[:, lanes_of(shard)] = main
        act_scr[0:COLS, lanes_of(shard)] = masked_rows(scal, above[:COLS], UP2).astype(BF)
        act_scr[COLS : 2 * COLS, lanes_of(shard)] = masked_rows(scal, above[COLS:], UP1).astype(BF)
        end = 2 * COLS + pix
        act_scr[end : end + COLS, lanes_of(shard)] = masked_rows(scal, below[:COLS], DOWN1).astype(BF)
        act_scr[end + COLS :, lanes_of(shard)] = masked_rows(scal, below[COLS:], DOWN2).astype(BF)
    result = convolve(act_scr, weight, rows)
    out[...] = result.astype(BF)
    inner = result[COLS : COLS + pix]
    spread(out_sums, column_sums(inner, inner * inner))


def convolve(act_scr, weight, rows):
    channels = act_scr.shape[1]
    parts = []
    for kx in range(3):
        acc = None
        for ky in range(3):
            tap = (ky * 3 + kx) * channels
            term = dot(act_scr[ky * COLS : ky * COLS + rows, :], weight[tap : tap + channels, :])
            acc = term if acc is None else acc + term
        parts.append(acc)
    return shift_columns(parts[1], parts[0], parts[2])


def conv2_kernel(scal, own, oth, sums, vec, weight, base, act_below, out_f, out_low, out_sums, act_first, act_out, edges, act_scr, *, cells, size):
    pix = base.shape[0]
    cut = act_first.shape[0]
    act_first[...] = act_below[0:cut]
    act_out[0 : pix - cut, :] = act_below[cut:]
    for quarter in range(4):
        shard = shards(scal)[quarter]
        mean, inv = norm_stats(scal, sums, quarter, cells, size)
        gain, slope, offset = affine_of(scal, vec, quarter, 1, mean, inv)
        half = own if quarter < 2 else oth
        pre = half[:, part_of(quarter)].astype(F32) * slope + offset
        act = pre * jax.nn.sigmoid(pre)
        main = act[COLS : COLS + pix].astype(BF)
        act_scr[COLS : COLS + pix, lanes_of(shard)] = main
        act_out[pix - cut :, lanes_of(shard)] = main
        act_scr[0:COLS, lanes_of(shard)] = masked_rows(scal, act[:COLS], UP1).astype(BF)
        act_scr[COLS + pix :, lanes_of(shard)] = masked_rows(scal, act[COLS + pix :], DOWN1).astype(BF)
    result = convolve(act_scr, weight, pix) + base[...].astype(F32)
    out_f[...] = result
    low = result.astype(BF)
    out_low[...] = low
    if edges.shape[1] < pix:
        edges[0], edges[1] = low[: edges.shape[1]], low[pix - edges.shape[1] :]
    else:
        edges[0], edges[1] = low, low
    spread(out_sums, column_sums(result, result * result))


def qkv_kernel(scal, own, oth, sums, vec, cot_own, cot_oth, weight, out, act_out, cot_out, edges, *, cells, size):
    rows = edges.shape[1]
    edges[0], edges[1] = cot_own[0:rows], cot_own[cot_own.shape[0] - rows :]
    for quarter in range(4):
        shard = shards(scal)[quarter]
        mean, inv = norm_stats(scal, sums, quarter, cells, size)
        gain, slope, offset = affine_of(scal, vec, quarter, 2, mean, inv)
        half = own if quarter < 2 else oth
        cot = cot_own if quarter < 2 else cot_oth
        field = half[:, part_of(quarter)].astype(F32)
        act_out[:, lanes_of(shard)] = (field * slope + offset).astype(BF)
        cot_out[:, lanes_of(shard)] = cot[:, part_of(quarter)]
    for head in range(4):
        columns = weight[:, head * HALF : (head + 1) * HALF]
        fwd = dot(act_out[...], columns)
        back = dot(cot_out[...], columns[:, LANES:])
        out[head, :, :LANES] = fwd[:, :LANES].astype(BF)
        lane = lax.broadcasted_iota(jnp.int32, back.shape, 1)
        out[head, :, LANES:] = jnp.where(lane < HEAD, fwd[:, LANES:], back).astype(BF)


def below_stats(scal, total, own, oth, sums, vec, out_own, out_oth, out_stats, which, cells, size):
    rows = total.shape[0]
    pix = rows - 2 * COLS if which == 1 else rows
    inner = slice(COLS, COLS + pix) if which == 1 else slice(0, pix)
    for quarter in range(4):
        shard = shards(scal)[quarter]
        mean, inv = norm_stats(scal, sums, quarter, cells, size)
        gain, slope, offset = affine_of(scal, vec, quarter, which, mean, inv)
        half = own if quarter < 2 else oth
        part = part_of(quarter)
        if quarter < 2:
            out_own[:, part] = total[:, lanes_of(shard)]
        else:
            out_oth[:, part] = total[:, lanes_of(shard)].astype(BF)
        grad = total[inner, lanes_of(shard)]
        field = half[inner, part].astype(F32)
        if which < 2:
            grad = grad * silu_slope(field * slope + offset)
        result = column_sums(grad, grad * ((field - mean) * inv))
        slot = scal[H] if quarter < 2 else 1 - scal[H]
        for target in range(out_stats.shape[0] // 2):
            out_stats[pl.ds(2 * target + slot, 1), :, part] = result[None]


def qkv_back_kernel(scal, grads, weight, own, oth, sums, vec, out_own, out_oth, out_stats, tot_scr, *, cells, size):
    total = None
    for head in range(4):
        columns = weight[:, head * HALF : (head + 1) * HALF]
        grad = grads[head]
        lane = lax.broadcasted_iota(jnp.int32, grad.shape, 1)
        term = dot_t(jnp.where(lane < 3 * HEAD, grad, jnp.zeros_like(grad)), columns)
        total = term if total is None else total + term
    tot_scr[...] = total
    below_stats(scal, tot_scr, own, oth, sums, vec, out_own, out_oth, out_stats, 2, cells, size)


def out_kernel(scal, grads, weight, act, cot, proj_own, proj_oth, wgrad, tot_scr):
    channels = act.shape[1]
    act_t = act[...].astype(F32).T.astype(BF)
    total = None
    for pair in range(2):
        slot = jnp.where(scal[I] == pair, 0, 1)
        parts, outs = [], []
        for head in (2 * pair, 2 * pair + 1):
            columns = weight[:, head * HALF + LANES : (head + 1) * HALF]
            grad = grads[head]
            low = grad[:, LANES:]
            lane = lax.broadcasted_iota(jnp.int32, low.shape, 1)
            term = dot_t(jnp.where(lane < HEAD, jnp.zeros_like(low), low), columns)
            total = term if total is None else total + term
            parts.append(dot(act_t, grad))
            outs.append(dot(low.astype(F32).T[HEAD:].astype(BF), cot[...]))
        first, second = parts
        pieces = [
            jnp.concatenate([first[:, LANES : LANES + HEAD], second[:, LANES : LANES + HEAD]], axis=1)
            * 0.125,
            jnp.concatenate([first[:, :HEAD], second[:, :HEAD]], axis=1),
            jnp.concatenate([first[:, HEAD:LANES], second[:, HEAD:LANES]], axis=1),
        ]
        both = jnp.concatenate(outs, axis=0)
        pieces += [both[:, n * LANES : (n + 1) * LANES] for n in range(channels // LANES)]
        wgrad[pl.ds(slot, 1)] = jnp.concatenate(pieces, axis=0).astype(BF)[None]
    tot_scr[...] = total
    for quarter, shard in enumerate(shards(scal)):
        if quarter < 2:
            proj_own[:, part_of(quarter)] = tot_scr[:, lanes_of(shard)]
        else:
            proj_oth[:, part_of(quarter)] = tot_scr[:, lanes_of(shard)].astype(BF)


def total_stats(stats):
    total = stats[0]
    for source in range(1, stats.shape[0]):
        total = total + stats[source]
    return total


def norm_back(scal, quarter, sums, stats, vec, which, cells, size):
    mean, inv = norm_stats(scal, sums, quarter, cells, size)
    gain, slope, offset = affine_of(scal, vec, quarter, which, mean, inv)
    means = group_sum(total_stats(stats)[:, part_of(quarter)] * gain, size) / cells

    def back(grad, field):
        field = field.astype(F32)
        hat = (field - mean) * inv
        if which < 2:
            grad = grad * silu_slope(field * slope + offset)
        return (grad * gain - means[0:1] - hat * means[1:2]) * inv

    return back


def norm3_back_kernel(
    scal, part, recv, dtop, dbot, field, ftop, fbot, cot, ctop, cbot, sums, stats, vec, out_f, ext, away, *, cells, size
):
    pix = part.shape[0]
    end = 2 * COLS + pix
    for quarter in range(2):
        lanes = part_of(quarter)
        back = norm_back(scal, quarter, sums, stats, vec, 2, cells, size)
        main = back(part[:, lanes] + recv[:, lanes].astype(F32), field[:, lanes])
        main = main + cot[:, lanes].astype(F32)
        out_f[:, lanes] = main
        ext[2 * COLS : end, lanes] = main.astype(BF)
        head = back(dtop[:, lanes].astype(F32), ftop[:, lanes]) + ctop[:, lanes].astype(F32)
        tail = back(dbot[:, lanes].astype(F32), fbot[:, lanes]) + cbot[:, lanes].astype(F32)
        ext[0:COLS, lanes] = masked_rows(scal, head[:COLS], UP2).astype(BF)
        ext[COLS : 2 * COLS, lanes] = masked_rows(scal, head[COLS:], UP1).astype(BF)
        ext[end : end + COLS, lanes] = masked_rows(scal, tail[:COLS], DOWN1).astype(BF)
        ext[end + COLS :, lanes] = masked_rows(scal, tail[COLS:], DOWN2).astype(BF)
    away[...] = ext[COLS : end + COLS, lanes_of(1 - scal[I])]


def norm2_back_kernel(scal, part, recv, field, sums, stats, vec, ext, away, *, cells, size):
    rows = part.shape[0]
    for quarter in range(2):
        lanes = part_of(quarter)
        back = norm_back(scal, quarter, sums, stats, vec, 1, cells, size)
        main = back(part[:, lanes] + recv[:, lanes].astype(F32), field[:, lanes])
        ext[0:COLS, lanes] = masked_rows(scal, main[:COLS], UP1).astype(BF)
        ext[COLS : rows - COLS, lanes] = main[COLS : rows - COLS].astype(BF)
        ext[rows - COLS :, lanes] = masked_rows(scal, main[rows - COLS :], DOWN1).astype(BF)
    away[...] = ext[:, lanes_of(1 - scal[I])]


def conv_back_kernel(scal, ext, weight, own, oth, sums, vec, out_own, out_oth, out_stats, tot_scr, *, which, cells, size):
    rows, channels = tot_scr.shape
    parts = []
    for kx in range(3):
        acc = None
        for ky in range(3):
            tap = (ky * 3 + kx) * channels
            start = (2 - ky) * COLS
            term = dot_t(ext[start : start + rows, :], weight[tap : tap + channels, :])
            acc = term if acc is None else acc + term
        parts.append(acc)
    tot_scr[...] = shift_columns(parts[1], parts[2], parts[0])
    below_stats(scal, tot_scr, own, oth, sums, vec, out_own, out_oth, out_stats, which, cells, size)


def last_kernel(scal, part, recv, field, sums, stats, vec, resid_grad, keep, send, tot_scr, *, cells, size):
    i = scal[I]
    for quarter in range(2):
        lanes = part_of(quarter)
        back = norm_back(scal, quarter, sums, stats, vec, 0, cells, size)
        main = back(part[:, lanes] + recv[:, lanes].astype(F32), field[:, lanes])
        tot_scr[:, lanes] = main + resid_grad[:, lanes]
    keep[...] = tot_scr[:, lanes_of(i)]
    send[...] = tot_scr[:, lanes_of(1 - i)].astype(BF)


def weight_grads(scal, act_one, act_two, ext_one, ext_two, rhs_scr, out_scr):
    pix, channels = act_one.shape
    rows = ext_two.shape[0]
    first = (ext_one.shape[0] - rows) // 2
    own = ext_one[first : first + rows, lanes_of(scal[I])]
    for image, wide in enumerate((own, ext_two[...])):
        wide = wide.astype(F32)
        col = lax.broadcasted_iota(jnp.int32, wide.shape, 0) % COLS
        for kx in range(3):
            if kx == 0:
                moved = jnp.where(col < COLS - 1, pltpu.roll(wide, rows - 1, 0), 0.0)
            elif kx == 2:
                moved = jnp.where(col > 0, pltpu.roll(wide, 1, 0), 0.0)
            else:
                moved = wide
            moved = moved.astype(BF)
            for ky in range(3):
                start = (2 - ky) * COLS
                tap = ky * 3 + kx
                lanes = slice(tap * LANES, (tap + 1) * LANES)
                rhs_scr[image * pix : (image + 1) * pix, lanes] = moved[start : start + pix]
    both = jnp.concatenate([act_one, act_two], axis=0)
    for tap in range(0, 9, 2):
        count = min(2, 9 - tap)
        total = lax.dot_general(
            both,
            rhs_scr[:, tap * LANES : (tap + count) * LANES],
            (((0,), (0,)), ((), ())),
            preferred_element_type=F32,
        )
        for n in range(count):
            out_scr[(tap + n) * channels : (tap + n + 1) * channels, :] = total[
                :, n * LANES : (n + 1) * LANES
            ]


def weight_grad_one_kernel(
    scal, up, low, up_there, low_there, ext_one, ext_two, keep, send, rhs_scr, out_scr
):
    cut = up.shape[0]
    mine = jnp.concatenate([up[...], low[0:cut]], axis=0)
    theirs = jnp.concatenate([up_there[...], low_there[0:cut]], axis=0)
    weight_grads(scal, mine, theirs, ext_one, ext_two, rhs_scr, out_scr)
    core = scal[B] % 2
    count = out_scr.shape[0] // 2
    at = lambda n: pl.ds(pl.multiple_of(n * count, count), count)
    keep[...] = out_scr[at(core), :].reshape(keep.shape)
    send[...] = out_scr[at(1 - core), :].astype(BF).reshape(send.shape)


def weight_grad_two_kernel(scal, act, act_there, ext_one, ext_two, wp, out, rhs_scr, out_scr):
    cut = act.shape[0] // 3
    weight_grads(scal, act[cut:], act_there[cut:], ext_one, ext_two, rhs_scr, out_scr)
    blocks = out.shape[0]
    rows = out_scr.shape[0] // blocks
    extra = wp.shape[1] // blocks
    out[:, :rows] = out_scr[...].astype(BF).reshape(blocks, rows, LANES)
    for part in range(2):
        first = rows + part * extra
        out[:, first : first + extra] = wp[part].reshape(blocks, extra, LANES)


def other_sum_kernel(scal, parts, out):
    first = parts.shape[1] - out.shape[0]
    total = parts[0, first:].astype(F32)
    for source in range(1, parts.shape[0]):
        total = total + parts[source, first:].astype(F32)
    out[...] = total.astype(BF)


def total_kernel(scal, own, parts, other, one, two, three, out):
    count = own.shape[0]
    extra = other.shape[0]
    first = own[...] + one[...].astype(F32) + two[...].astype(F32) + three[...].astype(F32)
    out[0:count] = first.astype(BF)
    second = parts[0, : count + extra].astype(F32)
    for source in range(1, parts.shape[0]):
        second = second + parts[source, : count + extra].astype(F32)
    out[count : 2 * count] = second[:count].astype(BF)
    out[2 * count :] = (second[count:] + other[...].astype(F32)).astype(BF)


def scatter_kernel(scal, keep, recv, own, *sends):
    chip = scal[B] // 2
    for mask in range(4):
        chunk = pl.ds(chip ^ mask, 1)
        value = (keep[chunk] + recv[chunk].astype(F32))[0]
        if mask == 0:
            own[...] = value
        else:
            sends[mask - 1][...] = value.astype(BF)


def place_kernel(scal, *refs):
    pieces, (one, two, qkv, out) = refs[:8], refs[8:]
    core, chip = scal[B] % 2, scal[B] // 2
    count = one.shape[0] // 8
    rows = qkv.shape[0] // 6
    for n, piece in enumerate(pieces):
        half = core if n < 4 else 1 - core
        source = chip ^ (n % 4)
        at = lambda slot, size: pl.ds(pl.multiple_of(slot * size, size), size)
        slot = 2 * source + half
        one[at(4 * half + source, count), :] = piece[:count].astype(F32)
        two[at(slot, count), :] = piece[count : 2 * count].astype(F32)
        extra = piece[2 * count :].astype(F32)

        @pl.when(slot < 6)
        def _(extra=extra, slot=slot):
            qkv[at(slot, rows), :] = extra

        @pl.when(slot >= 6)
        def _(extra=extra, slot=slot):
            for m in range(rows // LANES):
                column = (slot - 6) * (rows // LANES) + m
                out[:, lanes_of(column)] = extra[m * LANES : (m + 1) * LANES]


def channel_sums_kernel(scal, one, two, three, mine, theirs):
    rows = jnp.concatenate([total_stats(stats)[0:2] for stats in (one, two, three)], axis=0)
    rows = jnp.concatenate([rows, jnp.zeros((2, rows.shape[1]), F32)], axis=0)
    first, second = rows[:, :LANES], rows[:, LANES:]
    here = scal[I] == 0
    mine[...] = jnp.where(here, first, second)
    theirs[...] = jnp.where(here, second, first)


def channel_grads_kernel(scal, mine, recv, vec, emb, bias_grad, *outs):
    here = scal[I] == 0
    images = (
        jnp.where(here, mine[...], recv[...]),
        jnp.where(here, recv[...], mine[...]),
    )
    gain, bias = vec[4:5], vec[5:6]
    scales = [gain * rows[3:4] + bias * rows[2:3] for rows in images]
    shifts = [rows[2:3] for rows in images]
    grown = [1.0 + vec[8:9], 1.0 + vec[10:11]]
    both = images[0] + images[1]
    bias_grad[0:1] = scales[0] + scales[1]
    bias_grad[1:2] = shifts[0] + shifts[1]
    values = [
        both[1:2],
        both[0:1],
        grown[0] * images[0][3:4] + grown[1] * images[1][3:4],
        grown[0] * images[0][2:3] + grown[1] * images[1][2:3],
        both[5:6],
        both[4:5],
    ]
    for out, value in zip(outs, values):
        out[...] = value
    weight_grad = outs[6]
    turned = emb[...].T
    total = None
    for n, row in enumerate(scales + shifts):
        term = turned[:, n : n + 1] * row
        total = term if total is None else total + term
    weight_grad[...] = total


def out_add_kernel(scal, resid, part, recv, keep, send):
    total = resid[...] + part[...] + recv[...].astype(F32)
    first, second = total[:, :LANES].astype(BF), total[:, LANES:].astype(BF)
    here = scal[I] == 0
    keep[...] = jnp.where(here, first, second)
    send[...] = jnp.where(here, second, first)


def by_images_kernel(scal, out_keep, out_recv, in_keep, in_recv, block_output, input_grad):
    i = scal[I]
    for keep, recv, out in ((out_keep, out_recv, block_output), (in_keep, in_recv, input_grad)):
        out[pl.ds(i, 1)] = keep[...][None]
        out[pl.ds(1 - i, 1)] = recv[...].astype(out.dtype)[None]


def merge_kernel(scal, mine, recv, rest, out):
    out[:, :LANES] = (mine[...] + recv[...].astype(F32)).astype(BF)
    out[:, LANES:] = rest[...]


def context_grad_kernel(scal, context, d_zero, d_one, d_two, d_three, out, tot_scr, *, split):
    rows = out.shape[0]
    turned = [context[image].astype(F32).T.astype(BF) for image in range(2)]
    pieces = (d_zero, d_one, d_two, d_three)
    for h in range(2):
        total = None
        for image in range(2):
            slot = (2 * image + h) ^ scal[Z]
            chosen = pieces[0][...]
            for n in range(1, 4):
                chosen = jnp.where(slot == n, pieces[n][...], chosen)
            term = dot(turned[image], chosen)
            total = term if total is None else total + term
        tot_scr[:, h * LANES : (h + 1) * LANES] = total
    part = scal[B] % split
    out[...] = tot_scr[pl.ds(pl.multiple_of(part * rows, rows), rows), :].astype(BF)


def context_place_kernel(scal, pieces, out, *, split):
    rows = pieces.shape[1]
    for part in range(split):
        for t in range(2):
            first, second = ((2 * t + n) * split + part for n in range(2))
            for h in range(2):
                for kind in range(2):
                    start = h * LANES + kind * HEAD
                    value = jnp.concatenate(
                        [pieces[n, :, start : start + HEAD] for n in (first, second)], axis=1
                    )
                    column = (h + 2 * t) * LANES
                    out[part * rows : (part + 1) * rows, kind, column : column + LANES] = (
                        value.astype(F32)
                    )


def join_kernel(scal, own, *refs):
    pieces, out = refs[:8], refs[8]
    i, b = scal[I], scal[B]
    out[:, lanes_of(i)] = own[...]
    size = own.shape[0] // 8
    for core in range(2):
        for mask in range(4):
            source = b ^ (2 * mask + core)
            target = pl.ds(pl.multiple_of(source * size, size), size)
            out[target, lanes_of(1 - i)] = pieces[4 * core + mask][...]


def place_weight_kernel(scal, own, chunks, out, *, start, width):
    i = scal[I]
    rows = own.shape[0] // width
    size = own.shape[0] // chunks.shape[0]
    for n in range(width):
        out[:, lanes_of(i * width + n)] = own[n * rows : (n + 1) * rows]
    for source in range(chunks.shape[0]):
        n, first = divmod(source * size, rows)
        out[first : first + size, lanes_of((1 - i) * width + n)] = chunks[
            source, start : start + size
        ]


def attend_kernel(
    live, qd, kva, kvb, ctx, dqo, dkva, dkvb, dctx,
    kv_scr, kt_scr, vt_scr, s_scr, e_scr, acc_scr, *, chunk, unroll,
):
    step = pl.program_id(0)
    half_a, half_b, extra = kva.shape[0], kvb.shape[0], ctx.shape[0]
    keys = half_a + half_b
    total = keys + extra
    block = qd.shape[0]

    @pl.when(step == 0)
    def _():
        kv_scr[0:half_a, :] = kva[...]
        kv_scr[half_a:keys, :] = kvb[...]
        kv_scr[keys:total, :] = ctx[...]
        acc_scr[...] = jnp.zeros_like(acc_scr)

        def turn(rows):
            flipped = kv_scr[rows, :].astype(F32).T.astype(BF)
            kt_scr[:, rows] = flipped[:HEAD]
            vt_scr[0:HEAD, rows] = flipped[HEAD:]

        def turn_step(n, carry):
            turn(pl.ds(pl.multiple_of(n * 256, 256), 256))
            return carry

        lax.fori_loop(0, keys // 256, turn_step, 0)
        turn(slice(keys, total))
        vt_scr[HEAD:, :] = jnp.ones((16, total), BF)

    both = qd[...].astype(F32).T
    q_t = both[:HEAD].astype(BF)
    zero = jnp.zeros((HEAD, block), BF)
    q_side = jnp.concatenate([q_t, zero], axis=0)

    def score(rows, top, masked):
        s = dot(kv_scr[rows, :], q_side)
        if masked:
            index = lax.broadcasted_iota(jnp.int32, s.shape, 0)
            s = jnp.where(index < live[0], s, -1e30)
        s_scr[rows, :] = s
        return jnp.maximum(top, jnp.max(s.reshape(-1, 8, block), axis=0))

    def span(n):
        return pl.ds(pl.multiple_of(n * chunk, chunk), chunk)

    def over_keys(func, carry):
        return lax.fori_loop(
            0, keys // chunk, lambda n, c: func(span(n), c), carry, unroll=unroll
        )

    tail = pl.ds(keys, extra)
    top = score(tail, jnp.full((8, block), -1e30, F32), True)
    top = over_keys(lambda rows, c: score(rows, c, False), top)
    top = jnp.max(top, axis=0, keepdims=True)

    def weigh(rows, acc):
        e = jnp.exp(s_scr[rows, :] - top).astype(BF)
        e_scr[rows, :] = e
        return acc + dot(vt_scr[:, rows], e)

    out_t = weigh(tail, jnp.zeros((HEAD + 16, block), F32))
    out_t = over_keys(weigh, out_t)
    inv = 1.0 / out_t[HEAD : HEAD + 1]
    out_t = out_t[:HEAD] * inv
    d_t = both[HEAD:]
    delta = jnp.sum(d_t * out_t, axis=0, keepdims=True) * inv
    d_t = d_t * inv
    d_low = d_t.astype(BF)
    d_side = jnp.concatenate([zero, d_low], axis=0)

    def back(rows, acc):
        d_prob = dot(kv_scr[rows, :], d_side)
        e = e_scr[rows, :]
        d_score = (e.astype(F32) * (d_prob - delta)).astype(BF)
        acc_scr[0:HEAD, rows] += dot_t(q_t, d_score)
        acc_scr[HEAD:, rows] += dot_t(d_low, e)
        return acc + dot(kt_scr[:, rows], d_score)

    dq_t = back(tail, jnp.zeros((HEAD, block), F32))
    dq_t = over_keys(back, dq_t)
    dqo[...] = jnp.concatenate([dq_t, out_t], axis=0).T.astype(BF)

    @pl.when(step == pl.num_programs(0) - 1)
    def _():
        dkva[...] = acc_scr[:, 0:half_a].T
        dkvb[...] = acc_scr[:, half_a:keys].T.astype(BF)
        dctx[...] = acc_scr[:, keys:total].T


def attend(live, recv, kva, kvb, ctx, deps):
    queries = recv.shape[0]
    block = min(1024, queries)
    half_a, half_b, extra = recv.shape[0] if kva is recv else kva.shape[0], kvb.shape[0], ctx.shape[0]
    total = half_a + half_b + extra
    whole = lambda shape: pl.BlockSpec(shape, lambda n: (0, 0))
    kernel = functools.partial(attend_kernel, chunk=512, unroll=8)

    def inner(*refs):
        kernel(*refs[:5], *refs[5 + len(deps) :])

    return pl.pallas_call(
        inner,
        grid=(queries // block,),
        in_specs=[
            pl.BlockSpec(memory_space=pltpu.SMEM),
            pl.BlockSpec((block, LANES), lambda n: (n, 1)),
            whole((half_a, LANES)),
            whole((half_b, LANES)),
            whole((extra, LANES)),
        ]
        + [pl.BlockSpec(memory_space=pl.ANY)] * len(deps),
        out_specs=[
            pl.BlockSpec((block, LANES), lambda n: (n, 0)),
            whole((half_a, LANES)),
            whole((half_b, LANES)),
            whole((extra, LANES)),
        ],
        out_shape=[
            jax.ShapeDtypeStruct((queries, LANES), BF),
            jax.ShapeDtypeStruct((half_a, LANES), F32),
            jax.ShapeDtypeStruct((half_b, LANES), BF),
            jax.ShapeDtypeStruct((extra, LANES), F32),
        ],
        scratch_shapes=[
            pltpu.VMEM((total, LANES), BF),
            pltpu.VMEM((HEAD, total), BF),
            pltpu.VMEM((HEAD + 16, total), BF),
            pltpu.VMEM((total, block), F32),
            pltpu.VMEM((total, block), BF),
            pltpu.VMEM((LANES, total), F32),
        ],
        compiler_params=pltpu.CompilerParams(vmem_limit_bytes=VMEM_BYTES),
        cost_estimate=pl.CostEstimate(
            flops=int(38 * 1.15e9), bytes_accessed=1, transcendentals=0
        ),
    )(live, recv, kva, kvb, ctx, *deps)


def call(kernel, args, outs, scratch=(), deps=(), time=0.0):
    in_vmem = pl.BlockSpec(memory_space=pltpu.VMEM)
    in_smem = pl.BlockSpec(memory_space=pltpu.SMEM)
    anywhere = pl.BlockSpec(memory_space=pl.ANY)
    count = len(args)

    def inner(*refs):
        kernel(*refs[:count], *refs[count + len(deps) :])

    return pl.pallas_call(
        inner,
        in_specs=[in_smem] + [in_vmem] * (count - 1) + [anywhere] * len(deps),
        out_specs=[in_vmem] * len(outs),
        out_shape=[jax.ShapeDtypeStruct(s, d) for s, d in outs],
        scratch_shapes=[pltpu.VMEM(s, d) for s, d in scratch],
        compiler_params=pltpu.CompilerParams(vmem_limit_bytes=VMEM_BYTES),
        cost_estimate=pl.CostEstimate(
            flops=1 + int(time * 1.15e9), bytes_accessed=1, transcendentals=0
        ),
    )(*args, *deps)


def after(values, *deps):
    anywhere = pl.BlockSpec(memory_space=pl.ANY)
    count = len(values)

    def inner(*refs):
        pass

    return pl.pallas_call(
        inner,
        in_specs=[anywhere] * (count + len(deps)),
        out_specs=[anywhere] * count,
        out_shape=[jax.ShapeDtypeStruct(v.shape, v.dtype) for v in values],
        input_output_aliases={n: n for n in range(count)},
        cost_estimate=pl.CostEstimate(flops=1, bytes_accessed=1, transcendentals=0),
    )(*values, *deps)


def embed_features(timesteps, image_embed):
    half_width = image_embed.shape[1] // 2
    freqs = jnp.exp(-math.log(10000.0) * jnp.arange(half_width, dtype=F32) / half_width)
    angles = timesteps.astype(F32)[:, None] * freqs[None, :]
    return jax.nn.silu(jnp.concatenate([jnp.cos(angles), jnp.sin(angles)], axis=1) + image_embed)


def body(
    block_input,
    cotangent,
    image_embed,
    timesteps,
    text_len,
    context,
    conv1_weight,
    conv2_weight,
    embed_weight,
    embed_bias,
    norm1_gain,
    norm1_bias,
    norm2_gain,
    norm2_bias,
    norm3_gain,
    norm3_bias,
    qkv_weight,
    out_weight,
    ctx_weight,
):
    images, row_count, col_count, width = block_input.shape
    channels = qkv_weight.shape[0]
    size = channels // GROUPS
    blocks = lax.axis_size("blk")
    pix = row_count * col_count
    cells = float(pix * blocks * size)
    split = blocks // 4
    ctx_len = context.shape[1]
    b = lax.axis_index("blk")
    z = lax.axis_index("ch")
    h, i = z % 2, z // 2
    row, rows_all = b * row_count, blocks * row_count
    inside = [row >= 1, row + row_count < rows_all, row >= 2, row + row_count + 1 < rows_all]
    scal = jnp.stack([h, i] + [flag.astype(jnp.int32) for flag in inside] + [z, b]).astype(jnp.int32)


    def over_ch(value, mask):
        return lax.ppermute(value, "ch", [(n, n ^ mask) for n in range(4)])

    def over_blk(value, mask):
        return lax.ppermute(value, "blk", [(n, n ^ mask) for n in range(blocks)])

    def ring(value, step):
        return lax.ppermute(value, "blk", [(n, (n + step) % blocks) for n in range(blocks)])

    def halo(first, last):
        if row_count >= 2:
            return ring(last, 1), ring(first, -1)
        return (
            jnp.concatenate([ring(last, 2), ring(last, 1)], axis=0),
            jnp.concatenate([ring(first, -1), ring(first, -2)], axis=0),
        )

    pairs = [[n * 4 + 2 * m + k for n in range(blocks) for k in range(2)] for m in range(2)]

    def to_image(value):
        return lax.all_to_all(value, ("blk", "ch"), 0, 0, axis_index_groups=pairs)

    def by_image(first, second):
        return jnp.where(i == 0, first, second), jnp.where(i == 0, second, first)

    def plane(value):
        mine = [value] + [over_blk(value, 2 * mask) for mask in (1, 2, 3)]
        return mine + [over_blk(piece, 1) for piece in mine]

    w1_own = conv1_weight.reshape(-1, width)
    w2_own = conv2_weight.reshape(-1, width)
    heads = lambda v: v.reshape(channels, 2, HEAD)
    wp_own = jnp.stack(
        [
            jnp.concatenate([heads(qkv_weight[:, 1]), heads(qkv_weight[:, 2])], axis=2),
            jnp.concatenate([heads(qkv_weight[:, 0] * 0.125), heads(out_weight.T)], axis=2),
        ],
        axis=0,
    )
    wp_own = jnp.transpose(wp_own, (2, 0, 1, 3)).reshape(-1, LANES)
    w1_rows, w2_rows, wp_rows = (w.shape[0] // blocks for w in (w1_own, w2_own, wp_own))
    chunk_of = lambda w: lax.dynamic_slice_in_dim(w, b * (w.shape[0] // blocks), w.shape[0] // blocks, 0)
    w1_slice = chunk_of(w1_own)

    emb_act = embed_features(timesteps, image_embed).astype(BF)
    scale_shift = (
        jnp.einsum("ie,esc->isc", emb_act, embed_weight, preferred_element_type=F32) + embed_bias
    )
    local_vec = jnp.concatenate(
        [
            jnp.zeros((2, width), F32),
            jnp.stack([norm1_gain, norm1_bias, norm2_gain, norm2_bias, norm3_gain, norm3_bias]),
            scale_shift.reshape(4, width),
            jnp.zeros((4, width), F32),
        ],
        axis=0,
    )
    x_mine, x_theirs = call(
        image_split_kernel,
        [scal, block_input.reshape(images, pix, width)],
        [((pix, width), BF)] * 2,
        deps=[w1_slice],
    )
    w1_chunk = over_ch(w1_slice, 2)
    x_two, x_one = over_ch(x_theirs, 2), over_ch(x_mine, 1)
    x_three = over_ch(x_two, 1)
    if blocks == 8:
        w1_pieces = plane(w1_chunk)
    else:
        w1_pieces = [lax.all_gather(w1_chunk, "blk", axis=0, tiled=True)]
    x_sums = call(
        functools.partial(input_sums_kernel, blocks=blocks),
        [scal, block_input.reshape(images, pix, width), local_vec],
        [((4 * blocks, 16, width), F32)],
        deps=[x_mine],
    )[0]
    sums1 = lax.all_to_all(x_sums, ("blk", "ch"), 0, 0)
    two_source = jnp.concatenate([chunk_of(w2_own), chunk_of(wp_own)], axis=0)
    two_chunk = over_ch(two_source, 2)
    (two_chunk,) = after((two_chunk,), x_one, x_sums, x_three, *w1_pieces[1:4])
    wide = dict(axis=1)
    x_own = jnp.concatenate(by_image(x_mine, x_two), **wide)
    x_oth = jnp.concatenate(by_image(x_one, x_three), **wide)
    edge = min(2 * COLS, pix)
    x_top, x_bot = halo(
        jnp.concatenate([x_own[:edge], x_oth[:edge]], **wide),
        jnp.concatenate([x_own[pix - edge :], x_oth[pix - edge :]], **wide),
    )
    if blocks == 8:
        w1 = call(join_kernel, [scal, w1_own] + w1_pieces, [((w1_own.shape[0], HALF), BF)])[0]
    else:
        w1_oth = w1_pieces[0]
        w1 = jnp.concatenate(by_image(w1_own, w1_oth), **wide)
    two = lax.all_gather(two_chunk, "blk", axis=0)
    w2 = call(
        functools.partial(place_weight_kernel, start=0, width=1),
        [scal, w2_own, two],
        [((w2_own.shape[0], HALF), BF)],
    )[0]
    j = b // split
    ctx_rows = -(-ctx_len // 16) * 16
    ctx_w = jnp.stack(
        [
            lax.dynamic_slice_in_dim(
                ctx_weight, 128 * (hh + 2 * (j // 2)) + HEAD * (j % 2), HEAD, 2
            ).reshape(-1, 2 * HEAD)
            for hh in range(2)
        ]
    )
    ctx_term = jnp.einsum("itx,hxk->ihtk", context, ctx_w, preferred_element_type=F32)
    ctx_term = jnp.pad(
        ctx_term.astype(BF).reshape(4, ctx_len, 2 * HEAD),
        ((0, 0), (0, ctx_rows - ctx_len), (0, 0)),
    )
    ctx_kv = lax.psum_scatter(ctx_term, "ch", scatter_dimension=0)
    live = (CLIPTOK + jnp.where(i == 0, text_len[0], text_len[1])).astype(jnp.int32)[None]

    emb_f = jnp.repeat(emb_act.astype(F32), 2, axis=1)
    odd = (jnp.arange(emb_f.shape[1]) % 2)[None]
    emb_rows = jnp.concatenate(
        [emb_f * (1 - odd), emb_f * odd, jnp.zeros((4, emb_f.shape[1]), F32)], axis=0
    )
    kind = dict(cells=cells, size=size)
    ext = pix + 2 * COLS
    stat_shape = ((2 * blocks, 8, HALF), F32)

    c_mine, c_theirs = call(
        image_split_kernel,
        [scal, cotangent.reshape(images, pix, width)],
        [((pix, width), BF)] * 2,
        deps=[x_sums],
    )

    hid_own, hid_stat, act1, vec = call(
        functools.partial(conv1_kernel, **kind),
        [scal, x_own, x_oth, x_top, x_bot, sums1, w1],
        [((ext, HALF), BF), stat_shape, ((pix, channels), BF), ((4, 16, LANES), F32)],
        [((ext + 2 * COLS, channels), BF)],
        deps=[ctx_term, c_mine, emb_rows, live],
    )
    hid_oth = over_ch(hid_own, 1)
    sums2 = to_image(hid_stat)

    c_mine, c_theirs = after((c_mine, c_theirs), hid_oth, w2)
    c_one, c_two = over_ch(c_mine, 1), over_ch(c_theirs, 2)
    c_three = over_ch(c_two, 1)
    cot_own = jnp.concatenate(by_image(c_mine, c_two), **wide)
    cot_oth = jnp.concatenate(by_image(c_one, c_three), **wide)

    edges = ((2, edge, HALF), BF)
    res_f, res_own, res_stat, act_first, act_rest, res_edges = call(
        functools.partial(conv2_kernel, **kind),
        [scal, hid_own, hid_oth, sums2, vec, w2, x_own, act1],
        [
            ((pix, HALF), F32),
            ((pix, HALF), BF),
            stat_shape,
            ((pix // 2, channels), BF),
            ((pix + pix // 2, channels), BF),
            edges,
        ],
        [((ext, channels), BF)],
    )
    res_oth = over_ch(res_own, 1)
    sums3 = to_image(res_stat)
    wp = call(
        functools.partial(place_weight_kernel, start=w2_rows, width=4),
        [scal, wp_own, two],
        [((channels, 4 * HALF), BF)],
        deps=[res_oth],
    )[0]
    packed, act3, cot_all, cot_edges = call(
        functools.partial(qkv_kernel, **kind),
        [scal, res_own, res_oth, sums3, vec, cot_own, cot_oth, wp],
        [((4, pix, HALF), BF), ((pix, channels), BF), ((pix, channels), BF), edges],
        deps=[ctx_kv],
    )
    recv = lax.all_to_all(packed.reshape(blocks, pix // split, HALF), "blk", 0, 0)
    res_edges, act_first = after((res_edges, act_first), packed)
    res_top, res_bot = halo(res_edges[0], res_edges[1])
    cot_top, cot_bot = halo(cot_edges[0], cot_edges[1])
    first_there = over_ch(act_first, 2)
    (recv,) = after((recv,), res_top, res_bot, cot_top, cot_bot, first_there)
    recv = recv.reshape(-1, HALF)
    rest_there = over_ch(act_rest, 2)
    if split == 2:
        kva, kvb = recv, over_blk(recv[:, :LANES], 1)
    else:
        groups = [[n * split + m for m in range(split)] for n in range(4)]
        kv_all = lax.all_gather(
            recv[:, :LANES], "blk", axis=0, tiled=True, axis_index_groups=groups
        )
        kva, kvb = kv_all[: kv_all.shape[0] // 2], kv_all[kv_all.shape[0] // 2 :]
    dqo, dkva, dkvb, dctx = attend(live, recv, kva, kvb, ctx_kv, [])
    if split == 2:
        d_ctx = dctx + over_blk(dctx, 1)
        back = call(
            merge_kernel,
            [scal, dkva, over_blk(dkvb, 1), dqo],
            [((dqo.shape[0], HALF), BF)],
            deps=[rest_there],
        )[0]
    else:
        d_ctx = lax.psum(dctx, "blk", axis_index_groups=groups)
        d_kv = lax.psum_scatter(
            jnp.concatenate([dkva, dkvb.astype(F32)], axis=0),
            "blk",
            scatter_dimension=0,
            axis_index_groups=groups,
            tiled=True,
        )
        back = jnp.concatenate([d_kv.astype(BF), dqo], axis=1)
    grads = lax.all_to_all(back.reshape(blocks, pix // split, HALF), "blk", 0, 0)
    grads = grads.reshape(4, pix, HALF)

    features = context.shape[2] // split
    d_ctx = d_ctx[:ctx_len].astype(BF)
    ctx_part = call(
        functools.partial(context_grad_kernel, split=split),
        [scal, context, d_ctx] + [over_ch(d_ctx, mask) for mask in (1, 2, 3)],
        [((features, HALF), BF)],
        [((context.shape[2], HALF), F32)],
    )[0]
    ctx_all = lax.all_gather(ctx_part, "blk", axis=0)

    def low_grad(rows):
        return [((rows, HALF), F32), ((rows, HALF), BF), stat_shape]

    p3_own, p3_oth, st3 = call(
        functools.partial(qkv_back_kernel, **kind),
        [scal, grads, wp, res_own, res_oth, sums3, vec],
        low_grad(pix),
        [((pix, channels), F32)],
        deps=[ctx_part],
    )
    r3 = over_ch(p3_oth, 1)
    stats3 = to_image(st3)
    proj_own, proj_oth, wp_part = call(
        out_kernel,
        [scal, grads, wp, act3, cot_all],
        [((pix, HALF), F32), ((pix, HALF), BF), ((2, 4 * channels, LANES), BF)],
        [((pix, channels), F32)],
        deps=[r3],
    )
    first3 = (p3_own[:edge] + r3[:edge].astype(F32)).astype(BF)
    last3 = (p3_own[pix - edge :] + r3[pix - edge :].astype(F32)).astype(BF)
    d_top3, d_bot3 = halo(first3, last3)
    d_resid, ext2, away2 = call(
        functools.partial(norm3_back_kernel, **kind),
        [
            scal, p3_own, r3, d_top3, d_bot3, res_own, res_top, res_bot, cot_own, cot_top, cot_bot,
            sums3, stats3, vec,
        ],
        [((pix, HALF), F32), ((ext + 2 * COLS, HALF), BF), ((ext, LANES), BF)],
        deps=[proj_own],
    )
    there2 = over_ch(away2, 2)
    p2_own, p2_oth, st2 = call(
        functools.partial(conv_back_kernel, which=1, **kind),
        [scal, ext2, w2, hid_own, hid_oth, sums2, vec],
        low_grad(ext),
        [((ext, channels), F32)],
        time=8.0,
    )
    r2 = over_ch(p2_oth, 1)
    (st2,) = after((st2,), there2)
    stats2 = to_image(st2)
    conv_rows, wp_rows = 9 * channels // blocks, 4 * channels // blocks
    part2 = call(
        weight_grad_two_kernel,
        [scal, act_rest, rest_there, ext2, there2, wp_part],
        [((blocks, conv_rows + 2 * wp_rows, LANES), BF)],
        [((2 * pix, 9 * LANES), BF), ((9 * channels, LANES), F32)],
        deps=[r2],
    )[0]
    ext1, away1 = call(
        functools.partial(norm2_back_kernel, **kind),
        [scal, p2_own, r2, hid_own, sums2, stats2, vec],
        [((ext, HALF), BF), ((ext, LANES), BF)],
        deps=[part2, ctx_all],
    )
    parts2 = lax.all_to_all(part2, "blk", 0, 0)
    there1 = over_ch(away1, 2)
    p1_own, p1_oth, st1 = call(
        functools.partial(conv_back_kernel, which=0, **kind),
        [scal, ext1, w1, x_own, x_oth, sums1, vec],
        low_grad(pix),
        [((pix, channels), F32)],
        time=8.0,
    )
    (st1,) = after((st1,), there1, parts2)
    (proj_late,) = after((proj_oth,), there1)
    r1 = over_ch(p1_oth, 1)
    stats1 = to_image(st1)
    if blocks == 8:
        ctx_grad = call(
            functools.partial(context_place_kernel, split=split),
            [scal, ctx_all],
            [((context.shape[2], 2, channels), F32)],
            deps=[p1_own],
            time=10.0,
        )[0]
    else:
        ctx_grad = ctx_all.reshape(2, 2, split, features, 2, 2, HEAD)
        ctx_grad = jnp.transpose(ctx_grad, (2, 3, 5, 0, 4, 1, 6)).astype(F32)
    half_shape = (4, 9 * channels // 8, LANES)
    keep1, send1 = call(
        weight_grad_one_kernel,
        [scal, act_first, act_rest, first_there, rest_there, ext1, there1],
        [(half_shape, F32), (half_shape, BF)],
        [((2 * pix, 9 * LANES), BF), ((9 * channels, LANES), F32)],
        deps=[p1_own, ctx_grad],
        time=20.0,
    )
    if blocks == 8:
        own1, *sends = call(
            scatter_kernel,
            [scal, keep1, over_blk(send1, 1)],
            [((conv_rows, LANES), F32)] + [((conv_rows, LANES), BF)] * 3,
        )
    else:
        own1 = keep1
    if blocks == 8:
        other = call(other_sum_kernel, [scal, parts2], [((wp_rows, LANES), BF)], deps=[own1])[0]
        total = call(
            total_kernel,
            [scal, own1, parts2, over_ch(other, 2)]
            + [over_blk(v, 2 * n + 2) for n, v in enumerate(sends)],
            [((2 * conv_rows + wp_rows, LANES), BF)],
        )[0]
    else:
        total = own1
    out_keep, out_send = call(
        out_add_kernel,
        [scal, res_f, proj_own, over_ch(proj_late, 1)],
        [((pix, width), BF)] * 2,
        deps=[total],
    )
    in_keep, in_send = call(
        functools.partial(last_kernel, **kind),
        [scal, p1_own, r1, x_own, sums1, stats1, vec, d_resid],
        [((pix, width), F32), ((pix, width), BF)],
        [((pix, HALF), F32)],
        deps=[total],
        time=40.0,
    )
    sums_here, sums_away = call(
        channel_sums_kernel,
        [scal, stats1, stats2, stats3],
        [((8, LANES), F32)] * 2,
        deps=[total],
    )
    sums_recv = over_ch(sums_away, 2)
    out_recv, in_recv = over_ch(out_send, 2), over_ch(in_send, 2)
    bias_grad, *smalls, embed_weight_grad = call(
        channel_grads_kernel,
        [scal, sums_here, sums_recv, local_vec, emb_rows],
        [((2, LANES), F32)] + [((1, LANES), F32)] * 6 + [((emb_rows.shape[1], LANES), F32)],
        deps=[total],
        time=15.0,
    )
    block_output, input_grad = call(
        by_images_kernel,
        [scal, out_keep, out_recv, in_keep, in_recv],
        [((images, pix, width), BF), ((images, pix, width), F32)],
        deps=[total],
        time=10.0,
    )
    if blocks == 8:
        grad1, grad2, qkv_grad, out_grad = call(
            place_kernel,
            [scal] + plane(total),
            [((9 * channels, LANES), F32)] * 2
            + [((3 * channels, LANES), F32), ((LANES, channels), F32)],
            deps=[block_output, bias_grad],
        )
    else:
        flip = lambda c: jnp.where(b % 2 == 0, *((keep1.astype(BF), send1)[:: 1 - 2 * c]))
        grad1 = lax.psum(jnp.concatenate([flip(0), flip(1)], axis=0), "blk").astype(F32)
        sums = lax.psum(part2, "blk").astype(F32)
        cut = conv_rows + wp_rows
        grad2 = sums[:, :conv_rows]
        wp_grad = sums[:, conv_rows:cut] + over_ch(sums[:, cut:].astype(BF), 2).astype(F32)
        wp_grad = wp_grad.reshape(-1, LANES)
        qkv_grad, out_grad = wp_grad[: 3 * channels], wp_grad[3 * channels :]
        out_grad = jnp.concatenate(list(out_grad.reshape(-1, LANES, LANES)), axis=1)
    qkv_grad = jnp.transpose(qkv_grad.reshape(3, channels, LANES), (1, 0, 2))

    return (
        block_output.reshape(block_input.shape),
        input_grad.reshape(block_input.shape),
        grad1.reshape(conv1_weight.shape),
        grad2.reshape(conv2_weight.shape),
        embed_weight_grad.reshape(embed_weight.shape),
        bias_grad,
        *(value.reshape(width) for value in smalls),
        qkv_grad,
        out_grad,
        ctx_grad.reshape(ctx_weight.shape),
    )


def solution(mesh):
    return jax.shard_map(
        body,
        mesh=mesh,
        in_specs=(
            P(None, "blk", None, "ch"),
            P(None, "blk", None, "ch"),
            P(),
            P(),
            P(),
            P(None, None, "ch"),
            P(None, None, None, "ch"),
            P(None, None, None, "ch"),
            P(None, None, "ch"),
            P(None, "ch"),
            P("ch"),
            P("ch"),
            P("ch"),
            P("ch"),
            P("ch"),
            P("ch"),
            P(None, None, "ch"),
            P("ch", None),
            P("ch", None, None),
        ),
        out_specs=(
            P(None, "blk", None, "ch"),
            P(None, "blk", None, "ch"),
            P(None, None, None, "ch"),
            P(None, None, None, "ch"),
            P(None, None, "ch"),
            P(None, "ch"),
            P("ch"),
            P("ch"),
            P("ch"),
            P("ch"),
            P("ch"),
            P("ch"),
            P(None, None, "ch"),
            P("ch", None),
            P("ch", None, None),
        ),
        check_vma=False,
    )
```
